32 devices in a mesh: rows: 16 (over z, y, x), tp: 2 (over core).
Axes of the slice: x: 2, y: 2, z: 4, core: 2. Of those that a mesh axis runs over, the one named last changes fastest.
Arguments:
- tokens: bfloat16 [65536, 1024], P(('rows', 'tp')), may hold values from -6 to 6
- segment_ids: int32 [128, 512], P('rows'), may hold values from 0 to 7, never falling along the last dimension, each value on 1 to 256 neighbouring positions
- fill_counts: int32 [128], P('rows'), may hold values from 384 to 512
- qkv_weight: bfloat16 [3, 1024, 1024], P(None, 'rows', 'tp'), may hold values from -0.1875 to 0.1875
- qv_bias: bfloat16 [2, 1024], P(None, 'tp'), may hold values from -3 to 3
- out_weight: bfloat16 [1024, 1024], P('tp', 'rows'), may hold values from -0.75 to 0.75
- out_bias: bfloat16 [1024], replicated, may hold values from -3 to 3
- norm1_gain: bfloat16 [1024], replicated, may hold values from 0.099609375 to 1.8984375
- norm1_bias: bfloat16 [1024], replicated, may hold values from -3 to 3
- in_weight: bfloat16 [1024, 4096], P('rows', 'tp'), may hold values from -0.1875 to 0.1875
- in_bias: bfloat16 [4096], P('tp'), may hold values from -3 to 3
- down_weight: bfloat16 [4096, 1024], P('tp', 'rows'), may hold values from -0.09375 to 0.09375
- down_bias: bfloat16 [1024], replicated, may hold values from -3 to 3
- norm2_gain: bfloat16 [1024], replicated, may hold values from 0.099609375 to 1.8984375
- norm2_bias: bfloat16 [1024], replicated, may hold values from -3 to 3
- cotangent: bfloat16 [65536, 1024], P(('rows', 'tp')), may hold values from -6 to 6
Outputs:
- layer_out: bfloat16 [65536, 1024], P(('rows', 'tp'))
- tokens_grad: bfloat16 [65536, 1024], P(('rows', 'tp'))
- qv_bias_grad: float32 [2, 1024], replicated
- out_bias_grad: float32 [1024], replicated
- norm1_bias_grad: float32 [1024], replicated
- in_bias_grad: float32 [4096], replicated
- down_bias_grad: float32 [1024], replicated
- norm2_bias_grad: float32 [1024], replicated
The draws below stay inside these ranges and needn't reach their ends.
Inputs may be any that keep to these rules, and one draw needn't show every extreme that they name: `segment_ids`: within a packed row the numbers never fall; each of the 8 documents of a row takes at least one slot and at most half of the 512 slots. Slots from fill_counts on are padding.
All inputs are finite; a program needn't handle non-finite values.
Results may differ from the reference program's by a relative error of at most 0.014.
Values may be sent and summed in bfloat16 or wider, within the bound.
No kernel may reach another device: no remote copies, remote signals or barrier semaphores. Data moves between devices by JAX's collectives and lax.ppermute only.
A program may use at most 256 MiB of HBM per device.

```python
import math
import jax
import jax.numpy as jnp
import numpy as np
from jax import lax

D = 1024
HEADS = 16
FF = 4096
HEAD_DIM = 64
SLOTS = 512
DOCS = 8
ROWS = 128
TOKENS = 65536


def place_ends(entries, stream_key, least, largest):
    index_at = [jax.random.randint(jax.random.fold_in(stream_key, axis), (), 0, length) for axis, length in enumerate(entries.shape)]
    longest = entries.shape.index(max(entries.shape))
    neighbour = index_at[:longest] + [(index_at[longest] + 1) % entries.shape[longest]] + index_at[longest + 1:]
    return entries.at[tuple(index_at)].set(least).at[tuple(neighbour)].set(largest)


def block_levels(rng, extent, pieces, smallest, largest):
    factor_of = 1.0
    for axis_at, parts in pieces:
        draws = jax.random.uniform(jax.random.fold_in(jax.random.fold_in(rng, 6), axis_at), (parts,), jnp.float32, smallest / len(pieces), largest / len(pieces))
        factor_of = factor_of * jnp.repeat(jnp.exp(draws), extent[axis_at] // parts).reshape((-1,) + (1,) * (len(extent) - 1 - axis_at))
    return factor_of


def profile(number_of, total, most, skew):
    portions = [(1 << 20) // math.isqrt(grade ** skew) + 1 for grade in range(2, number_of + 1)]
    spare, given = total - most - (number_of - 1), [1] * (number_of - 1)
    while spare > 0:
        free = [i for i in range(number_of - 1) if given[i] < most]
        pool, left = sum([portions[i] for i in free]), spare
        for i in free:
            more = min(most - given[i], max(1, left * portions[i] // pool), spare)
            given[i] = given[i] + more
            spare = spare - more
    return np.array([most] + given)


def uneven_parts(stream_key, amount, total, limit, lean):
    if amount == 2:
        one = jax.random.randint(stream_key, (), max(1, total - limit), min(limit, total - 1) + 1)
        return jnp.stack([one, total - one])
    lengths = jnp.asarray(profile(amount, total, limit, lean), jnp.int32)
    twos = (amount - 1) // 2
    source_of, sink = lengths[1:1 + 2 * twos:2], lengths[2:2 + 2 * twos:2]
    slack = jnp.minimum(source_of - 1, limit - sink)
    shifted = jax.random.randint(jax.random.fold_in(stream_key, 1), (twos,), 0, 1 << 20) % (slack + 1)
    lengths = lengths.at[1:1 + 2 * twos:2].set(source_of - shifted).at[2:2 + 2 * twos:2].set(sink + shifted)
    return lengths[jax.random.permutation(jax.random.fold_in(stream_key, 2), amount)]


def centred(stream_key, extent, scale, reach, shards=(), kind=jnp.bfloat16):
    factor_of = block_levels(stream_key, extent, shards, -0.22, 0.18) if shards else 1.0
    result = jax.random.normal(stream_key, extent, jnp.float32) * scale * factor_of
    return jnp.minimum(jnp.maximum(result, -reach), reach).astype(kind)


def setup_inputs(seed: int = 0) -> dict:
    splits = jax.random.split(jax.random.key(seed), 17)
    return {
        "tokens": centred(splits[0], (TOKENS, D), 1.0, 6.0, ((0, 32),)),
        "segment_ids": jax.vmap(lambda own: jnp.searchsorted(jnp.cumsum(uneven_parts(own, DOCS, SLOTS, SLOTS // 2, 2)), jnp.arange(SLOTS), side="right"))(jax.random.split(splits[1], ROWS)).reshape((ROWS, SLOTS)).astype(jnp.int32),
        "fill_counts": place_ends(jax.random.randint(splits[2], (ROWS,), SLOTS * 3 // 4, SLOTS + 1), jax.random.fold_in(splits[2], 1), SLOTS * 3 // 4, SLOTS).astype(jnp.int32),
        "qkv_weight": centred(splits[3], (3, D, D), D ** -0.5, 0.1875, ((1, 16), (2, 2))),
        "qv_bias": centred(splits[4], (2, D), 0.5, 3.0, ((1, 2),)),
        "out_weight": centred(splits[5], (D, D), (D // 16) ** -0.5, 0.75, ((0, 2), (1, 16))),
        "out_bias": centred(splits[6], (D,), 0.5, 3.0),
        "norm1_gain": jnp.clip(1.0 + 0.18 * jax.random.normal(splits[7], (D,), jnp.float32), 0.099609375, 1.8984375).astype(jnp.bfloat16),
        "norm1_bias": centred(splits[8], (D,), 0.5, 3.0),
        "in_weight": centred(splits[9], (D, FF), D ** -0.5, 0.1875, ((0, 16), (1, 2))),
        "in_bias": centred(splits[10], (FF,), 0.5, 3.0, ((0, 2),)),
        "down_weight": centred(splits[11], (FF, D), FF ** -0.5, 0.09375, ((0, 2), (1, 16))),
        "down_bias": centred(splits[12], (D,), 0.5, 3.0),
        "norm2_gain": jnp.clip(1.0 + 0.18 * jax.random.normal(splits[13], (D,), jnp.float32), 0.099609375, 1.8984375).astype(jnp.bfloat16),
        "norm2_bias": centred(splits[14], (D,), 0.5, 3.0),
        "cotangent": centred(splits[15], (TOKENS, D), 1.0, 6.0, ((0, 32),)),
    }


@jax.custom_vjp
def low(v):
    return lax.optimization_barrier(v.astype(jnp.bfloat16)).astype(jnp.float32)

@jax.custom_vjp
def low_back(v):
    return v

def low_keep(v):
    return (low(v), None)

def low_pass(kept, grad):
    return (grad,)

def back_keep(v):
    return (v, None)

def back_low(kept, grad):
    return (low(grad),)
low.defvjp(low_keep, low_pass)
low_back.defvjp(back_keep, back_low)
EPSILON = 1e-05
MASKED = -1e+30
HIGHEST = lax.Precision.HIGHEST

def layer_norm(summed, gain_vec, shift_vec):
    row_mean = lax.optimization_barrier(jnp.mean(summed, -1, keepdims=True))
    centered = summed - row_mean
    variance = lax.optimization_barrier(jnp.mean(centered * centered, -1, keepdims=True))
    return centered * lax.rsqrt(variance + EPSILON) * gain_vec + shift_vec

def allowed_pairs(segment, filled):
    places = lax.iota(jnp.int32, segment.shape[0])
    same_doc = segment[:, None] == segment[None, :]
    live_key = (places[None, :] < filled) | (places[:, None] == places[None, :])
    return same_doc & live_key

def block_forward(operands, frozen_set, biases, gains):
    rows_x, segments, fill_rows = operands
    weight_q, weight_k, weight_v, weight_out, weight_in, weight_down = frozen_set
    bias_qv, bias_out, shift_one, bias_in, bias_down, shift_two = biases
    gain_one, gain_two = gains
    queries = low_back(low(jnp.dot(rows_x, weight_q, precision=HIGHEST) + bias_qv[0]))
    key_rows = low_back(low(jnp.dot(rows_x, weight_k, precision=HIGHEST)))
    value_rows = low_back(low(jnp.dot(rows_x, weight_v, precision=HIGHEST) + bias_qv[1]))
    batch_rows = segments.shape[0]
    shape_four = (batch_rows, SLOTS, HEADS, HEAD_DIM)
    scores = jnp.einsum('gqhd,gkhd->ghqk', queries.reshape(shape_four), key_rows.reshape(shape_four), precision=HIGHEST)
    scores = low_back(scores * (1.0 / math.sqrt(HEAD_DIM)))
    allowed = jax.vmap(allowed_pairs)(segments, fill_rows)
    scores = jnp.where(allowed[:, None], scores, MASKED)
    probs = low(jax.nn.softmax(scores, axis=-1))
    context = jnp.einsum('ghqk,gkhd->gqhd', probs, value_rows.reshape(shape_four), precision=HIGHEST)
    context = low_back(low(context.reshape(rows_x.shape)))
    attention = low_back(jnp.dot(context, weight_out, precision=HIGHEST) + bias_out)
    normed = layer_norm(rows_x + attention, gain_one, shift_one)
    inner = low_back(jnp.dot(low(normed), weight_in, precision=HIGHEST) + bias_in)
    activated = low(jax.nn.gelu(inner, approximate=False))
    branch = low_back(jnp.dot(activated, weight_down, precision=HIGHEST) + bias_down)
    return layer_norm(normed + branch, gain_two, shift_two)

def reference(tokens, segment_ids, fill_counts, qkv_weight, qv_bias, out_weight, out_bias, norm1_gain, norm1_bias, in_weight, in_bias, down_weight, down_bias, norm2_gain, norm2_bias, cotangent):
    group_rows = math.gcd(ROWS, 8)
    blocks = ROWS // group_rows
    width_rows = group_rows * SLOTS
    frozen_set = (qkv_weight[0].astype(jnp.float32), qkv_weight[1].astype(jnp.float32), qkv_weight[2].astype(jnp.float32), out_weight.astype(jnp.float32), in_weight.astype(jnp.float32), down_weight.astype(jnp.float32))
    gains = (norm1_gain.astype(jnp.float32), norm2_gain.astype(jnp.float32))
    segments = segment_ids.reshape(blocks, group_rows, SLOTS).astype(jnp.int32)
    fill_rows = fill_counts.reshape(blocks, group_rows).astype(jnp.int32)

    def forward(inputs_f, bias_qv, bias_out, shift_one, bias_in, bias_down, shift_two):
        biases = (bias_qv, bias_out, shift_one, bias_in, bias_down, shift_two)

        def one_block(operands):
            return block_forward(operands, frozen_set, biases, gains)
        return lax.map(jax.checkpoint(one_block), (inputs_f, segments, fill_rows))
    inputs_f = tokens.astype(jnp.float32).reshape(blocks, width_rows, D)
    outputs, pull_back = jax.vjp(forward, inputs_f, qv_bias.astype(jnp.float32), out_bias.astype(jnp.float32), norm1_bias.astype(jnp.float32), in_bias.astype(jnp.float32), down_bias.astype(jnp.float32), norm2_bias.astype(jnp.float32))
    grads = pull_back(cotangent.astype(jnp.float32).reshape(blocks, width_rows, D))
    return (outputs.reshape(TOKENS, D).astype(jnp.bfloat16), grads[0].reshape(TOKENS, D).astype(jnp.bfloat16), grads[1], grads[2], grads[3], grads[4], grads[5], grads[6])
```

```python
import math

import jax
import jax.numpy as jnp
from jax import lax
from jax.experimental import pallas as pl
from jax.experimental.pallas import tpu as pltpu
from jax.sharding import PartitionSpec as P

D = 1024
FF = 4096
HEADS = 16
HEAD_DIM = 64
SLOTS = 512
GROUP = 4
WIDE = GROUP * HEAD_DIM
PAIR = 2 * HEAD_DIM
GROUPS = HEADS // GROUP
TILE = 256
HIDDEN = 512
EPSILON = 1e-05
MASKED = -1e30
SCALE = 1.0 / math.sqrt(HEAD_DIM)
VMEM_BYTES = 60 * 2**20

NN = (((1,), (0,)), ((), ()))
NT = (((1,), (1,)), ((), ()))


def mul(left, right, dims=NN):
    return lax.dot_general(left, right, dims, preferred_element_type=jnp.float32)


def low(values):
    return values.astype(jnp.bfloat16)


def wide(values):
    return values.astype(jnp.float32)


def norm_forward(summed, gain_vec, shift_vec):
    row_mean = jnp.mean(summed, -1, keepdims=True)
    centered = summed - row_mean
    inverse = lax.rsqrt(jnp.mean(centered * centered, -1, keepdims=True) + EPSILON)
    normal = centered * inverse
    return (normal * gain_vec + shift_vec, normal, inverse)


def norm_backward(grad_in, normal, inverse, gain_vec):
    scaled = grad_in * gain_vec
    return inverse * (
        scaled
        - jnp.mean(scaled, -1, keepdims=True)
        - normal * jnp.mean(scaled * normal, -1, keepdims=True)
    )


def mask_bias(seg_col, seg_row, filled):
    keys = lax.broadcasted_iota(jnp.int32, (SLOTS, SLOTS), 0)
    places = lax.broadcasted_iota(jnp.int32, (SLOTS, SLOTS), 1)
    allowed = (seg_col == seg_row) & ((keys < filled) | (keys == places))
    return jnp.where(allowed, 0.0, MASKED)


def half_rows(rows, head):
    zeros = jnp.zeros((HEAD_DIM, rows.shape[1]), rows.dtype)
    return jnp.concatenate([rows, zeros] if head % 2 == 0 else [zeros, rows], 0)


def attend_kernel(fill_ref, x_ref, segc_ref, segr_ref, w_ref, b_ref, qkv_ref, ctx_ref, lse_ref, bias_ref):
    row = pl.program_id(0)

    @pl.when(pl.program_id(1) == 0)
    def _():
        bias_ref[...] = mask_bias(segc_ref[0], segr_ref[0], fill_ref[row])

    x = x_ref[...]
    weight = [w_ref[:, 0, i].reshape(D, WIDE) for i in range(3)]
    q = low(mul(x, weight[0]) + b_ref[0:1, :])
    k = low(mul(x, weight[1]))
    v = low(mul(x, weight[2]) + b_ref[1:2, :])
    qkv_ref[0] = q
    qkv_ref[1] = k
    qkv_ref[2] = v
    q_t = (q * jnp.bfloat16(SCALE)).T
    v_t = v.T
    ones = jnp.ones((HEAD_DIM, SLOTS), jnp.bfloat16)
    context = []
    for head in range(GROUP):
        own = slice(head * HEAD_DIM, (head + 1) * HEAD_DIM)
        pair = slice(head // 2 * PAIR, (head // 2 + 1) * PAIR)
        scores = mul(k[:, pair], half_rows(q_t[own], head)) + bias_ref[...]
        top = jnp.max(scores, 0, keepdims=True)
        probs = low(jnp.exp(scores - top))
        out = mul(jnp.concatenate([v_t[own], ones], 0), probs)
        total = out[HEAD_DIM : HEAD_DIM + 1]
        context.append(low(out[:HEAD_DIM] / total))
        lse_ref[0, 0, head : head + 1, :] = top + jnp.log(total)
    ctx_ref[...] = jnp.concatenate(context, 0).T


def attend_back_kernel(
    fill_ref, qkv_ref, ctx_ref, dctx_ref, lse_ref, segc_ref, segr_ref, w_ref, sum_ref, out_ref, qvb_ref, bias_ref, acc_ref
):
    row = pl.program_id(0)
    group = pl.program_id(1)

    @pl.when(group == 0)
    def _():
        bias_ref[...] = mask_bias(segc_ref[0], segr_ref[0], fill_ref[row])
        acc_ref[...] = wide(sum_ref[...])

    @pl.when((group == 0) & (row == 0))
    def _():
        qvb_ref[...] = jnp.zeros_like(qvb_ref)

    q = qkv_ref[0]
    k = qkv_ref[1]
    v = qkv_ref[2]
    d_out = dctx_ref[...]
    product = wide(d_out) * wide(ctx_ref[...])
    high = low(product)
    rest = low(product - wide(high))
    picks = lax.broadcasted_iota(jnp.int32, (16, WIDE), 1) // HEAD_DIM
    picks = low(jnp.where(picks == lax.broadcasted_iota(jnp.int32, (16, WIDE), 0), 1.0, 0.0))
    delta = mul(picks, high, NT) + mul(picks, rest, NT)
    q_t = (q * jnp.bfloat16(SCALE)).T
    k_t = k.T
    d_out_t = d_out.T
    d_q, d_k, d_v = [], [], []
    for head in range(GROUP):
        own = slice(head * HEAD_DIM, (head + 1) * HEAD_DIM)
        pair = slice(head // 2 * PAIR, (head // 2 + 1) * PAIR)
        scores = mul(k[:, pair], half_rows(q_t[own], head)) + bias_ref[...]
        probs = jnp.exp(scores - lse_ref[0, 0, head : head + 1, :])
        probs_grad = mul(v[:, pair], half_rows(d_out_t[own], head))
        scores_grad = low(probs * (probs_grad - delta[head : head + 1]))
        probs_low = low(probs)
        d_v.append(low(mul(d_out_t[own], probs_low, NT)))
        d_k.append(low(mul(q_t[own], scores_grad, NT)))
        d_q.append(low(mul(k_t[own], scores_grad) * SCALE))
    d_q = jnp.concatenate(d_q, 0).T
    d_k = jnp.concatenate(d_k, 0).T
    d_v = jnp.concatenate(d_v, 0).T
    columns = pl.ds(pl.multiple_of(group * WIDE, WIDE), WIDE)
    qvb_ref[0:1, columns] += jnp.sum(wide(d_q), 0, keepdims=True)
    qvb_ref[1:2, columns] += jnp.sum(wide(d_v), 0, keepdims=True)
    total = acc_ref[...]
    for i, grad in enumerate((d_q, d_k, d_v)):
        total = total + mul(grad, w_ref[:, 0, i].reshape(D, WIDE), NT)
    acc_ref[...] = total

    @pl.when(group == GROUPS - 1)
    def _():
        out_ref[...] = low(total)


def gelu_and_slope(v):
    phi = 0.5 * (1.0 + lax.erf(v * math.sqrt(0.5)))
    bell = jnp.exp(-0.5 * v * v) * (1.0 / math.sqrt(2.0 * math.pi))
    return v * phi, phi + v * bell


def feed_kernel(
    x_ref, ctx_ref, ct_ref, wo_ref, wi_ref, wd_ref, vec_ref, bi_ref,
    out_ref, dctx_ref, sum_ref, vecg_ref, big_ref, slope_ref,
):
    @pl.when(pl.program_id(0) == 0)
    def _():
        vecg_ref[...] = jnp.zeros_like(vecg_ref)
        big_ref[...] = jnp.zeros_like(big_ref)

    out_bias, gain_one, bias_one, down_bias, gain_two, bias_two = [vec_ref[i : i + 1, :] for i in range(6)]
    half = D // 2
    hidden = FF // 2
    ctx = ctx_ref[...]
    out_w = [wo_ref[:, t].reshape(D, half) for t in range(2)]
    attention = mul(ctx[:, :half], out_w[0], NT) + mul(ctx[:, half:], out_w[1], NT) + out_bias
    normed, normal_one, inverse_one = norm_forward(wide(x_ref[...]) + attention, gain_one, bias_one)
    normed_low = low(normed)
    branch = normed + down_bias
    chunks = [(t, c) for t in range(2) for c in range(hidden // HIDDEN)]
    for t, c in chunks:
        part = slice(c * HIDDEN, (c + 1) * HIDDEN)
        flat = slice(t * hidden + c * HIDDEN, t * hidden + (c + 1) * HIDDEN)
        inner = mul(normed_low, wi_ref[:, t, :, part].reshape(D, HIDDEN)) + bi_ref[0:1, flat]
        act, slope = gelu_and_slope(inner)
        slope_ref[:, flat] = low(slope)
        branch = branch + mul(low(act), wd_ref[:, t, :, part].reshape(D, HIDDEN), NT)
    final, normal_two, inverse_two = norm_forward(branch, gain_two, bias_two)
    out_ref[...] = low(final)
    final_grad = wide(ct_ref[...])
    sum_two = norm_backward(final_grad, normal_two, inverse_two, gain_two)
    branch_grad = low(sum_two)
    normed_grad = sum_two
    for t, c in chunks:
        part = slice(c * HIDDEN, (c + 1) * HIDDEN)
        flat = slice(t * hidden + c * HIDDEN, t * hidden + (c + 1) * HIDDEN)
        act_grad = mul(branch_grad, wd_ref[:, t, :, part].reshape(D, HIDDEN))
        inner_grad = low(act_grad * wide(slope_ref[:, flat]))
        big_ref[0:1, flat] += jnp.sum(wide(inner_grad), 0, keepdims=True)
        normed_grad = normed_grad + mul(inner_grad, wi_ref[:, t, :, part].reshape(D, HIDDEN), NT)
    sum_one = low(norm_backward(normed_grad, normal_one, inverse_one, gain_one))
    sum_ref[...] = sum_one
    for t in range(2):
        dctx_ref[:, t * half : (t + 1) * half] = low(mul(sum_one, out_w[t]))
    sums = (wide(sum_one), normed_grad, wide(branch_grad), final_grad)
    for i, term in enumerate(sums):
        vecg_ref[i : i + 1, :] += jnp.sum(term, 0, keepdims=True)


def params(grid_rank):
    return pltpu.CompilerParams(
        dimension_semantics=("arbitrary",) * grid_rank, vmem_limit_bytes=VMEM_BYTES
    )


def attend(tokens, seg_col, seg_row, fills, w_qkv, b_qv):
    rows = tokens.shape[0] // SLOTS
    n = w_qkv.shape[0]
    chunk = w_qkv.shape[3]
    return pl.pallas_call(
        attend_kernel,
        grid=(rows, GROUPS),
        in_specs=[
            pl.BlockSpec(memory_space=pltpu.SMEM),
            pl.BlockSpec((SLOTS, D), lambda r, g: (r, 0)),
            pl.BlockSpec((1, SLOTS, 1), lambda r, g: (r, 0, 0)),
            pl.BlockSpec((1, 1, SLOTS), lambda r, g: (r, 0, 0)),
            pl.BlockSpec((n, 1, 3, chunk, WIDE), lambda r, g: (0, g // 2, 0, 0, g % 2)),
            pl.BlockSpec((2, WIDE), lambda r, g: (0, g)),
        ],
        out_specs=[
            pl.BlockSpec((3, SLOTS, WIDE), lambda r, g: (0, r, g)),
            pl.BlockSpec((SLOTS, WIDE), lambda r, g: (r, g)),
            pl.BlockSpec((1, 1, GROUP, SLOTS), lambda r, g: (r, g, 0, 0)),
        ],
        out_shape=[
            jax.ShapeDtypeStruct((3, rows * SLOTS, D), jnp.bfloat16),
            jax.ShapeDtypeStruct((rows * SLOTS, D), jnp.bfloat16),
            jax.ShapeDtypeStruct((rows, GROUPS, GROUP, SLOTS), jnp.float32),
        ],
        scratch_shapes=[pltpu.VMEM((SLOTS, SLOTS), jnp.float32)],
        compiler_params=params(2),
        name="attend",
    )(fills, tokens, seg_col, seg_row, w_qkv, b_qv)


def attend_back(qkv, context, context_grad, lse, seg_col, seg_row, fills, w_qkv, sum_one):
    rows = context.shape[0] // SLOTS
    n = w_qkv.shape[0]
    chunk = w_qkv.shape[3]
    return pl.pallas_call(
        attend_back_kernel,
        grid=(rows, GROUPS),
        in_specs=[
            pl.BlockSpec(memory_space=pltpu.SMEM),
            pl.BlockSpec((3, SLOTS, WIDE), lambda r, g: (0, r, g)),
            pl.BlockSpec((SLOTS, WIDE), lambda r, g: (r, g)),
            pl.BlockSpec((SLOTS, WIDE), lambda r, g: (r, g)),
            pl.BlockSpec((1, 1, GROUP, SLOTS), lambda r, g: (r, g, 0, 0)),
            pl.BlockSpec((1, SLOTS, 1), lambda r, g: (r, 0, 0)),
            pl.BlockSpec((1, 1, SLOTS), lambda r, g: (r, 0, 0)),
            pl.BlockSpec((n, 1, 3, chunk, WIDE), lambda r, g: (0, g // 2, 0, 0, g % 2)),
            pl.BlockSpec((SLOTS, D), lambda r, g: (r, 0)),
        ],
        out_specs=[
            pl.BlockSpec((SLOTS, D), lambda r, g: (r, 0)),
            pl.BlockSpec((8, D), lambda r, g: (0, 0)),
        ],
        out_shape=[
            jax.ShapeDtypeStruct((rows * SLOTS, D), jnp.bfloat16),
            jax.ShapeDtypeStruct((8, D), jnp.float32),
        ],
        scratch_shapes=[
            pltpu.VMEM((SLOTS, SLOTS), jnp.float32),
            pltpu.VMEM((SLOTS, D), jnp.float32),
        ],
        compiler_params=params(2),
        name="attend_back",
    )(fills, qkv, context, context_grad, lse, seg_col, seg_row, w_qkv, sum_one)


def feed(tokens, context, cotangent, w_out, w_in, w_down, vectors, in_bias):
    count = tokens.shape[0]
    tile = pl.BlockSpec((TILE, D), lambda i: (i, 0))

    def whole(array):
        return pl.BlockSpec(array.shape, lambda i: (0,) * array.ndim, pipeline_mode=pl.Buffered(1))

    return pl.pallas_call(
        feed_kernel,
        grid=(count // TILE,),
        in_specs=[tile, tile, tile] + [whole(a) for a in (w_out, w_in, w_down, vectors, in_bias)],
        out_specs=[
            tile,
            tile,
            tile,
            pl.BlockSpec((8, D), lambda i: (0, 0)),
            pl.BlockSpec((8, FF), lambda i: (0, 0)),
        ],
        out_shape=[
            jax.ShapeDtypeStruct((count, D), jnp.bfloat16),
            jax.ShapeDtypeStruct((count, D), jnp.bfloat16),
            jax.ShapeDtypeStruct((count, D), jnp.bfloat16),
            jax.ShapeDtypeStruct((8, D), jnp.float32),
            jax.ShapeDtypeStruct((8, FF), jnp.float32),
        ],
        scratch_shapes=[pltpu.VMEM((TILE, FF), jnp.bfloat16)],
        compiler_params=params(1),
        name="feed",
    )(tokens, context, cotangent, w_out, w_in, w_down, vectors, in_bias)


def layer(tokens, cotangent, segments, fills, w_qkv, w_out, w_in, w_down, b_qv, vectors, in_bias):
    seg_col = segments[:, :, None]
    seg_row = segments[:, None, :]
    qkv, context, lse = attend(tokens, seg_col, seg_row, fills, w_qkv, b_qv)
    layer_out, context_grad, sum_one, vec_grads, in_grads = feed(
        tokens, context, cotangent, w_out, w_in, w_down, vectors, in_bias
    )
    tokens_grad, qv_grads = attend_back(
        qkv, context, context_grad, lse, seg_col, seg_row, fills, w_qkv, sum_one
    )
    return layer_out, tokens_grad, qv_grads, vec_grads, in_grads


def shards(
    tokens,
    segment_ids,
    fill_counts,
    qkv_weight,
    qv_bias,
    out_weight,
    out_bias,
    norm1_gain,
    norm1_bias,
    in_weight,
    in_bias,
    down_weight,
    down_bias,
    norm2_gain,
    norm2_bias,
    cotangent,
):
    n = lax.axis_size("rows")
    core = lax.axis_index("tp")
    rows_here = tokens.shape[0] // SLOTS
    segments = lax.dynamic_slice_in_dim(segment_ids, core * rows_here, rows_here, 0)
    fills = lax.dynamic_slice_in_dim(fill_counts, core * rows_here, rows_here, 0)

    def gather(shard):
        whole = lax.all_gather(shard, ("rows", "tp"), axis=0, tiled=False)
        return whole.reshape((n, 2) + shard.shape)

    w_qkv = gather(qkv_weight)
    w_out = gather(out_weight.T)
    w_in = gather(in_weight)
    w_down = gather(down_weight.T)

    own = jnp.concatenate([qv_bias.reshape(-1), in_bias])
    other = lax.ppermute(own, "tp", [(0, 1), (1, 0)])
    both = jnp.where(core == 0, jnp.stack([own, other]), jnp.stack([other, own])).astype(jnp.float32)
    width = qv_bias.shape[1]
    b_qv = both[:, : 2 * width].reshape(2, 2, width).transpose(1, 0, 2).reshape(2, 2 * width)
    b_in = both[:, 2 * width :].reshape(1, -1)
    vectors = wide(
        jnp.stack([out_bias, norm1_gain, norm1_bias, down_bias, norm2_gain, norm2_bias, out_bias, out_bias])
    )
    layer_out, tokens_grad, qv_grads, vec_grads, in_grads = layer(
        tokens, cotangent, segments, fills, w_qkv, w_out, w_in, w_down, b_qv, vectors, b_in
    )
    qv, vec, hid = lax.psum((qv_grads[:2], vec_grads[:4], in_grads[0]), ("rows", "tp"))
    return (layer_out, tokens_grad, qv, vec[0], vec[1], hid, vec[2], vec[3])


def solution(mesh):
    return jax.shard_map(
        shards,
        mesh=mesh,
        in_specs=(
            P(("rows", "tp"), None),
            P("rows", None),
            P("rows"),
            P(None, "rows", "tp"),
            P(None, "tp"),
            P("tp", "rows"),
            P(),
            P(),
            P(),
            P("rows", "tp"),
            P("tp"),
            P("tp", "rows"),
            P(),
            P(),
            P(),
            P(("rows", "tp"), None),
        ),
        out_specs=(P(("rows", "tp"), None), P(("rows", "tp"), None), P(), P(), P(), P(), P(), P()),
        check_vma=False,
    )
```

```python
from functools import partial
import math

import jax
import jax.numpy as jnp
from jax import lax
from jax.experimental import pallas as pl
from jax.experimental.pallas import tpu as pltpu
from jax.sharding import PartitionSpec as P

D = 1024
FF = 4096
HEADS = 16
HEAD_DIM = 64
SLOTS = 512
GROUP = 4
WIDE = GROUP * HEAD_DIM
PAIR = 2 * HEAD_DIM
GROUPS = HEADS // GROUP
TILE = 256
HIDDEN = 512
EPSILON = 1e-05
MASKED = -1e30
SCALE = 1.0 / math.sqrt(HEAD_DIM)
VMEM_BYTES = 60 * 2**20

NN = (((1,), (0,)), ((), ()))
NT = (((1,), (1,)), ((), ()))


def mul(left, right, dims=NN):
    return lax.dot_general(left, right, dims, preferred_element_type=jnp.float32)


def low(values):
    return values.astype(jnp.bfloat16)


def wide(values):
    return values.astype(jnp.float32)


def norm_forward(summed, gain_vec, shift_vec):
    row_mean = jnp.mean(summed, -1, keepdims=True)
    centered = summed - row_mean
    inverse = lax.rsqrt(jnp.mean(centered * centered, -1, keepdims=True) + EPSILON)
    normal = centered * inverse
    return (normal * gain_vec + shift_vec, normal, inverse)


def norm_backward(grad_in, normal, inverse, gain_vec):
    scaled = grad_in * gain_vec
    return inverse * (
        scaled
        - jnp.mean(scaled, -1, keepdims=True)
        - normal * jnp.mean(scaled * normal, -1, keepdims=True)
    )


def mask_bias(seg_col, seg_row, filled):
    keys = lax.broadcasted_iota(jnp.int32, (SLOTS, SLOTS), 0)
    places = lax.broadcasted_iota(jnp.int32, (SLOTS, SLOTS), 1)
    allowed = (seg_col == seg_row) & ((keys < filled) | (keys == places))
    return jnp.where(allowed, 0.0, MASKED)


def half_rows(rows, head):
    zeros = jnp.zeros((HEAD_DIM, rows.shape[1]), rows.dtype)
    return jnp.concatenate([rows, zeros] if head % 2 == 0 else [zeros, rows], 0)


def fetch(refs, scratch, sem, columns=None):
    copies = []
    half = len(refs) // 2
    for i, ref in enumerate(refs):
        size = ref.shape[0]
        if columns is not None:
            ref = ref.at[:, :, :, columns]
        target = scratch.at[i // half, pl.ds(i % half * size, size)]
        copies.append(pltpu.make_async_copy(ref, target, sem.at[i]))
        copies[-1].start()
    return copies


def set_weight(w_ref, slot_ref, other, part, columns=slice(None)):
    parts = [w_ref[slot_ref[other, c], part, :, columns] for c in range(w_ref.shape[0])]
    return jnp.concatenate(parts, 0)


def columns_of(w_ref, slot_ref, other, columns):
    there = w_ref.at[other]
    return jnp.concatenate([there[slot_ref[other, c], :, columns] for c in range(there.shape[0])], 0)


def attend_kernel(step, count, fill_ref, slot_ref, x_ref, segc_ref, segr_ref, b_ref, *rest):
    qkv_ref, ctx_ref, lse_ref, w_ref, sem = rest[-5:]

    @pl.when(pl.program_id(0) == 0)
    def _():
        copies = []
        for i, ref in enumerate(rest[:count]):
            size = ref.shape[0]
            source = ref.at[:, :, :, pl.ds(step % 2 * WIDE, WIDE)]
            copies.append(pltpu.make_async_copy(source, w_ref.at[pl.ds(i * size, size)], sem.at[i]))
            copies[-1].start()
        for copy in copies:
            copy.wait()

    x = x_ref[...]
    weight = [set_weight(w_ref, slot_ref, step // 2, i) for i in range(3)]
    bias = mask_bias(segc_ref[0], segr_ref[0], fill_ref[pl.program_id(0)])
    q = low(mul(x, weight[0]) + b_ref[0:1, :])
    k = low(mul(x, weight[1]))
    v = low(mul(x, weight[2]) + b_ref[1:2, :])
    qkv_ref[0] = q
    qkv_ref[1] = k
    qkv_ref[2] = v
    q_t = (q * jnp.bfloat16(SCALE)).T
    v_t = v.T
    ones = jnp.ones((HEAD_DIM, SLOTS), jnp.bfloat16)
    context = []
    for head in range(GROUP):
        own = slice(head * HEAD_DIM, (head + 1) * HEAD_DIM)
        pair = slice(head // 2 * PAIR, (head // 2 + 1) * PAIR)
        scores = mul(k[:, pair], half_rows(q_t[own], head)) + bias
        top = jnp.max(scores, 0, keepdims=True)
        probs = low(jnp.exp(scores - top))
        out = mul(jnp.concatenate([v_t[own], ones], 0), probs)
        total = out[HEAD_DIM : HEAD_DIM + 1]
        context.append(low(out[:HEAD_DIM] / total))
        lse_ref[0, 0, head : head + 1, :] = top + jnp.log(total)
    ctx_ref[...] = jnp.concatenate(context, 0).T


def attend_back_kernel(
    count, fill_ref, slot_ref, qkv_ref, ctx_ref, dctx_ref, lse_ref, segc_ref, segr_ref, *rest
):
    sum_ref, out_ref, qvb_ref, bias_ref, acc_ref, w_ref, sem = rest[-7:]
    row = pl.program_id(0)
    group = pl.program_id(1)

    @pl.when(group == 0)
    def _():
        bias_ref[...] = mask_bias(segc_ref[0], segr_ref[0], fill_ref[row])
        acc_ref[...] = wide(sum_ref[...])

    @pl.when((group == 0) & (row == 0))
    def _():
        qvb_ref[...] = jnp.zeros_like(qvb_ref)
        for copy in fetch(rest[:count], w_ref, sem):
            copy.wait()

    q = qkv_ref[0]
    k = qkv_ref[1]
    v = qkv_ref[2]
    d_out = dctx_ref[...]
    product = wide(d_out) * wide(ctx_ref[...])
    high = low(product)
    rest = low(product - wide(high))
    picks = lax.broadcasted_iota(jnp.int32, (16, WIDE), 1) // HEAD_DIM
    picks = low(jnp.where(picks == lax.broadcasted_iota(jnp.int32, (16, WIDE), 0), 1.0, 0.0))
    delta = mul(picks, high, NT) + mul(picks, rest, NT)
    q_t = (q * jnp.bfloat16(SCALE)).T
    k_t = k.T
    d_out_t = d_out.T
    d_q, d_k, d_v = [], [], []
    for head in range(GROUP):
        own = slice(head * HEAD_DIM, (head + 1) * HEAD_DIM)
        pair = slice(head // 2 * PAIR, (head // 2 + 1) * PAIR)
        scores = mul(k[:, pair], half_rows(q_t[own], head)) + bias_ref[...]
        probs = jnp.exp(scores - lse_ref[0, 0, head : head + 1, :])
        probs_grad = mul(v[:, pair], half_rows(d_out_t[own], head))
        scores_grad = low(probs * (probs_grad - delta[head : head + 1]))
        probs_low = low(probs)
        d_v.append(low(mul(d_out_t[own], probs_low, NT)))
        d_k.append(low(mul(q_t[own], scores_grad, NT)))
        d_q.append(low(mul(k_t[own], scores_grad) * SCALE))
    d_q = jnp.concatenate(d_q, 0).T
    d_k = jnp.concatenate(d_k, 0).T
    d_v = jnp.concatenate(d_v, 0).T
    columns = pl.ds(pl.multiple_of(group * WIDE, WIDE), WIDE)
    qvb_ref[0:1, columns] += jnp.sum(wide(d_q), 0, keepdims=True)
    qvb_ref[1:2, columns] += jnp.sum(wide(d_v), 0, keepdims=True)
    half_set = pl.ds(pl.multiple_of(group % 2 * WIDE, WIDE), WIDE)
    total = acc_ref[...]
    for i, grad in enumerate((d_q, d_k, d_v)):
        weight = set_weight(w_ref.at[group // 2], slot_ref, group // 2, i, half_set)
        total = total + mul(grad, weight, NT)
    acc_ref[...] = total

    @pl.when(group == GROUPS - 1)
    def _():
        out_ref[...] = low(total)


def gelu_and_slope(v):
    phi = 0.5 * (1.0 + lax.erf(v * math.sqrt(0.5)))
    bell = jnp.exp(-0.5 * v * v) * (1.0 / math.sqrt(2.0 * math.pi))
    return v * phi, phi + v * bell


FLAT = 1024
PIECES = 2 * FLAT // HIDDEN


def piece_weight(first_ref, late_ref, slot_ref, piece, down):
    ref, width = (first_ref, FLAT) if piece < PIECES else (late_ref, FF // 2 - FLAT)
    other, start = divmod(piece % PIECES * HIDDEN, width)
    return columns_of(ref, slot_ref, other, pl.ds(down * width + start, HIDDEN))


def out_columns(first_ref, slot_ref, group):
    return columns_of(first_ref, slot_ref, group // 2, pl.ds(2 * FLAT + group % 2 * WIDE, WIDE))


def vectors_of(vec_ref):
    return [vec_ref[i : i + 1, :] for i in range(6)]


def front_kernel(count, slot_ref, x_ref, ctx_ref, vec_ref, bi_ref, *rest):
    normal_ref, inv_ref, branch_ref, slope_ref, first_ref, sem = rest[-6:]

    @pl.when(pl.program_id(0) == 0)
    def _():
        for copy in fetch(rest[:count], first_ref, sem):
            copy.wait()

    out_bias, gain_one, bias_one, down_bias, _, _ = vectors_of(vec_ref)
    ctx = ctx_ref[...]
    attention = out_bias
    for group in range(GROUPS):
        columns = slice(group * WIDE, (group + 1) * WIDE)
        attention = attention + mul(ctx[:, columns], out_columns(first_ref, slot_ref, group), NT)
    normed, normal_one, inverse_one = norm_forward(wide(x_ref[...]) + attention, gain_one, bias_one)
    normal_ref[...] = normal_one
    inv_ref[...] = jnp.broadcast_to(inverse_one, inv_ref.shape)
    normed_low = low(normed)
    branch = normed + down_bias
    for piece in range(PIECES):
        flat = slice(piece * HIDDEN, (piece + 1) * HIDDEN)
        inner = mul(normed_low, piece_weight(first_ref, None, slot_ref, piece, 0)) + bi_ref[0:1, flat]
        act, slope = gelu_and_slope(inner)
        slope_ref[:, flat] = low(slope)
        branch = branch + mul(low(act), piece_weight(first_ref, None, slot_ref, piece, 1), NT)
    branch_ref[...] = branch


def back_kernel(
    counts, slot_ref, normal_ref, inv_ref, branch_ref, slope_ref, ct_ref, vec_ref, bi_ref, *rest
):
    out_ref, dctx_ref, sum_ref, vecg_ref, big_ref, keep_ref, first_ref, first_sem, late_ref, late_sem = rest[-10:]

    @pl.when(pl.program_id(0) == 0)
    def _():
        vecg_ref[...] = jnp.zeros_like(vecg_ref)
        big_ref[...] = jnp.zeros_like(big_ref)
        late = fetch(rest[counts[0] : sum(counts)], late_ref, late_sem)
        for copy in late + fetch(rest[: counts[0]], first_ref, first_sem):
            copy.wait()

    _, gain_one, bias_one, _, gain_two, bias_two = vectors_of(vec_ref)
    weight = partial(piece_weight, first_ref, late_ref, slot_ref)
    normal_one = normal_ref[...]
    inverse_one = inv_ref[:, 0:1]
    normed_low = low(normal_one * gain_one + bias_one)
    branch = branch_ref[...]
    for piece in range(PIECES, FF // HIDDEN):
        flat = slice(piece * HIDDEN, (piece + 1) * HIDDEN)
        inner = mul(normed_low, weight(piece, 0)) + bi_ref[0:1, flat]
        act, slope = gelu_and_slope(inner)
        keep_ref[:, (piece - PIECES) * HIDDEN : (piece - PIECES + 1) * HIDDEN] = low(slope)
        branch = branch + mul(low(act), weight(piece, 1), NT)
    final, normal_two, inverse_two = norm_forward(branch, gain_two, bias_two)
    out_ref[...] = low(final)
    final_grad = wide(ct_ref[...])
    sum_two = norm_backward(final_grad, normal_two, inverse_two, gain_two)
    branch_grad = low(sum_two)
    normed_grad = sum_two
    for piece in range(FF // HIDDEN):
        flat = slice(piece * HIDDEN, (piece + 1) * HIDDEN)
        if piece < PIECES:
            slope = slope_ref[:, flat]
        else:
            slope = keep_ref[:, (piece - PIECES) * HIDDEN : (piece - PIECES + 1) * HIDDEN]
        inner_grad = low(mul(branch_grad, weight(piece, 1)) * wide(slope))
        big_ref[0:1, flat] += jnp.sum(wide(inner_grad), 0, keepdims=True)
        normed_grad = normed_grad + mul(inner_grad, weight(piece, 0), NT)
    sum_one = low(norm_backward(normed_grad, normal_one, inverse_one, gain_one))
    sum_ref[...] = sum_one
    for group in range(GROUPS):
        columns = slice(group * WIDE, (group + 1) * WIDE)
        dctx_ref[:, columns] = low(mul(sum_one, out_columns(first_ref, slot_ref, group)))
    sums = (wide(sum_one), normed_grad, wide(branch_grad), final_grad)
    for i, term in enumerate(sums):
        vecg_ref[i : i + 1, :] += jnp.sum(term, 0, keepdims=True)


def params(grid_rank):
    return pltpu.CompilerParams(
        dimension_semantics=("arbitrary",) * grid_rank, vmem_limit_bytes=VMEM_BYTES
    )


def cost(flops, moved):
    return pl.CostEstimate(flops=int(flops), bytes_accessed=int(moved), transcendentals=0)


SCALARS = pl.BlockSpec(memory_space=pltpu.SMEM)
ANYWHERE = pl.BlockSpec(memory_space=pl.ANY)


def whole(array):
    return pl.BlockSpec(array.shape, lambda *_: (0,) * array.ndim, pipeline_mode=pl.Buffered(1))


def slot_scratch(pieces):
    half = len(pieces) // 2
    n = sum(w.shape[0] for w in pieces[:half])
    return [
        pltpu.VMEM((2, n) + pieces[0].shape[1:], pieces[0].dtype),
        pltpu.SemaphoreType.DMA((len(pieces),)),
    ]


def attend(step, earlier, tokens, seg_col, seg_row, fills, slots, pieces, bias):
    rows = tokens.shape[0] // SLOTS
    return pl.pallas_call(
        partial(attend_kernel, step, len(pieces)),
        grid=(rows,),
        in_specs=[
            SCALARS,
            SCALARS,
            pl.BlockSpec((SLOTS, D), lambda r: (r, 0)),
            pl.BlockSpec((1, SLOTS, 1), lambda r: (r, 0, 0)),
            pl.BlockSpec((1, 1, SLOTS), lambda r: (r, 0, 0)),
            whole(bias),
        ]
        + [ANYWHERE] * (len(pieces) + len(earlier)),
        out_specs=[
            pl.BlockSpec((3, SLOTS, WIDE), lambda r: (0, r, step)),
            pl.BlockSpec((SLOTS, WIDE), lambda r: (r, step)),
            pl.BlockSpec((1, 1, GROUP, SLOTS), lambda r: (r, step, 0, 0)),
        ],
        out_shape=[
            jax.ShapeDtypeStruct((3, rows * SLOTS, D), jnp.bfloat16),
            jax.ShapeDtypeStruct((rows * SLOTS, D), jnp.bfloat16),
            jax.ShapeDtypeStruct((rows, GROUPS, GROUP, SLOTS), jnp.float32),
        ],
        scratch_shapes=[
            pltpu.VMEM((sum(w.shape[0] for w in pieces),) + pieces[0].shape[1:3] + (WIDE,), jnp.bfloat16),
            pltpu.SemaphoreType.DMA((len(pieces),)),
        ],
        input_output_aliases={6 + len(pieces) + i: i for i in range(len(earlier))},
        compiler_params=params(1),
        cost_estimate=cost(15e9, 10e6),
        name="attend",
    )(fills, slots, tokens, seg_col, seg_row, bias, *pieces, *earlier)


def attend_back(qkv, context, context_grad, lse, seg_col, seg_row, fills, slots, weights, sum_one):
    rows = context.shape[0] // SLOTS
    return pl.pallas_call(
        partial(attend_back_kernel, len(weights)),
        grid=(rows, GROUPS),
        in_specs=[
            SCALARS,
            SCALARS,
            pl.BlockSpec((3, SLOTS, WIDE), lambda r, g: (0, r, g)),
            pl.BlockSpec((SLOTS, WIDE), lambda r, g: (r, g)),
            pl.BlockSpec((SLOTS, WIDE), lambda r, g: (r, g)),
            pl.BlockSpec((1, 1, GROUP, SLOTS), lambda r, g: (r, g, 0, 0)),
            pl.BlockSpec((1, SLOTS, 1), lambda r, g: (r, 0, 0)),
            pl.BlockSpec((1, 1, SLOTS), lambda r, g: (r, 0, 0)),
        ]
        + [ANYWHERE] * len(weights)
        + [pl.BlockSpec((SLOTS, D), lambda r, g: (r, 0))],
        out_specs=[
            pl.BlockSpec((SLOTS, D), lambda r, g: (r, 0)),
            pl.BlockSpec((8, D), lambda r, g: (0, 0)),
        ],
        out_shape=[
            jax.ShapeDtypeStruct((rows * SLOTS, D), jnp.bfloat16),
            jax.ShapeDtypeStruct((8, D), jnp.float32),
        ],
        scratch_shapes=[
            pltpu.VMEM((SLOTS, SLOTS), jnp.float32),
            pltpu.VMEM((SLOTS, D), jnp.float32),
        ]
        + slot_scratch(weights),
        compiler_params=params(2),
        cost_estimate=cost(50e9, 30e6),
        name="attend_back",
    )(fills, slots, qkv, context, context_grad, lse, seg_col, seg_row, *weights, sum_one)


def tiles(width):
    return pl.BlockSpec((TILE, width), lambda i: (i, 0))


def feed_front(slots, tokens, context, first, vectors, in_bias):
    count = tokens.shape[0]
    return pl.pallas_call(
        partial(front_kernel, len(first)),
        grid=(count // TILE,),
        in_specs=[SCALARS, tiles(D), tiles(D), whole(vectors), whole(in_bias)] + [ANYWHERE] * len(first),
        out_specs=[tiles(D), tiles(128), tiles(D), tiles(2 * FLAT)],
        out_shape=[
            jax.ShapeDtypeStruct((count, D), jnp.float32),
            jax.ShapeDtypeStruct((count, 128), jnp.float32),
            jax.ShapeDtypeStruct((count, D), jnp.float32),
            jax.ShapeDtypeStruct((count, 2 * FLAT), jnp.bfloat16),
        ],
        scratch_shapes=slot_scratch(first),
        compiler_params=params(1),
        cost_estimate=cost(25e9, 30e6),
        name="feed_front",
    )(slots, tokens, context, vectors, in_bias, *first)


def feed_back(slots, front, cotangent, first, late, vectors, in_bias):
    count = cotangent.shape[0]
    return pl.pallas_call(
        partial(back_kernel, (len(first), len(late))),
        grid=(count // TILE,),
        in_specs=[SCALARS, tiles(D), tiles(128), tiles(D), tiles(2 * FLAT), tiles(D), whole(vectors), whole(in_bias)]
        + [ANYWHERE] * (len(first) + len(late)),
        out_specs=[
            tiles(D),
            tiles(D),
            tiles(D),
            pl.BlockSpec((8, D), lambda i: (0, 0)),
            pl.BlockSpec((8, FF), lambda i: (0, 0)),
        ],
        out_shape=[
            jax.ShapeDtypeStruct((count, D), jnp.bfloat16),
            jax.ShapeDtypeStruct((count, D), jnp.bfloat16),
            jax.ShapeDtypeStruct((count, D), jnp.bfloat16),
            jax.ShapeDtypeStruct((8, D), jnp.float32),
            jax.ShapeDtypeStruct((8, FF), jnp.float32),
        ],
        scratch_shapes=[pltpu.VMEM((TILE, FF - 2 * FLAT), jnp.bfloat16)] + slot_scratch(first) + slot_scratch(late),
        compiler_params=params(1),
        cost_estimate=cost(75e9, 40e6),
        name="feed_back",
    )(slots, *front, cotangent, vectors, in_bias, *first, *late)


def stage_bits(n):
    bits = n.bit_length() - 1
    in_z = -(-bits // 3)
    in_y = -(-(bits - in_z) // 2)
    in_x = bits - in_z - in_y
    x = list(range(in_x))
    y = list(range(in_x, in_x + in_y))
    z = list(range(in_x + in_y, bits))
    return z + y + x, z[::-1] + x + y


def partner(block, n, stage):
    bits = [order[stage] for order in stage_bits(n)]
    pairs = [(2 * i + core, 2 * (i ^ (1 << bits[core])) + core) for i in range(n) for core in range(2)]
    return lax.ppermute(block, ("rows", "tp"), pairs)


def joined(*blocks):
    return jnp.concatenate(blocks, 0)


def swap_cores(block):
    return lax.ppermute(block, "tp", [(0, 1), (1, 0)])


def after(value, *earlier):
    return lax.optimization_barrier((value, earlier))[0]


def together(*values):
    return lax.optimization_barrier(values)


def slot_table(n):
    apart = jnp.arange(n, dtype=jnp.int32) ^ lax.axis_index("rows")
    tables = []
    for order in stage_bits(n):
        tables.append(sum(((apart >> bit) & 1) << place for place, bit in enumerate(order)))
    core = lax.axis_index("tp")
    return jnp.where(core == 0, jnp.stack(tables), jnp.stack(tables[::-1]))


def sum_over_all(values, n):
    values = values + swap_cores(values)
    step = 1
    while step < n:
        values = values + lax.ppermute(values, "rows", [(i, i ^ step) for i in range(n)])
        step *= 2
    return values


def shards(
    tokens,
    segment_ids,
    fill_counts,
    qkv_weight,
    qv_bias,
    out_weight,
    out_bias,
    norm1_gain,
    norm1_bias,
    in_weight,
    in_bias,
    down_weight,
    down_bias,
    norm2_gain,
    norm2_bias,
    cotangent,
):
    n = lax.axis_size("rows")
    core = lax.axis_index("tp")
    rows_here = tokens.shape[0] // SLOTS
    down_t = down_weight.T
    width = qv_bias.shape[1]

    last = n.bit_length() - 2

    def spread(blocks, stages):
        for stage in stages:
            blocks = blocks + [partner(block, n, stage) for block in blocks]
        return blocks

    middle = range(2, last)
    q = qkv_weight[None]
    q = joined(q, partner(q, n, 0))
    q = joined(q, partner(q, n, 1))
    first = jnp.concatenate([in_weight[:, :FLAT], down_t[:, :FLAT], out_weight.T], 1)[None]
    q, first = together(q, first)
    q_own = spread([q], middle)
    first = joined(first, partner(first, n, 0))
    segments = lax.dynamic_slice_in_dim(segment_ids, core * rows_here, rows_here, 0)
    fills = lax.dynamic_slice_in_dim(fill_counts, core * rows_here, rows_here, 0)
    seg_col = segments[:, :, None]
    seg_row = segments[:, None, :]
    slots = slot_table(n)
    own = jnp.concatenate([qv_bias.reshape(-1), in_bias])
    other = swap_cores(own)
    by_distance = [wide(b) for b in (own, other)]
    b_qv = [b[: 2 * width].reshape(2, width) for b in by_distance]
    b_in = [b[2 * width :] for b in by_distance]
    b_hidden = jnp.concatenate([b_in[0][:FLAT], b_in[1][:FLAT], b_in[0][FLAT:], b_in[1][FLAT:]]).reshape(1, -1)
    vectors = wide(
        jnp.concatenate([out_bias, norm1_gain, norm1_bias, down_bias, norm2_gain, norm2_bias, out_bias, out_bias])
    ).reshape(8, D)
    small = (seg_col, seg_row, fills, slots, b_qv, b_hidden, vectors)
    q_own, first, small = together(q_own, first, small)
    seg_col, seg_row, fills, slots, b_qv, b_hidden, vectors = small
    q_own = spread(q_own, [last])
    first_got = partner(first, n, 1)

    def run(step, earlier):
        bias = b_qv[step // 2][:, step % 2 * WIDE : (step % 2 + 1) * WIDE]
        pieces = q_others if step >= 2 else q_own
        return attend(step, earlier, tokens, seg_col, seg_row, fills, slots, pieces, bias)

    late = jnp.concatenate([in_weight[:, FLAT:], down_t[:, FLAT:]], 1)[None]
    q_own, first_got, late = together(q_own, first_got, late)
    first = joined(first, first_got)
    q_others = [swap_cores(w) for w in q_own]
    first_own = spread([first], middle)
    late_got = partner(late, n, 0)
    results = run(0, ())
    results, first_own, late_got, q_others = together(results, first_own, late_got, q_others)
    late = joined(late, late_got)
    first_own = spread(first_own, [last])
    late_got = partner(late, n, 1)
    results = run(1, results)
    results = run(2, results)
    results, first_own, late_got = together(results, first_own, late_got)
    late = joined(late, late_got)
    first_others = [swap_cores(w) for w in first_own]
    late_own = spread([late], middle)
    results = run(3, results)
    results, late_own = together(results, late_own)
    late_own = spread(late_own, [last])

    qkv, context, lse = results
    first = first_own + first_others
    front = feed_front(slots, tokens, context, first, vectors, b_hidden)
    front, late_own = together(front, late_own)
    late = late_own + [swap_cores(w) for w in late_own]
    layer_out, context_grad, sum_one, vec_grads, in_grads = feed_back(
        slots, front, cotangent, first, late, vectors, b_hidden
    )
    hidden = in_grads[0].reshape(2, 2, FF // 4)
    hidden = jnp.where(core == 0, hidden, hidden[:, ::-1]).transpose(1, 0, 2)
    early = jnp.concatenate([vec_grads[:4].reshape(-1), hidden.reshape(-1)])
    early = jnp.sum(lax.all_gather(early, ("rows", "tp"), axis=0), 0)
    vec = early[: 4 * D].reshape(4, D)

    tokens_grad, qv_grads = attend_back(
        qkv, context, context_grad, lse, seg_col, seg_row, fills, slots, q_own + q_others, sum_one
    )
    qv = qv_grads[:2].reshape(2, 2, D // 2)
    qv = jnp.where(core == 0, qv, qv[:, ::-1]).reshape(2, D)
    qv = sum_over_all(qv, n)
    return (layer_out, tokens_grad, qv, vec[0], vec[1], early[4 * D :], vec[2], vec[3])


def solution(mesh):
    return jax.shard_map(
        shards,
        mesh=mesh,
        in_specs=(
            P(("rows", "tp"), None),
            P("rows", None),
            P("rows"),
            P(None, "rows", "tp"),
            P(None, "tp"),
            P("tp", "rows"),
            P(),
            P(),
            P(),
            P("rows", "tp"),
            P("tp"),
            P("tp", "rows"),
            P(),
            P(),
            P(),
            P(("rows", "tp"), None),
        ),
        out_specs=(P(("rows", "tp"), None), P(("rows", "tp"), None), P(), P(), P(), P(), P(), P()),
        check_vma=False,
    )
```

```python
from functools import partial
import math

import jax
import jax.numpy as jnp
from jax import lax
from jax.experimental import pallas as pl
from jax.experimental.pallas import tpu as pltpu
from jax.sharding import PartitionSpec as P

D = 1024
FF = 4096
HEADS = 16
HEAD_DIM = 64
SLOTS = 512
GROUP = 4
WIDE = GROUP * HEAD_DIM
PAIR = 2 * HEAD_DIM
GROUPS = HEADS // GROUP
TILE = 256
HIDDEN = 1024
STRIP = 32
EPSILON = 1e-05
MASKED = -1e30
SCALE = 1.0 / math.sqrt(HEAD_DIM)
VMEM_BYTES = 60 * 2**20

NN = (((1,), (0,)), ((), ()))
NT = (((1,), (1,)), ((), ()))
TT = (((0,), (1,)), ((), ()))


def mul(left, right, dims=NN):
    return lax.dot_general(left, right, dims, preferred_element_type=jnp.float32)


def low(values):
    return values.astype(jnp.bfloat16)


def wide(values):
    return values.astype(jnp.float32)


def norm_forward(summed, gain_vec, shift_vec):
    row_mean = jnp.mean(summed, -1, keepdims=True)
    centered = summed - row_mean
    inverse = lax.rsqrt(jnp.mean(centered * centered, -1, keepdims=True) + EPSILON)
    normal = centered * inverse
    return (normal * gain_vec + shift_vec, normal, inverse)


def norm_backward(grad_in, normal, inverse, gain_vec):
    scaled = grad_in * gain_vec
    return inverse * (
        scaled
        - jnp.mean(scaled, -1, keepdims=True)
        - normal * jnp.mean(scaled * normal, -1, keepdims=True)
    )


def mask_bias(seg_col, seg_row, filled):
    keys = lax.broadcasted_iota(jnp.int32, (SLOTS, SLOTS), 0)
    places = lax.broadcasted_iota(jnp.int32, (SLOTS, SLOTS), 1)
    allowed = (seg_col == seg_row) & ((keys < filled) | (keys == places))
    return jnp.where(allowed, 0.0, MASKED)


def half_rows(rows, head):
    zeros = jnp.zeros((HEAD_DIM, rows.shape[1]), rows.dtype)
    return jnp.concatenate([rows, zeros] if head % 2 == 0 else [zeros, rows], 0)


def fetch(refs, scratch, sem, columns=None, start=True):
    copies = []
    half = len(refs) // 2
    for i, ref in enumerate(refs):
        size = ref.shape[0]
        target = scratch.at[i // half, pl.ds(i % half * size, size)]
        if columns is not None:
            ref, target = ref.at[:, :, columns], target.at[:, :, columns]
        copies.append(pltpu.make_async_copy(ref, target, sem.at[i]))
        if start:
            copies[-1].start()
    return copies


def first_or_later(step, body):
    @pl.when(step == 0)
    def _():
        body(True)

    @pl.when(step != 0)
    def _():
        body(False)


def wait_all(copies):
    for copy in copies:
        copy.wait()


def set_weight(w_ref, slot_ref, other, part, columns=slice(None)):
    parts = [w_ref[slot_ref[other, c], part, :, columns] for c in range(w_ref.shape[0])]
    return jnp.concatenate(parts, 0)


def columns_of(w_ref, slot_ref, other, columns):
    there = w_ref.at[other]
    return jnp.concatenate([there[slot_ref[other, c], :, columns] for c in range(there.shape[0])], 0)


def attend_kernel(step, count, fill_ref, slot_ref, x_ref, segc_ref, segr_ref, b_ref, *rest):
    qk_ref, kv_ref, ctx_ref, lse_ref, w_ref, sem = rest[-6:]

    @pl.when(pl.program_id(0) == 0)
    def _():
        copies = []
        for i, ref in enumerate(rest[:count]):
            size = ref.shape[0]
            source = ref.at[:, :, :, pl.ds(step % 2 * WIDE, WIDE)]
            copies.append(pltpu.make_async_copy(source, w_ref.at[pl.ds(i * size, size)], sem.at[i]))
            copies[-1].start()
        for copy in copies:
            copy.wait()

    x = x_ref[...]
    weight = [set_weight(w_ref, slot_ref, step // 2, i) for i in range(3)]
    bias = mask_bias(segc_ref[0], segr_ref[0], fill_ref[pl.program_id(0)])
    q = low(mul(x, weight[0]) + b_ref[0:1, :])
    k = low(mul(x, weight[1]))
    v = low(mul(x, weight[2]) + b_ref[1:2, :])
    q_t = (q * jnp.bfloat16(SCALE)).T
    v_t = v.T
    qk_ref[0, 0] = q_t
    qk_ref[1, 0] = k.T
    kv_ref[0] = k
    kv_ref[1] = v
    ones = jnp.ones((HEAD_DIM, SLOTS), jnp.bfloat16)

    def score(head):
        own = slice(head * HEAD_DIM, (head + 1) * HEAD_DIM)
        pair = slice(head // 2 * PAIR, (head // 2 + 1) * PAIR)
        return mul(k[:, pair], half_rows(q_t[own], head)) + bias

    def finish(head, top, probs):
        own = slice(head * HEAD_DIM, (head + 1) * HEAD_DIM)
        out = mul(jnp.concatenate([v_t[own], ones], 0), probs)
        total = out[HEAD_DIM : HEAD_DIM + 1]
        ctx_ref[0, own] = low(out[:HEAD_DIM] / total)
        lse_ref[0, 0, head : head + 1, :] = top + jnp.log(total)

    scores = score(0)
    done = None
    for head in range(GROUP):
        following = score(head + 1) if head + 1 < GROUP else None
        if done is not None:
            finish(head - 1, *done)
        top = jnp.max(scores, 0, keepdims=True)
        done = top, low(jnp.exp(scores - top))
        scores = following
    finish(GROUP - 1, *done)


def attend_back_kernel(count, fill_ref, slot_ref, qk_ref, kv_ref, dctx_ref, delta_ref, lse_ref, segc_ref, segr_ref, *rest):
    sum_ref, out_ref, qvb_ref, bias_ref, acc_ref, w_ref, sem = rest[-7:]
    row = pl.program_id(0)
    group = pl.program_id(1)

    @pl.when(group == 0)
    def _():
        bias_ref[...] = mask_bias(segc_ref[0], segr_ref[0], fill_ref[row])
        acc_ref[...] = wide(sum_ref[...])

    def body(arriving):
        if arriving:
            qvb_ref[...] = jnp.zeros_like(qvb_ref)
            fetch(rest[:count], w_ref, sem)
        d_q, d_k, d_v = [], [], []
        for head in range(GROUP):
            own = slice(head * HEAD_DIM, (head + 1) * HEAD_DIM)
            pair = slice(head // 2 * PAIR, (head // 2 + 1) * PAIR)
            q_t, k_t, d_out_t = qk_ref[0, 0, own], qk_ref[1, 0, own], dctx_ref[0, own]
            scores = mul(kv_ref[0, :, pair], half_rows(q_t, head)) + bias_ref[...]
            probs = jnp.exp(scores - lse_ref[0, 0, head : head + 1, :])
            probs_grad = mul(kv_ref[1, :, pair], half_rows(d_out_t, head))
            scores_grad = low(probs * (probs_grad - delta_ref[0, 0, head : head + 1, :]))
            probs_low = low(probs)
            d_v.append(low(mul(d_out_t, probs_low, NT)))
            d_k.append(low(mul(q_t, scores_grad, NT)))
            d_q.append(low(mul(k_t, scores_grad) * SCALE))
        if arriving:
            wait_all(fetch(rest[:count], w_ref, sem, start=False))
        ones = jnp.ones((16, SLOTS), jnp.bfloat16)
        columns = pl.ds(pl.multiple_of(group * WIDE, WIDE), WIDE)
        half_set = pl.ds(pl.multiple_of(group % 2 * WIDE, WIDE), WIDE)
        total = acc_ref[...]
        for i, grad in enumerate((d_q, d_k, d_v)):
            grad = jnp.concatenate(grad, 0)
            weight = set_weight(w_ref.at[group // 2], slot_ref, group // 2, i, half_set)
            total = total + mul(grad, weight, TT)
            if i != 1:
                qvb_ref[i // 2 : i // 2 + 1, columns] += mul(ones, grad, NT)[0:1]
        acc_ref[...] = total

    first_or_later(row * GROUPS + group, body)

    @pl.when(group == GROUPS - 1)
    def _():
        out_ref[...] = low(acc_ref[...])


def gelu_and_slope(v):
    phi = 0.5 * (1.0 + lax.erf(v * math.sqrt(0.5)))
    bell = jnp.exp(-0.5 * v * v) * (1.0 / math.sqrt(2.0 * math.pi))
    return v * phi, phi + v * bell


FLAT = 1024
PIECES = 2 * FLAT // HIDDEN


def piece_weight(first_ref, late_ref, slot_ref, piece, down):
    ref, width = (first_ref, FLAT) if piece < PIECES else (late_ref, FF // 2 - FLAT)
    other, start = divmod(piece % PIECES * HIDDEN, width)
    return columns_of(ref, slot_ref, other, pl.ds(down * width + start, HIDDEN))


def out_columns(first_ref, slot_ref, group):
    return columns_of(first_ref, slot_ref, group // 2, pl.ds(2 * FLAT + group % 2 * WIDE, WIDE))


def vectors_of(vec_ref):
    return [vec_ref[i : i + 1, :] for i in range(6)]


def front_kernel(count, slot_ref, x_ref, ctx_ref, vec_ref, bi_ref, *rest):
    normal_ref, inv_ref, branch_ref, slope_ref, low_ref, first_ref, sem = rest[-7:]


    @pl.when(pl.program_id(0) == 0)
    def _():
        wait_all(fetch(rest[:count], first_ref, sem))

    out_bias, gain_one, bias_one, down_bias, _, _ = vectors_of(vec_ref)
    attention = out_bias
    for group in range(GROUPS):
        part = slice(group * WIDE, (group + 1) * WIDE)
        attention = attention + mul(ctx_ref[0, part], out_columns(first_ref, slot_ref, group), TT)
    branch_ref[...] = attention
    for start in range(0, TILE, STRIP):
        rows = slice(start, start + STRIP)
        normed, normal_one, inverse_one = norm_forward(wide(x_ref[rows]) + branch_ref[rows], gain_one, bias_one)
        normal_ref[rows] = normal_one
        inv_ref[rows] = jnp.broadcast_to(inverse_one, (STRIP, 128))
        low_ref[rows] = low(normed)
        branch_ref[rows] = normed + down_bias
    normed_low = low_ref[...]
    branch = branch_ref[...]

    for piece in range(PIECES):
        flat = slice(piece * HIDDEN, (piece + 1) * HIDDEN)
        inner = mul(normed_low, piece_weight(first_ref, None, slot_ref, piece, 0)) + bi_ref[0:1, flat]
        act, slope = gelu_and_slope(inner)
        slope_ref[:, flat] = low(slope)
        branch = branch + mul(low(act), piece_weight(first_ref, None, slot_ref, piece, 1), NT)
    branch_ref[...] = branch


def back_kernel(
    counts, slot_ref, normal_ref, inv_ref, branch_ref, slope_ref, ct_ref, ctx_ref, vec_ref, bi_ref, *rest
):
    out_ref, dctx_ref, delta_ref, sum_ref, vecg_ref, big_ref, keep_ref, acc_ref, low_ref, first_ref, first_sem, late_ref, late_sem = rest[-13:]


    @pl.when(pl.program_id(0) == 0)
    def _():
        vecg_ref[...] = jnp.zeros_like(vecg_ref)
        big_ref[...] = jnp.zeros_like(big_ref)
        late = fetch(rest[counts[0] : sum(counts)], late_ref, late_sem)
        wait_all(late + fetch(rest[: counts[0]], first_ref, first_sem))

    _, gain_one, bias_one, _, gain_two, bias_two = vectors_of(vec_ref)
    weight = partial(piece_weight, first_ref, late_ref, slot_ref)
    strips = [slice(start, start + STRIP) for start in range(0, TILE, STRIP)]

    def add(total, term):
        term = jnp.sum(term.reshape(STRIP // 8, 8, D), 0)
        return term if total is None else total + term

    for rows in strips:
        low_ref[rows] = low(normal_ref[rows] * gain_one + bias_one)
    normed_low = low_ref[...]
    branch = branch_ref[...]
    for piece in range(PIECES, FF // HIDDEN):
        flat = slice(piece * HIDDEN, (piece + 1) * HIDDEN)
        inner = mul(normed_low, weight(piece, 0)) + bi_ref[0:1, flat]
        act, slope = gelu_and_slope(inner)
        keep_ref[:, (piece - PIECES) * HIDDEN : (piece - PIECES + 1) * HIDDEN] = low(slope)
        branch = branch + mul(low(act), weight(piece, 1), NT)
    acc_ref[...] = branch
    sums = [None] * 4
    for rows in strips:
        final, normal_two, inverse_two = norm_forward(acc_ref[rows], gain_two, bias_two)
        out_ref[rows] = low(final)
        final_grad = wide(ct_ref[rows])
        sum_two = norm_backward(final_grad, normal_two, inverse_two, gain_two)
        acc_ref[rows] = sum_two
        low_ref[rows] = low(sum_two)
        sums[2] = add(sums[2], wide(low(sum_two)))
        sums[3] = add(sums[3], final_grad)
    branch_grad = low_ref[...]
    normed_grad = acc_ref[...]
    for piece in range(FF // HIDDEN):
        flat = slice(piece * HIDDEN, (piece + 1) * HIDDEN)
        if piece < PIECES:
            slope = slope_ref[:, flat]
        else:
            slope = keep_ref[:, (piece - PIECES) * HIDDEN : (piece - PIECES + 1) * HIDDEN]
        inner_grad = low(mul(branch_grad, weight(piece, 1)) * wide(slope))
        big_ref[0:1, flat] += jnp.sum(wide(inner_grad), 0, keepdims=True)
        normed_grad = normed_grad + mul(inner_grad, weight(piece, 0), NT)
    acc_ref[...] = normed_grad
    for rows in strips:
        normed_grad = acc_ref[rows]
        sum_one = low(norm_backward(normed_grad, normal_ref[rows], inv_ref[rows, 0:1], gain_one))
        sum_ref[rows] = sum_one
        sums[0] = add(sums[0], wide(sum_one))
        sums[1] = add(sums[1], normed_grad)
    sum_one = sum_ref[...]
    for group in range(GROUPS):
        part = slice(group * WIDE, (group + 1) * WIDE)
        context_grad = low(mul(sum_one, out_columns(first_ref, slot_ref, group))).T
        dctx_ref[0, part] = context_grad
        product = wide(context_grad) * wide(ctx_ref[0, part])
        for head in range(GROUP):
            own = slice(head * HEAD_DIM, (head + 1) * HEAD_DIM)
            delta_ref[0, group, head : head + 1, :] = jnp.sum(product[own], 0, keepdims=True)
    for i, term in enumerate(sums):
        vecg_ref[i : i + 1, :] += jnp.sum(term, 0, keepdims=True)


def params(grid_rank):
    return pltpu.CompilerParams(
        dimension_semantics=("arbitrary",) * grid_rank, vmem_limit_bytes=VMEM_BYTES
    )


def cost(flops, moved):
    return pl.CostEstimate(flops=int(flops), bytes_accessed=int(moved), transcendentals=0)


SCALARS = pl.BlockSpec(memory_space=pltpu.SMEM)
ANYWHERE = pl.BlockSpec(memory_space=pl.ANY)


def whole(array):
    return pl.BlockSpec(array.shape, lambda *_: (0,) * array.ndim, pipeline_mode=pl.Buffered(1))


def slot_scratch(pieces):
    half = len(pieces) // 2
    n = sum(w.shape[0] for w in pieces[:half])
    return [
        pltpu.VMEM((2, n) + pieces[0].shape[1:], pieces[0].dtype),
        pltpu.SemaphoreType.DMA((len(pieces),)),
    ]


def attend(step, earlier, tokens, seg_col, seg_row, fills, slots, pieces, bias):
    rows = tokens.shape[0] // SLOTS
    return pl.pallas_call(
        partial(attend_kernel, step, len(pieces)),
        grid=(rows,),
        in_specs=[
            SCALARS,
            SCALARS,
            pl.BlockSpec((SLOTS, D), lambda r: (r, 0)),
            pl.BlockSpec((1, SLOTS, 1), lambda r: (r, 0, 0)),
            pl.BlockSpec((1, 1, SLOTS), lambda r: (r, 0, 0)),
            whole(bias),
        ]
        + [ANYWHERE] * (len(pieces) + len(earlier)),
        out_specs=[
            pl.BlockSpec((2, 1, WIDE, SLOTS), lambda r: (0, r, step, 0)),
            pl.BlockSpec((2, SLOTS, WIDE), lambda r: (0, r, step)),
            pl.BlockSpec((1, WIDE, SLOTS), lambda r: (r, step, 0)),
            pl.BlockSpec((1, 1, GROUP, SLOTS), lambda r: (r, step, 0, 0)),
        ],
        out_shape=[
            jax.ShapeDtypeStruct((2, rows, D, SLOTS), jnp.bfloat16),
            jax.ShapeDtypeStruct((2, rows * SLOTS, D), jnp.bfloat16),
            jax.ShapeDtypeStruct((rows, D, SLOTS), jnp.bfloat16),
            jax.ShapeDtypeStruct((rows, GROUPS, GROUP, SLOTS), jnp.float32),
        ],
        scratch_shapes=[
            pltpu.VMEM((sum(w.shape[0] for w in pieces),) + pieces[0].shape[1:3] + (WIDE,), jnp.bfloat16),
            pltpu.SemaphoreType.DMA((len(pieces),)),
        ],
        input_output_aliases={6 + len(pieces) + i: i for i in range(len(earlier))},
        compiler_params=params(1),
        cost_estimate=cost(15e9, 10e6),
        name="attend",
    )(fills, slots, tokens, seg_col, seg_row, bias, *pieces, *earlier)


def attend_back(qk, kv, context_grad, delta, lse, seg_col, seg_row, fills, slots, weights, sum_one):
    rows = kv.shape[1] // SLOTS
    return pl.pallas_call(
        partial(attend_back_kernel, len(weights)),
        grid=(rows, GROUPS),
        in_specs=[
            SCALARS,
            SCALARS,
            pl.BlockSpec((2, 1, WIDE, SLOTS), lambda r, g: (0, r, g, 0)),
            pl.BlockSpec((2, SLOTS, WIDE), lambda r, g: (0, r, g)),
            pl.BlockSpec((1, WIDE, SLOTS), lambda r, g: (r, g, 0)),
            pl.BlockSpec((1, 1, GROUP, SLOTS), lambda r, g: (r, g, 0, 0)),
            pl.BlockSpec((1, 1, GROUP, SLOTS), lambda r, g: (r, g, 0, 0)),
            pl.BlockSpec((1, SLOTS, 1), lambda r, g: (r, 0, 0)),
            pl.BlockSpec((1, 1, SLOTS), lambda r, g: (r, 0, 0)),
        ]
        + [ANYWHERE] * len(weights)
        + [pl.BlockSpec((SLOTS, D), lambda r, g: (r, 0))],
        out_specs=[
            pl.BlockSpec((SLOTS, D), lambda r, g: (r, 0)),
            pl.BlockSpec((8, D), lambda r, g: (0, 0)),
        ],
        out_shape=[
            jax.ShapeDtypeStruct((rows * SLOTS, D), jnp.bfloat16),
            jax.ShapeDtypeStruct((8, D), jnp.float32),
        ],
        scratch_shapes=[
            pltpu.VMEM((SLOTS, SLOTS), jnp.float32),
            pltpu.VMEM((SLOTS, D), jnp.float32),
        ]
        + slot_scratch(weights),
        compiler_params=params(2),
        cost_estimate=cost(50e9, 30e6),
        name="attend_back",
    )(fills, slots, qk, kv, context_grad, delta, lse, seg_col, seg_row, *weights, sum_one)


def tiles(width):
    return pl.BlockSpec((TILE, width), lambda i: (i, 0))


PER_ROW = SLOTS // TILE
ROWS_T = pl.BlockSpec((1, D, TILE), lambda i: (i // PER_ROW, 0, i % PER_ROW))


def feed_front(slots, tokens, context, first, vectors, in_bias):
    count = tokens.shape[0]
    return pl.pallas_call(
        partial(front_kernel, len(first)),
        grid=(count // TILE,),
        in_specs=[SCALARS, tiles(D), ROWS_T, whole(vectors), whole(in_bias)] + [ANYWHERE] * len(first),
        out_specs=[tiles(D), tiles(128), tiles(D), tiles(2 * FLAT)],
        out_shape=[
            jax.ShapeDtypeStruct((count, D), jnp.float32),
            jax.ShapeDtypeStruct((count, 128), jnp.float32),
            jax.ShapeDtypeStruct((count, D), jnp.float32),
            jax.ShapeDtypeStruct((count, 2 * FLAT), jnp.bfloat16),
        ],
        scratch_shapes=[pltpu.VMEM((TILE, D), jnp.bfloat16)] + slot_scratch(first),
        compiler_params=params(1),
        cost_estimate=cost(25e9, 30e6),
        name="feed_front",
    )(slots, tokens, context, vectors, in_bias, *first)


def feed_back(slots, front, cotangent, context, first, late, vectors, in_bias):
    count = cotangent.shape[0]
    return pl.pallas_call(
        partial(back_kernel, (len(first), len(late))),
        grid=(count // TILE,),
        in_specs=[SCALARS, tiles(D), tiles(128), tiles(D), tiles(2 * FLAT), tiles(D), ROWS_T, whole(vectors), whole(in_bias)]
        + [ANYWHERE] * (len(first) + len(late)),
        out_specs=[
            tiles(D),
            ROWS_T,
            pl.BlockSpec((1, GROUPS, GROUP, TILE), lambda i: (i // PER_ROW, 0, 0, i % PER_ROW)),
            tiles(D),
            pl.BlockSpec((8, D), lambda i: (0, 0)),
            pl.BlockSpec((8, FF), lambda i: (0, 0)),
        ],
        out_shape=[
            jax.ShapeDtypeStruct((count, D), jnp.bfloat16),
            jax.ShapeDtypeStruct((count // SLOTS, D, SLOTS), jnp.bfloat16),
            jax.ShapeDtypeStruct((count // SLOTS, GROUPS, GROUP, SLOTS), jnp.float32),
            jax.ShapeDtypeStruct((count, D), jnp.bfloat16),
            jax.ShapeDtypeStruct((8, D), jnp.float32),
            jax.ShapeDtypeStruct((8, FF), jnp.float32),
        ],
        scratch_shapes=[
            pltpu.VMEM((TILE, FF - 2 * FLAT), jnp.bfloat16),
            pltpu.VMEM((TILE, D), jnp.float32),
            pltpu.VMEM((TILE, D), jnp.bfloat16),
        ]
        + slot_scratch(first)
        + slot_scratch(late),
        compiler_params=params(1),
        cost_estimate=cost(75e9, 40e6),
        name="feed_back",
    )(slots, *front, cotangent, context, vectors, in_bias, *first, *late)


def stage_bits(n):
    bits = n.bit_length() - 1
    in_z = -(-bits // 3)
    in_y = -(-(bits - in_z) // 2)
    in_x = bits - in_z - in_y
    x = list(range(in_x))
    y = list(range(in_x, in_x + in_y))
    z = list(range(in_x + in_y, bits))
    return z + y + x, z[::-1] + x + y


def partner(block, n, stage):
    bits = [order[stage] for order in stage_bits(n)]
    pairs = [(2 * i + core, 2 * (i ^ (1 << bits[core])) + core) for i in range(n) for core in range(2)]
    return lax.ppermute(block, ("rows", "tp"), pairs)


def joined(*blocks):
    return jnp.concatenate(blocks, 0)


def swap_cores(block):
    return lax.ppermute(block, "tp", [(0, 1), (1, 0)])


def after(value, *earlier):
    return lax.optimization_barrier((value, earlier))[0]


def together(*values):
    return lax.optimization_barrier(values)


def slot_table(n):
    apart = jnp.arange(n, dtype=jnp.int32) ^ lax.axis_index("rows")
    tables = []
    for order in stage_bits(n):
        tables.append(sum(((apart >> bit) & 1) << place for place, bit in enumerate(order)))
    core = lax.axis_index("tp")
    return jnp.where(core == 0, jnp.stack(tables), jnp.stack(tables[::-1]))


def sum_over_all(values, n):
    values = values + swap_cores(values)
    step = 1
    while step < n:
        values = values + lax.ppermute(values, "rows", [(i, i ^ step) for i in range(n)])
        step *= 2
    return values


def shards(
    tokens,
    segment_ids,
    fill_counts,
    qkv_weight,
    qv_bias,
    out_weight,
    out_bias,
    norm1_gain,
    norm1_bias,
    in_weight,
    in_bias,
    down_weight,
    down_bias,
    norm2_gain,
    norm2_bias,
    cotangent,
):
    n = lax.axis_size("rows")
    core = lax.axis_index("tp")
    rows_here = tokens.shape[0] // SLOTS
    down_t = down_weight.T
    width = qv_bias.shape[1]

    last = n.bit_length() - 2

    def spread(blocks, stages):
        for stage in stages:
            blocks = blocks + [partner(block, n, stage) for block in blocks]
        return blocks

    middle = range(2, last)
    q = qkv_weight[None]
    q = joined(q, partner(q, n, 0))
    q = joined(q, partner(q, n, 1))
    first = jnp.concatenate([in_weight[:, :FLAT], down_t[:, :FLAT], out_weight.T], 1)[None]
    q, first = together(q, first)
    q_own = spread([q], middle)
    first = joined(first, partner(first, n, 0))
    segments = lax.dynamic_slice_in_dim(segment_ids, core * rows_here, rows_here, 0)
    fills = lax.dynamic_slice_in_dim(fill_counts, core * rows_here, rows_here, 0)
    seg_col = segments[:, :, None]
    seg_row = segments[:, None, :]
    slots = slot_table(n)
    own = jnp.concatenate([qv_bias.reshape(-1), in_bias])
    other = swap_cores(own)
    by_distance = [wide(b) for b in (own, other)]
    b_qv = [b[: 2 * width].reshape(2, width) for b in by_distance]
    b_in = [b[2 * width :] for b in by_distance]
    b_hidden = jnp.concatenate([b_in[0][:FLAT], b_in[1][:FLAT], b_in[0][FLAT:], b_in[1][FLAT:]]).reshape(1, -1)
    vectors = wide(
        jnp.concatenate([out_bias, norm1_gain, norm1_bias, down_bias, norm2_gain, norm2_bias, out_bias, out_bias])
    ).reshape(8, D)
    small = (seg_col, seg_row, fills, slots, b_qv, b_hidden, vectors)
    q_own, first, small = together(q_own, first, small)
    seg_col, seg_row, fills, slots, b_qv, b_hidden, vectors = small
    q_own = spread(q_own, [last])
    first_got = partner(first, n, 1)

    def run(step, earlier):
        bias = b_qv[step // 2][:, step % 2 * WIDE : (step % 2 + 1) * WIDE]
        pieces = q_others if step >= 2 else q_own
        return attend(step, earlier, tokens, seg_col, seg_row, fills, slots, pieces, bias)

    late = jnp.concatenate([in_weight[:, FLAT:], down_t[:, FLAT:]], 1)[None]
    q_own, first_got, late = together(q_own, first_got, late)
    first = joined(first, first_got)
    q_others = [swap_cores(w) for w in q_own]
    first_own = spread([first], middle)
    late_got = partner(late, n, 0)
    results = run(0, ())
    results, first_own, late_got, q_others = together(results, first_own, late_got, q_others)
    late = joined(late, late_got)
    first_own = spread(first_own, [last])
    late_got = partner(late, n, 1)
    results = run(1, results)
    results = run(2, results)
    results, first_own, late_got = together(results, first_own, late_got)
    late = joined(late, late_got)
    first_others = [swap_cores(w) for w in first_own]
    late_own = spread([late], middle)
    results = run(3, results)
    results, late_own = together(results, late_own)
    late_own = spread(late_own, [last])

    qk, kv, context, lse = results
    first = first_own + first_others
    front = feed_front(slots, tokens, context, first, vectors, b_hidden)
    front, late_own = together(front, late_own)
    late = late_own + [swap_cores(w) for w in late_own]
    layer_out, context_grad, delta, sum_one, vec_grads, in_grads = feed_back(
        slots, front, cotangent, context, first, late, vectors, b_hidden
    )
    hidden = in_grads[0].reshape(2, 2, FF // 4)
    hidden = jnp.where(core == 0, hidden, hidden[:, ::-1]).transpose(1, 0, 2)
    early = jnp.concatenate([vec_grads[:4].reshape(-1), hidden.reshape(-1)])
    early = jnp.sum(lax.all_gather(early, ("rows", "tp"), axis=0), 0)
    vec = early[: 4 * D].reshape(4, D)

    tokens_grad, qv_grads = attend_back(
        qk, kv, context_grad, delta, lse, seg_col, seg_row, fills, slots, q_own + q_others, sum_one
    )
    qv = qv_grads[:2].reshape(2, 2, D // 2)
    qv = jnp.where(core == 0, qv, qv[:, ::-1]).reshape(2, D)
    qv = sum_over_all(qv, n)
    return (layer_out, tokens_grad, qv, vec[0], vec[1], early[4 * D :], vec[2], vec[3])


def solution(mesh):
    return jax.shard_map(
        shards,
        mesh=mesh,
        in_specs=(
            P(("rows", "tp"), None),
            P("rows", None),
            P("rows"),
            P(None, "rows", "tp"),
            P(None, "tp"),
            P("tp", "rows"),
            P(),
            P(),
            P(),
            P("rows", "tp"),
            P("tp"),
            P("tp", "rows"),
            P(),
            P(),
            P(),
            P(("rows", "tp"), None),
        ),
        out_specs=(P(("rows", "tp"), None), P(("rows", "tp"), None), P(), P(), P(), P(), P(), P()),
        check_vma=False,
    )
```

```python
from functools import partial
import math

import jax
import jax.numpy as jnp
from jax import lax
from jax.experimental import pallas as pl
from jax.experimental.pallas import tpu as pltpu
from jax.sharding import PartitionSpec as P

D = 1024
FF = 4096
HEADS = 16
HEAD_DIM = 64
SLOTS = 512
GROUP = 4
WIDE = GROUP * HEAD_DIM
PAIR = 2 * HEAD_DIM
GROUPS = HEADS // GROUP
TILE = 256
STRIP = 32
EPSILON = 1e-05
MASKED = -1e30
SCALE = 1.0 / math.sqrt(HEAD_DIM)
VMEM_BYTES = 60 * 2**20

NN = (((1,), (0,)), ((), ()))
NT = (((1,), (1,)), ((), ()))
TT = (((0,), (1,)), ((), ()))


def mul(left, right, dims=NN):
    return lax.dot_general(left, right, dims, preferred_element_type=jnp.float32)


def low(values):
    return values.astype(jnp.bfloat16)


def wide(values):
    return values.astype(jnp.float32)


def norm_forward(summed, gain_vec, shift_vec):
    row_mean = jnp.mean(summed, -1, keepdims=True)
    centered = summed - row_mean
    inverse = lax.rsqrt(jnp.mean(centered * centered, -1, keepdims=True) + EPSILON)
    normal = centered * inverse
    return (normal * gain_vec + shift_vec, normal, inverse)


def norm_backward(grad_in, normal, inverse, gain_vec):
    scaled = grad_in * gain_vec
    return inverse * (
        scaled
        - jnp.mean(scaled, -1, keepdims=True)
        - normal * jnp.mean(scaled * normal, -1, keepdims=True)
    )


def mask_bias(seg_col, seg_row, filled):
    keys = lax.broadcasted_iota(jnp.int32, (SLOTS, SLOTS), 0)
    places = lax.broadcasted_iota(jnp.int32, (SLOTS, SLOTS), 1)
    allowed = (seg_col == seg_row) & ((keys < filled) | (keys == places))
    return jnp.where(allowed, 0.0, MASKED)


def half_rows(rows, head):
    zeros = jnp.zeros((HEAD_DIM, rows.shape[1]), rows.dtype)
    return jnp.concatenate([rows, zeros] if head % 2 == 0 else [zeros, rows], 0)


def fetch(refs, scratch, sem, start=True):
    copies = []
    for i, ref in enumerate(refs):
        size = ref.shape[0]
        copies.append(pltpu.make_async_copy(ref, scratch.at[pl.ds(i * size, size)], sem.at[i]))
        if start:
            copies[-1].start()
    return copies


def fetch_sets(refs, scratch, sem, start=True):
    sets = scratch.shape[0]
    size = len(refs) // sets
    copies = []
    for i in range(sets):
        copies += fetch(refs[i * size : (i + 1) * size], scratch.at[i], sem.at[i], start)
    return copies


def first_or_later(step, body):
    @pl.when(step == 0)
    def _():
        body(True)

    @pl.when(step != 0)
    def _():
        body(False)


def wait_all(copies):
    for copy in copies:
        copy.wait()


def set_weight(w_ref, slot_ref, other, part):
    return jnp.concatenate([w_ref[slot_ref[other, c], part] for c in range(w_ref.shape[0])], 0)


def columns_of(w_ref, slot_ref, other, columns):
    there = w_ref.at[other]
    return jnp.concatenate([there[slot_ref[other, c], :, columns] for c in range(there.shape[0])], 0)


def attend_kernel(step, count, fill_ref, slot_ref, x_ref, segc_ref, segr_ref, b_ref, *rest):
    other, half = step % 2, step // 2
    qk_ref, kv_ref, ctx_ref, lse_ref, w_ref, sem = rest[-6:]

    @pl.when(pl.program_id(0) == 0)
    def _():
        wait_all(fetch(rest[:count], w_ref, sem))

    x = x_ref[...]
    weight = [set_weight(w_ref, slot_ref, other, i) for i in range(3)]
    columns = slice(half * WIDE, (half + 1) * WIDE)
    b_q, b_v = wide(b_ref[0:1, columns]), wide(b_ref[1:2, columns])
    bias = mask_bias(segc_ref[0], segr_ref[0], fill_ref[pl.program_id(0)])
    q = low(mul(x, weight[0]) + b_q)
    k = low(mul(x, weight[1]))
    v = low(mul(x, weight[2]) + b_v)
    q_t = (q * jnp.bfloat16(SCALE)).T
    v_t = v.T
    qk_ref[0, 0] = q_t
    qk_ref[1, 0] = k.T
    kv_ref[0] = k
    kv_ref[1] = v
    ones = jnp.ones((HEAD_DIM, SLOTS), jnp.bfloat16)

    def score(head):
        own = slice(head * HEAD_DIM, (head + 1) * HEAD_DIM)
        pair = slice(head // 2 * PAIR, (head // 2 + 1) * PAIR)
        return mul(k[:, pair], half_rows(q_t[own], head)) + bias

    def finish(head, top, probs):
        own = slice(head * HEAD_DIM, (head + 1) * HEAD_DIM)
        out = mul(jnp.concatenate([v_t[own], ones], 0), probs)
        total = out[HEAD_DIM : HEAD_DIM + 1]
        ctx_ref[0, own] = low(out[:HEAD_DIM] / total)
        lse_ref[0, 0, head : head + 1, :] = top + jnp.log(total)

    scores = score(0)
    done = None
    for head in range(GROUP):
        following = score(head + 1) if head + 1 < GROUP else None
        if done is not None:
            finish(head - 1, *done)
        top = jnp.max(scores, 0, keepdims=True)
        done = top, low(jnp.exp(scores - top))
        scores = following
    finish(GROUP - 1, *done)


def attend_back_kernel(count, fill_ref, slot_ref, qk_ref, kv_ref, dctx_ref, delta_ref, lse_ref, segc_ref, segr_ref, *rest):
    sum_ref, out_ref, qvb_ref, bias_ref, acc_ref, w_ref, sem = rest[-7:]
    row = pl.program_id(0)
    group = pl.program_id(1)

    @pl.when(group == 0)
    def _():
        bias_ref[...] = mask_bias(segc_ref[0], segr_ref[0], fill_ref[row])
        acc_ref[...] = wide(sum_ref[...])

    def body(arriving):
        if arriving:
            qvb_ref[...] = jnp.zeros_like(qvb_ref)
            fetch_sets(rest[:count], w_ref, sem)
        d_q, d_k, d_v = [], [], []
        for head in range(GROUP):
            own = slice(head * HEAD_DIM, (head + 1) * HEAD_DIM)
            pair = slice(head // 2 * PAIR, (head // 2 + 1) * PAIR)
            q_t, k_t, d_out_t = qk_ref[0, 0, own], qk_ref[1, 0, own], dctx_ref[0, own]
            scores = mul(kv_ref[0, :, pair], half_rows(q_t, head)) + bias_ref[...]
            probs = jnp.exp(scores - lse_ref[0, 0, head : head + 1, :])
            probs_grad = mul(kv_ref[1, :, pair], half_rows(d_out_t, head))
            scores_grad = low(probs * (probs_grad - delta_ref[0, 0, head : head + 1, :]))
            probs_low = low(probs)
            d_v.append(low(mul(d_out_t, probs_low, NT)))
            d_k.append(low(mul(q_t, scores_grad, NT)))
            d_q.append(low(mul(k_t, scores_grad) * SCALE))
        if arriving:
            wait_all(fetch_sets(rest[:count], w_ref, sem, start=False))
        ones = jnp.ones((16, SLOTS), jnp.bfloat16)
        columns = pl.ds(pl.multiple_of(group * WIDE, WIDE), WIDE)
        total = acc_ref[...]
        for i, grad in enumerate((d_q, d_k, d_v)):
            grad = jnp.concatenate(grad, 0)
            weight = set_weight(w_ref.at[group], slot_ref, group % 2, i)
            total = total + mul(grad, weight, TT)
            if i != 1:
                qvb_ref[i // 2 : i // 2 + 1, columns] += mul(ones, grad, NT)[0:1]
        acc_ref[...] = total

    first_or_later(row * GROUPS + group, body)

    @pl.when(group == GROUPS - 1)
    def _():
        out_ref[...] = low(acc_ref[...])


def gelu_and_slope(v):
    phi = 0.5 * (1.0 + lax.erf(v * math.sqrt(0.5)))
    bell = jnp.exp(-0.5 * v * v) * (1.0 / math.sqrt(2.0 * math.pi))
    return v * phi, phi + v * bell


FIRST = 1024
LATE = FF // 2 - FIRST
LATE_PIECE = 1024
PIECES = [(False, other, 0, FIRST) for other in range(2)]
PIECES += [(True, other, start, LATE_PIECE) for other in range(2) for start in range(0, LATE, LATE_PIECE)]


def flat_of(piece):
    late, other, start, size = piece
    begin = 2 * FIRST + other * LATE + start if late else other * FIRST
    return slice(begin, begin + size)


def first_columns(first_ref, slot_ref, other, columns):
    n, _, chunk, _ = first_ref.shape
    return first_ref[:, slot_ref[2, 0] ^ other, :, columns].reshape(n * chunk, columns.size)


def piece_weight(first_ref, late_ref, slot_ref, piece, down):
    late, other, start, size = piece
    if late:
        return columns_of(late_ref, slot_ref, other, pl.ds(down * LATE + start, size))
    return first_columns(first_ref, slot_ref, other, pl.ds(down * FIRST + start, size))


def piece_bias(b_refs, piece):
    late, other, start, size = piece
    begin = FIRST * late + start
    return wide(b_refs[other][begin : begin + size]).reshape(1, size)


def out_columns(first_ref, slot_ref, group):
    return first_columns(first_ref, slot_ref, group % 2, pl.ds(2 * FIRST + group // 2 * WIDE, WIDE))


def row_of(ref):
    return wide(ref[...]).reshape(1, D)


def front_kernel(
    slot_ref, x_ref, ctx_ref, vec_refs, bi_refs, first_ref, normal_ref, inv_ref, branch_ref, slope_ref, low_ref
):
    out_bias, gain_one, bias_one, down_bias = [row_of(ref) for ref in vec_refs]
    attention = out_bias
    for group in range(GROUPS):
        part = slice(group * WIDE, (group + 1) * WIDE)
        attention = attention + mul(ctx_ref[0, part], out_columns(first_ref, slot_ref, group), TT)
    branch_ref[...] = attention
    for start in range(0, TILE, STRIP):
        rows = slice(start, start + STRIP)
        normed, normal_one, inverse_one = norm_forward(wide(x_ref[rows]) + branch_ref[rows], gain_one, bias_one)
        normal_ref[rows] = normal_one
        inv_ref[rows] = jnp.broadcast_to(inverse_one, (STRIP, 128))
        low_ref[rows] = low(normed)
        branch_ref[rows] = normed + down_bias
    normed_low = low_ref[...]
    branch = branch_ref[...]

    for piece in PIECES[:2]:
        inner = mul(normed_low, piece_weight(first_ref, None, slot_ref, piece, 0)) + piece_bias(bi_refs, piece)
        act, slope = gelu_and_slope(inner)
        slope_ref[:, flat_of(piece)] = low(slope)
        branch = branch + mul(low(act), piece_weight(first_ref, None, slot_ref, piece, 1), NT)
    branch_ref[...] = branch


def back_kernel(
    count, slot_ref, normal_ref, inv_ref, branch_ref, slope_ref, ct_ref, ctx_ref, vec_refs, bi_refs, first_ref, *rest
):
    out_ref, dctx_ref, delta_ref, sum_ref, vecg_ref, big_ref, keep_ref, acc_ref, low_ref, late_ref, late_sem = rest[-11:]


    @pl.when(pl.program_id(0) == 0)
    def _():
        vecg_ref[...] = jnp.zeros_like(vecg_ref)
        big_ref[...] = jnp.zeros_like(big_ref)
        wait_all(fetch_sets(rest[:count], late_ref, late_sem))

    gain_one, bias_one, gain_two, bias_two = [row_of(ref) for ref in vec_refs]
    weight = partial(piece_weight, first_ref, late_ref, slot_ref)
    strips = [slice(start, start + STRIP) for start in range(0, TILE, STRIP)]

    def add(total, term):
        term = jnp.sum(term.reshape(STRIP // 8, 8, D), 0)
        return term if total is None else total + term

    for rows in strips:
        low_ref[rows] = low(normal_ref[rows] * gain_one + bias_one)
    normed_low = low_ref[...]
    branch = branch_ref[...]
    for piece in PIECES[2:]:
        inner = mul(normed_low, weight(piece, 0)) + piece_bias(bi_refs, piece)
        act, slope = gelu_and_slope(inner)
        flat = flat_of(piece)
        keep_ref[:, flat.start - 2 * FIRST : flat.stop - 2 * FIRST] = low(slope)
        branch = branch + mul(low(act), weight(piece, 1), NT)
    acc_ref[...] = branch
    sums = [None] * 4
    for rows in strips:
        final, normal_two, inverse_two = norm_forward(acc_ref[rows], gain_two, bias_two)
        out_ref[rows] = low(final)
        final_grad = wide(ct_ref[rows])
        sum_two = norm_backward(final_grad, normal_two, inverse_two, gain_two)
        acc_ref[rows] = sum_two
        low_ref[rows] = low(sum_two)
        sums[2] = add(sums[2], wide(low(sum_two)))
        sums[3] = add(sums[3], final_grad)
    branch_grad = low_ref[...]
    normed_grad = acc_ref[...]
    for piece in PIECES:
        flat = flat_of(piece)
        slope = keep_ref[:, flat.start - 2 * FIRST : flat.stop - 2 * FIRST] if piece[0] else slope_ref[:, flat]
        inner_grad = low(mul(branch_grad, weight(piece, 1)) * wide(slope))
        big_ref[0:1, flat] += jnp.sum(wide(inner_grad), 0, keepdims=True)
        normed_grad = normed_grad + mul(inner_grad, weight(piece, 0), NT)
    acc_ref[...] = normed_grad
    for rows in strips:
        normed_grad = acc_ref[rows]
        sum_one = low(norm_backward(normed_grad, normal_ref[rows], inv_ref[rows, 0:1], gain_one))
        sum_ref[rows] = sum_one
        sums[0] = add(sums[0], wide(sum_one))
        sums[1] = add(sums[1], normed_grad)
    sum_one = sum_ref[...]
    for group in range(GROUPS):
        part = slice(group * WIDE, (group + 1) * WIDE)
        context_grad = low(mul(sum_one, out_columns(first_ref, slot_ref, group))).T
        dctx_ref[0, part] = context_grad
        product = wide(context_grad) * wide(ctx_ref[0, part])
        for head in range(GROUP):
            own = slice(head * HEAD_DIM, (head + 1) * HEAD_DIM)
            delta_ref[0, group, head : head + 1, :] = jnp.sum(product[own], 0, keepdims=True)
    for i, term in enumerate(sums):
        vecg_ref[i : i + 1, :] += jnp.sum(term, 0, keepdims=True)


def params(grid_rank):
    return pltpu.CompilerParams(
        dimension_semantics=("arbitrary",) * grid_rank, vmem_limit_bytes=VMEM_BYTES
    )


def cost(flops, moved):
    return pl.CostEstimate(flops=int(flops), bytes_accessed=int(moved), transcendentals=0)


SCALARS = pl.BlockSpec(memory_space=pltpu.SMEM)
ANYWHERE = pl.BlockSpec(memory_space=pl.ANY)


def wholes(arrays):
    return tuple(whole(array) for array in arrays)


def whole(array):
    return pl.BlockSpec(array.shape, lambda *_: (0,) * array.ndim, pipeline_mode=pl.Buffered(1))


def slot_scratch(pieces, sets):
    count = len(pieces) // sets
    n = sum(w.shape[0] for w in pieces[:count])
    return [
        pltpu.VMEM((sets, n) + pieces[0].shape[1:], pieces[0].dtype),
        pltpu.SemaphoreType.DMA((sets, count)),
    ]


def attend(step, earlier, tokens, seg_col, seg_row, fills, slots, pieces, bias):
    rows = tokens.shape[0] // SLOTS
    return pl.pallas_call(
        partial(attend_kernel, step, len(pieces)),
        grid=(rows,),
        in_specs=[
            SCALARS,
            SCALARS,
            pl.BlockSpec((SLOTS, D), lambda r: (r, 0)),
            pl.BlockSpec((1, SLOTS, 1), lambda r: (r, 0, 0)),
            pl.BlockSpec((1, 1, SLOTS), lambda r: (r, 0, 0)),
            whole(bias),
        ]
        + [ANYWHERE] * (len(pieces) + len(earlier)),
        out_specs=[
            pl.BlockSpec((2, 1, WIDE, SLOTS), lambda r: (0, r, step, 0)),
            pl.BlockSpec((2, SLOTS, WIDE), lambda r: (0, r, step)),
            pl.BlockSpec((1, WIDE, SLOTS), lambda r: (r, step, 0)),
            pl.BlockSpec((1, 1, GROUP, SLOTS), lambda r: (r, step, 0, 0)),
        ],
        out_shape=[
            jax.ShapeDtypeStruct((2, rows, D, SLOTS), jnp.bfloat16),
            jax.ShapeDtypeStruct((2, rows * SLOTS, D), jnp.bfloat16),
            jax.ShapeDtypeStruct((rows, D, SLOTS), jnp.bfloat16),
            jax.ShapeDtypeStruct((rows, GROUPS, GROUP, SLOTS), jnp.float32),
        ],
        scratch_shapes=[
            pltpu.VMEM((sum(w.shape[0] for w in pieces),) + pieces[0].shape[1:], jnp.bfloat16),
            pltpu.SemaphoreType.DMA((len(pieces),)),
        ],
        input_output_aliases={6 + len(pieces) + i: i for i in range(len(earlier))},
        compiler_params=params(1),
        cost_estimate=cost(15e9, 10e6),
        name="attend",
    )(fills, slots, tokens, seg_col, seg_row, bias, *pieces, *earlier)


def attend_back(qk, kv, context_grad, delta, lse, seg_col, seg_row, fills, slots, weights, sum_one):
    rows = kv.shape[1] // SLOTS
    return pl.pallas_call(
        partial(attend_back_kernel, len(weights)),
        grid=(rows, GROUPS),
        in_specs=[
            SCALARS,
            SCALARS,
            pl.BlockSpec((2, 1, WIDE, SLOTS), lambda r, g: (0, r, g, 0)),
            pl.BlockSpec((2, SLOTS, WIDE), lambda r, g: (0, r, g)),
            pl.BlockSpec((1, WIDE, SLOTS), lambda r, g: (r, g, 0)),
            pl.BlockSpec((1, 1, GROUP, SLOTS), lambda r, g: (r, g, 0, 0)),
            pl.BlockSpec((1, 1, GROUP, SLOTS), lambda r, g: (r, g, 0, 0)),
            pl.BlockSpec((1, SLOTS, 1), lambda r, g: (r, 0, 0)),
            pl.BlockSpec((1, 1, SLOTS), lambda r, g: (r, 0, 0)),
        ]
        + [ANYWHERE] * len(weights)
        + [pl.BlockSpec((SLOTS, D), lambda r, g: (r, 0))],
        out_specs=[
            pl.BlockSpec((SLOTS, D), lambda r, g: (r, 0)),
            pl.BlockSpec((8, D), lambda r, g: (0, 0)),
        ],
        out_shape=[
            jax.ShapeDtypeStruct((rows * SLOTS, D), jnp.bfloat16),
            jax.ShapeDtypeStruct((8, D), jnp.float32),
        ],
        scratch_shapes=[
            pltpu.VMEM((SLOTS, SLOTS), jnp.float32),
            pltpu.VMEM((SLOTS, D), jnp.float32),
        ]
        + slot_scratch(weights, GROUPS),
        compiler_params=params(2),
        cost_estimate=cost(50e9, 30e6),
        name="attend_back",
    )(fills, slots, qk, kv, context_grad, delta, lse, seg_col, seg_row, *weights, sum_one)


def tiles(width):
    return pl.BlockSpec((TILE, width), lambda i: (i, 0))


PER_ROW = SLOTS // TILE
ROWS_T = pl.BlockSpec((1, D, TILE), lambda i: (i // PER_ROW, 0, i % PER_ROW))


def feed_front(slots, tokens, context, first, vectors, in_bias):
    count = tokens.shape[0]
    return pl.pallas_call(
        front_kernel,
        grid=(count // TILE,),
        in_specs=[SCALARS, tiles(D), ROWS_T, wholes(vectors), wholes(in_bias), whole(first)],
        out_specs=[tiles(D), tiles(128), tiles(D), tiles(2 * FIRST)],
        out_shape=[
            jax.ShapeDtypeStruct((count, D), jnp.float32),
            jax.ShapeDtypeStruct((count, 128), jnp.float32),
            jax.ShapeDtypeStruct((count, D), jnp.float32),
            jax.ShapeDtypeStruct((count, 2 * FIRST), jnp.bfloat16),
        ],
        scratch_shapes=[pltpu.VMEM((TILE, D), jnp.bfloat16)],
        compiler_params=params(1),
        cost_estimate=cost(25e9, 30e6),
        name="feed_front",
    )(slots, tokens, context, vectors, in_bias, first)


def feed_back(slots, front, cotangent, context, first, late, vectors, in_bias):
    count = cotangent.shape[0]
    return pl.pallas_call(
        partial(back_kernel, len(late)),
        grid=(count // TILE,),
        in_specs=[SCALARS, tiles(D), tiles(128), tiles(D), tiles(2 * FIRST), tiles(D), ROWS_T, wholes(vectors), wholes(in_bias), whole(first)]
        + [ANYWHERE] * len(late),
        out_specs=[
            tiles(D),
            ROWS_T,
            pl.BlockSpec((1, GROUPS, GROUP, TILE), lambda i: (i // PER_ROW, 0, 0, i % PER_ROW)),
            tiles(D),
            pl.BlockSpec((8, D), lambda i: (0, 0)),
            pl.BlockSpec((8, FF), lambda i: (0, 0)),
        ],
        out_shape=[
            jax.ShapeDtypeStruct((count, D), jnp.bfloat16),
            jax.ShapeDtypeStruct((count // SLOTS, D, SLOTS), jnp.bfloat16),
            jax.ShapeDtypeStruct((count // SLOTS, GROUPS, GROUP, SLOTS), jnp.float32),
            jax.ShapeDtypeStruct((count, D), jnp.bfloat16),
            jax.ShapeDtypeStruct((8, D), jnp.float32),
            jax.ShapeDtypeStruct((8, FF), jnp.float32),
        ],
        scratch_shapes=[
            pltpu.VMEM((TILE, 2 * LATE), jnp.bfloat16),
            pltpu.VMEM((TILE, D), jnp.float32),
            pltpu.VMEM((TILE, D), jnp.bfloat16),
        ]
        + slot_scratch(late, 2),
        compiler_params=params(1),
        cost_estimate=cost(75e9, 40e6),
        name="feed_back",
    )(slots, *front, cotangent, context, vectors, in_bias, first, *late)


def stage_bits(n):
    bits = n.bit_length() - 1
    in_z = -(-bits // 3)
    in_y = -(-(bits - in_z) // 2)
    in_x = bits - in_z - in_y
    x = list(range(in_x))
    y = list(range(in_x, in_x + in_y))
    z = list(range(in_x + in_y, bits))
    return z + y + x, z[::-1] + x + y


def partner(block, n, stage):
    bits = [order[stage] for order in stage_bits(n)]
    pairs = [(2 * i + core, 2 * (i ^ (1 << bits[core])) + core) for i in range(n) for core in range(2)]
    return lax.ppermute(block, ("rows", "tp"), pairs)


def joined(*blocks):
    return jnp.concatenate(blocks, 0)


def swap_cores(block):
    return lax.ppermute(block, "tp", [(0, 1), (1, 0)])


def after(value, *earlier):
    return lax.optimization_barrier((value, earlier))[0]


def together(*values):
    return lax.optimization_barrier(values)


def slot_table(n):
    apart = jnp.arange(n, dtype=jnp.int32) ^ lax.axis_index("rows")
    tables = []
    for order in stage_bits(n):
        tables.append(sum(((apart >> bit) & 1) << place for place, bit in enumerate(order)))
    core = lax.axis_index("tp")
    ordered = jnp.where(core == 0, jnp.stack(tables), jnp.stack(tables[::-1]))
    return jnp.concatenate([ordered, jnp.full((1, n), core, jnp.int32)], 0)


def sum_over_all(values, n):
    values = values + swap_cores(values)
    step = 1
    while step < n:
        values = values + lax.ppermute(values, "rows", [(i, i ^ step) for i in range(n)])
        step *= 2
    return values


def shards(
    tokens,
    segment_ids,
    fill_counts,
    qkv_weight,
    qv_bias,
    out_weight,
    out_bias,
    norm1_gain,
    norm1_bias,
    in_weight,
    in_bias,
    down_weight,
    down_bias,
    norm2_gain,
    norm2_bias,
    cotangent,
):
    n = lax.axis_size("rows")
    core = lax.axis_index("tp")
    rows_here = tokens.shape[0] // SLOTS
    down_t = down_weight.T

    last = n.bit_length() - 2

    def spread(block, stages):
        for stage in stages:
            block = joined(block, partner(block, n, stage))
        return block

    a = qkv_weight[None, :, :, :WIDE]
    a = joined(a, partner(a, n, 0))
    a, b = together(a, qkv_weight[None, :, :, WIDE:])
    a_got = partner(a, n, 1)
    b_got = partner(b, n, 0)
    first = jnp.concatenate([in_weight[:, :FIRST], down_t[:, :FIRST], out_weight.T], 1)

    a, a_got, b, b_got, first = together(a, a_got, b, b_got, first)
    first = lax.all_gather(first, ("rows", "tp"), axis=0, tiled=False).reshape((n, 2) + first.shape)
    a = joined(a, a_got)
    b = joined(b, b_got)
    for stage in range(2, last):
        a_got = partner(a, n, stage)
        a = a if stage == last - 1 else joined(a, a_got)
    b_got = partner(b, n, 1)
    segments = lax.dynamic_slice_in_dim(segment_ids, core * rows_here, rows_here, 0)
    fills = lax.dynamic_slice_in_dim(fill_counts, core * rows_here, rows_here, 0)
    slots = slot_table(n)
    small = (segments[:, :, None], segments[:, None, :], fills, slots)
    b_qv = (qv_bias, swap_cores(qv_bias))
    b_in = (in_bias, swap_cores(in_bias))
    late = jnp.concatenate([in_weight[:, FIRST:], down_t[:, FIRST:]], 1)[None]

    a, a_got, b, b_got, late, small, b_qv, b_in = together(a, a_got, b, b_got, late, small, b_qv, b_in)
    a = joined(a, a_got)
    a_other = swap_cores(a)
    a_got = partner(a, n, last)
    b = joined(b, b_got)

    def run(step, earlier, *pieces):
        return attend(step, earlier, tokens, *small, pieces, b_qv[step % 2])

    a, a_got, a_other, b, late = together(a, a_got, a_other, b, late)
    a_other_got = swap_cores(a_got)
    for stage in range(2, last):
        b_got = partner(b, n, stage)
        b = b if stage == last - 1 else joined(b, b_got)
    late_got = partner(late, n, 0)
    results = run(0, (), a, a_got)

    results, a_other_got, b, b_got, late, late_got = together(results, a_other_got, b, b_got, late, late_got)
    b = joined(b, b_got)
    late = joined(late, late_got)
    late_got = partner(late, n, 1)
    b_other = swap_cores(b)
    b_got = partner(b, n, last)
    results = run(1, results, a_other, a_other_got)

    results, b_other, b_got, late, late_got = together(results, b_other, b_got, late, late_got)
    b_other_got = swap_cores(b_got)
    late = joined(late, late_got)
    for stage in range(2, last):
        late_got = partner(late, n, stage)
        late = late if stage == last - 1 else joined(late, late_got)
    results = run(2, results, b, b_got)

    results, b_other_got = together(results, b_other_got)
    results = run(3, results, b_other, b_other_got)

    results, late, late_got = together(results, late, late_got)
    late_own = [late, late_got]
    late_others = [swap_cores(w) for w in late_own]
    late_far = [partner(w, n, last) for w in late_own]

    qk, kv, context, lse = results
    front = feed_front(slots, tokens, context, first, (out_bias, norm1_gain, norm1_bias, down_bias), b_in)

    front, late_others, late_far = together(front, late_others, late_far)
    late_others += [swap_cores(w) for w in late_far]
    vectors = (norm1_gain, norm1_bias, norm2_gain, norm2_bias)
    layer_out, context_grad, delta, sum_one, vec_grads, in_grads = feed_back(
        slots, front, cotangent, context, first, late_own + late_far + late_others, vectors, b_in
    )
    hidden = [in_grads[0, : 2 * FIRST].reshape(2, FIRST), in_grads[0, 2 * FIRST :].reshape(2, LATE)]
    hidden = jnp.concatenate(hidden, 1)
    hidden = jnp.where(core == 0, hidden, hidden[::-1])
    early = jnp.concatenate([vec_grads[:4].reshape(-1), hidden.reshape(-1)])
    early = jnp.sum(lax.all_gather(early, ("rows", "tp"), axis=0), 0)
    vec = early[: 4 * D].reshape(4, D)

    a_set = [a, a_got, a_other, a_other_got]
    b_set = [b, b_got, b_other, b_other_got]
    tokens_grad, qv_grads = attend_back(
        qk, kv, context_grad, delta, lse, *small, a_set + b_set, sum_one
    )
    qv = qv_grads[:2].reshape(2, 2, 2, WIDE)
    qv = jnp.where(core == 0, qv, qv[:, :, ::-1]).transpose(0, 2, 1, 3).reshape(2, D)
    qv = sum_over_all(qv, n)
    return (layer_out, tokens_grad, qv, vec[0], vec[1], early[4 * D :], vec[2], vec[3])


def solution(mesh):
    return jax.shard_map(
        shards,
        mesh=mesh,
        in_specs=(
            P(("rows", "tp"), None),
            P("rows", None),
            P("rows"),
            P(None, "rows", "tp"),
            P(None, "tp"),
            P("tp", "rows"),
            P(),
            P(),
            P(),
            P("rows", "tp"),
            P("tp"),
            P("tp", "rows"),
            P(),
            P(),
            P(),
            P(("rows", "tp"), None),
        ),
        out_specs=(P(("rows", "tp"), None), P(("rows", "tp"), None), P(), P(), P(), P(), P(), P()),
        check_vma=False,
    )
```

```python
from functools import partial
import math

import jax
import jax.numpy as jnp
from jax import lax
from jax.experimental import pallas as pl
from jax.experimental.pallas import tpu as pltpu
from jax.sharding import PartitionSpec as P

D = 1024
FF = 4096
HEADS = 16
HEAD_DIM = 64
SLOTS = 512
GROUP = 4
WIDE = GROUP * HEAD_DIM
PAIR = 2 * HEAD_DIM
GROUPS = HEADS // GROUP
TILE = 256
STRIP = 32
EPSILON = 1e-05
MASKED = -1e30
SCALE = 1.0 / math.sqrt(HEAD_DIM)
VMEM_BYTES = 60 * 2**20

NN = (((1,), (0,)), ((), ()))
NT = (((1,), (1,)), ((), ()))
TT = (((0,), (1,)), ((), ()))


def mul(left, right, dims=NN):
    return lax.dot_general(left, right, dims, preferred_element_type=jnp.float32)


def low(values):
    return values.astype(jnp.bfloat16)


def wide(values):
    return values.astype(jnp.float32)


def norm_forward(summed, gain_vec, shift_vec):
    row_mean = jnp.mean(summed, -1, keepdims=True)
    centered = summed - row_mean
    inverse = lax.rsqrt(jnp.mean(centered * centered, -1, keepdims=True) + EPSILON)
    normal = centered * inverse
    return (normal * gain_vec + shift_vec, normal, inverse)


def norm_backward(grad_in, normal, inverse, gain_vec):
    scaled = grad_in * gain_vec
    return inverse * (
        scaled
        - jnp.mean(scaled, -1, keepdims=True)
        - normal * jnp.mean(scaled * normal, -1, keepdims=True)
    )


def mask_bias(seg_col, seg_row, filled):
    keys = lax.broadcasted_iota(jnp.int32, (SLOTS, SLOTS), 0)
    places = lax.broadcasted_iota(jnp.int32, (SLOTS, SLOTS), 1)
    allowed = (seg_col == seg_row) & ((keys < filled) | (keys == places))
    return jnp.where(allowed, 0.0, MASKED)


def half_rows(rows, head):
    zeros = jnp.zeros((HEAD_DIM, rows.shape[1]), rows.dtype)
    return jnp.concatenate([rows, zeros] if head % 2 == 0 else [zeros, rows], 0)


def fetch(refs, scratch, sem, start=True):
    copies = []
    for i, ref in enumerate(refs):
        size = ref.shape[0]
        copies.append(pltpu.make_async_copy(ref, scratch.at[pl.ds(i * size, size)], sem.at[i]))
        if start:
            copies[-1].start()
    return copies


def fetch_sets(refs, scratch, sem, start=True):
    sets = scratch.shape[0]
    size = len(refs) // sets
    copies = []
    for i in range(sets):
        copies += fetch(refs[i * size : (i + 1) * size], scratch.at[i], sem.at[i], start)
    return copies


def first_or_later(step, body):
    @pl.when(step == 0)
    def _():
        body(True)

    @pl.when(step != 0)
    def _():
        body(False)


def wait_all(copies):
    for copy in copies:
        copy.wait()


def set_weight(w_ref, slot_ref, other, part):
    return jnp.concatenate([w_ref[slot_ref[other, c], part] for c in range(w_ref.shape[0])], 0)


def columns_of(w_ref, slot_ref, other, columns):
    there = w_ref.at[other]
    return jnp.concatenate([there[slot_ref[other, c], :, columns] for c in range(there.shape[0])], 0)


def attend_kernel(step, count, fill_ref, slot_ref, x_ref, segc_ref, segr_ref, b_ref, *rest):
    other, half = step % 2, step // 2
    qk_ref, kv_ref, ctx_ref, lse_ref, w_ref, sem = rest[-6:]

    @pl.when(pl.program_id(0) == 0)
    def _():
        wait_all(fetch(rest[:count], w_ref, sem))

    x = x_ref[...]
    weight = [set_weight(w_ref, slot_ref, other, i) for i in range(3)]
    columns = slice(half * WIDE, (half + 1) * WIDE)
    b_q, b_v = wide(b_ref[0:1, columns]), wide(b_ref[1:2, columns])
    bias = mask_bias(segc_ref[0], segr_ref[0], fill_ref[pl.program_id(0)])
    q = low(mul(x, weight[0]) + b_q)
    k = low(mul(x, weight[1]))
    v = low(mul(x, weight[2]) + b_v)
    q_t = (q * jnp.bfloat16(SCALE)).T
    v_t = v.T
    qk_ref[0, 0] = q_t
    qk_ref[1, 0] = k.T
    kv_ref[0] = k
    kv_ref[1] = v
    ones = jnp.ones((HEAD_DIM, SLOTS), jnp.bfloat16)

    def score(head):
        own = slice(head * HEAD_DIM, (head + 1) * HEAD_DIM)
        pair = slice(head // 2 * PAIR, (head // 2 + 1) * PAIR)
        return mul(k[:, pair], half_rows(q_t[own], head)) + bias

    def finish(head, top, probs):
        own = slice(head * HEAD_DIM, (head + 1) * HEAD_DIM)
        out = mul(jnp.concatenate([v_t[own], ones], 0), probs)
        total = out[HEAD_DIM : HEAD_DIM + 1]
        ctx_ref[0, own] = low(out[:HEAD_DIM] / total)
        lse_ref[0, 0, head : head + 1, :] = top + jnp.log(total)

    scores = score(0)
    done = None
    for head in range(GROUP):
        following = score(head + 1) if head + 1 < GROUP else None
        if done is not None:
            finish(head - 1, *done)
        top = jnp.max(scores, 0, keepdims=True)
        done = top, low(jnp.exp(scores - top))
        scores = following
    finish(GROUP - 1, *done)


def attend_back_kernel(count, fill_ref, slot_ref, qk_ref, kv_ref, dctx_ref, delta_ref, lse_ref, segc_ref, segr_ref, *rest):
    sum_ref, out_ref, qvb_ref, bias_ref, acc_ref, w_ref, sem = rest[-7:]
    row = pl.program_id(0)
    group = pl.program_id(1)

    @pl.when(group == 0)
    def _():
        bias_ref[...] = mask_bias(segc_ref[0], segr_ref[0], fill_ref[row])
        acc_ref[...] = wide(sum_ref[...])

    def body(arriving):
        if arriving:
            qvb_ref[...] = jnp.zeros_like(qvb_ref)
            fetch_sets(rest[:count], w_ref, sem)
        d_q, d_k, d_v = [], [], []
        for head in range(GROUP):
            own = slice(head * HEAD_DIM, (head + 1) * HEAD_DIM)
            pair = slice(head // 2 * PAIR, (head // 2 + 1) * PAIR)
            q_t, k_t, d_out_t = qk_ref[0, 0, own], qk_ref[1, 0, own], dctx_ref[0, own]
            scores = mul(kv_ref[0, :, pair], half_rows(q_t, head)) + bias_ref[...]
            probs = jnp.exp(scores - lse_ref[0, 0, head : head + 1, :])
            probs_grad = mul(kv_ref[1, :, pair], half_rows(d_out_t, head))
            scores_grad = low(probs * (probs_grad - delta_ref[0, 0, head : head + 1, :]))
            probs_low = low(probs)
            d_v.append(low(mul(d_out_t, probs_low, NT)))
            d_k.append(low(mul(q_t, scores_grad, NT)))
            d_q.append(low(mul(k_t, scores_grad) * SCALE))
        if arriving:
            wait_all(fetch_sets(rest[:count], w_ref, sem, start=False))
        ones = jnp.ones((16, SLOTS), jnp.bfloat16)
        place = (slot_ref[2, 0] ^ (group % 2)) * 2 + group // 2
        columns = pl.ds(pl.multiple_of(place * WIDE, WIDE), WIDE)
        total = acc_ref[...]
        for i, grad in enumerate((d_q, d_k, d_v)):
            grad = jnp.concatenate(grad, 0)
            weight = set_weight(w_ref.at[group], slot_ref, group % 2, i)
            total = total + mul(grad, weight, TT)
            if i != 1:
                qvb_ref[i // 2 : i // 2 + 1, columns] += mul(ones, grad, NT)[0:1]
        acc_ref[...] = total

    first_or_later(row * GROUPS + group, body)

    @pl.when(group == GROUPS - 1)
    def _():
        out_ref[...] = low(acc_ref[...])


def gelu_and_slope(v):
    phi = 0.5 * (1.0 + lax.erf(v * math.sqrt(0.5)))
    bell = jnp.exp(-0.5 * v * v) * (1.0 / math.sqrt(2.0 * math.pi))
    return v * phi, phi + v * bell


FIRST = 1024
LATE = FF // 2 - FIRST
LATE_PIECE = 1024
PIECES = [(False, other, 0, FIRST) for other in range(2)]
PIECES += [(True, other, start, LATE_PIECE) for other in range(2) for start in range(0, LATE, LATE_PIECE)]


def flat_of(piece):
    late, other, start, size = piece
    begin = 2 * FIRST + other * LATE + start if late else other * FIRST
    return slice(begin, begin + size)


def first_columns(first_ref, slot_ref, other, columns):
    n, _, chunk, _ = first_ref.shape
    return first_ref[:, slot_ref[2, 0] ^ other, :, columns].reshape(n * chunk, columns.size)


def piece_weight(first_ref, late_ref, slot_ref, piece, down):
    late, other, start, size = piece
    if late:
        return columns_of(late_ref, slot_ref, other, pl.ds(down * LATE + start, size))
    return first_columns(first_ref, slot_ref, other, pl.ds(down * FIRST + start, size))


assert FIRST == LATE == LATE_PIECE == D


def piece_bias(b_refs, piece):
    late, other, start, size = piece
    begin = FIRST * late + start
    return wide(b_refs[other][begin : begin + size]).reshape(1, size)


def out_columns(first_ref, slot_ref, group):
    return first_columns(first_ref, slot_ref, group % 2, pl.ds(2 * FIRST + group // 2 * WIDE, WIDE))


def row_of(ref):
    return wide(ref[...]).reshape(1, D)


def front_kernel(
    slot_ref, x_ref, ctx_ref, vec_refs, bi_refs, first_ref, normal_ref, inv_ref, branch_ref, slope_ref, low_ref
):
    out_bias, gain_one, bias_one, down_bias = [row_of(ref) for ref in vec_refs]
    attention = out_bias
    for group in range(GROUPS):
        part = slice(group * WIDE, (group + 1) * WIDE)
        attention = attention + mul(ctx_ref[0, part], out_columns(first_ref, slot_ref, group), TT)
    branch_ref[...] = attention
    for start in range(0, TILE, STRIP):
        rows = slice(start, start + STRIP)
        normed, normal_one, inverse_one = norm_forward(wide(x_ref[rows]) + branch_ref[rows], gain_one, bias_one)
        normal_ref[rows] = normal_one
        inv_ref[rows] = jnp.broadcast_to(inverse_one, (STRIP, 128))
        low_ref[rows] = low(normed)
        branch_ref[rows] = normed + down_bias
    normed_low = low_ref[...]
    branch = branch_ref[...]

    for piece in PIECES[:2]:
        inner = mul(normed_low, piece_weight(first_ref, None, slot_ref, piece, 0)) + piece_bias(bi_refs, piece)
        act, slope = gelu_and_slope(inner)
        slope_ref[:, flat_of(piece)] = low(slope)
        branch = branch + mul(low(act), piece_weight(first_ref, None, slot_ref, piece, 1), NT)
    branch_ref[...] = branch


def back_kernel(
    count, slot_ref, normal_ref, inv_ref, branch_ref, slope_ref, ct_ref, ctx_ref, vec_refs, bi_refs, first_ref, *rest
):
    out_ref, dctx_ref, delta_ref, sum_ref, sums_ref, keep_ref, acc_ref, low_ref, late_ref, late_sem = rest[-10:]


    @pl.when(pl.program_id(0) == 0)
    def _():
        sums_ref[...] = jnp.zeros_like(sums_ref)
        wait_all(fetch_sets(rest[:count], late_ref, late_sem))

    gain_one, bias_one, gain_two, bias_two = [row_of(ref) for ref in vec_refs]
    weight = partial(piece_weight, first_ref, late_ref, slot_ref)
    strips = [slice(start, start + STRIP) for start in range(0, TILE, STRIP)]

    def add(total, term):
        term = jnp.sum(term.reshape(STRIP // 8, 8, D), 0)
        return term if total is None else total + term

    for rows in strips:
        low_ref[rows] = low(normal_ref[rows] * gain_one + bias_one)
    normed_low = low_ref[...]
    branch = branch_ref[...]
    for piece in PIECES[2:]:
        inner = mul(normed_low, weight(piece, 0)) + piece_bias(bi_refs, piece)
        act, slope = gelu_and_slope(inner)
        flat = flat_of(piece)
        keep_ref[:, flat.start - 2 * FIRST : flat.stop - 2 * FIRST] = low(slope)
        branch = branch + mul(low(act), weight(piece, 1), NT)
    acc_ref[...] = branch
    sums = [None] * 4
    for rows in strips:
        final, normal_two, inverse_two = norm_forward(acc_ref[rows], gain_two, bias_two)
        out_ref[rows] = low(final)
        final_grad = wide(ct_ref[rows])
        sum_two = norm_backward(final_grad, normal_two, inverse_two, gain_two)
        acc_ref[rows] = sum_two
        low_ref[rows] = low(sum_two)
        sums[2] = add(sums[2], wide(low(sum_two)))
        sums[3] = add(sums[3], final_grad)
    branch_grad = low_ref[...]
    normed_grad = acc_ref[...]
    for piece in PIECES:
        flat = flat_of(piece)
        slope = keep_ref[:, flat.start - 2 * FIRST : flat.stop - 2 * FIRST] if piece[0] else slope_ref[:, flat]
        inner_grad = low(mul(branch_grad, weight(piece, 1)) * wide(slope))
        late, other = piece[:2]
        place = pl.ds(4 + 2 * (slot_ref[2, 0] ^ other) + int(late), 1)
        sums_ref[place, :] += jnp.sum(wide(inner_grad), 0, keepdims=True)
        normed_grad = normed_grad + mul(inner_grad, weight(piece, 0), NT)
    acc_ref[...] = normed_grad
    for rows in strips:
        normed_grad = acc_ref[rows]
        sum_one = low(norm_backward(normed_grad, normal_ref[rows], inv_ref[rows, 0:1], gain_one))
        sum_ref[rows] = sum_one
        sums[0] = add(sums[0], wide(sum_one))
        sums[1] = add(sums[1], normed_grad)
    sum_one = sum_ref[...]
    for group in range(GROUPS):
        part = slice(group * WIDE, (group + 1) * WIDE)
        context_grad = low(mul(sum_one, out_columns(first_ref, slot_ref, group))).T
        dctx_ref[0, part] = context_grad
        product = wide(context_grad) * wide(ctx_ref[0, part])
        for head in range(GROUP):
            own = slice(head * HEAD_DIM, (head + 1) * HEAD_DIM)
            delta_ref[0, group, head : head + 1, :] = jnp.sum(product[own], 0, keepdims=True)
    for i, term in enumerate(sums):
        sums_ref[i : i + 1, :] += jnp.sum(term, 0, keepdims=True)


def params(grid_rank):
    return pltpu.CompilerParams(
        dimension_semantics=("arbitrary",) * grid_rank, vmem_limit_bytes=VMEM_BYTES
    )


def cost(flops, moved):
    return pl.CostEstimate(flops=int(flops), bytes_accessed=int(moved), transcendentals=0)


SCALARS = pl.BlockSpec(memory_space=pltpu.SMEM)
ANYWHERE = pl.BlockSpec(memory_space=pl.ANY)


def wholes(arrays):
    return tuple(whole(array) for array in arrays)


def whole(array):
    return pl.BlockSpec(array.shape, lambda *_: (0,) * array.ndim, pipeline_mode=pl.Buffered(1))


def slot_scratch(pieces, sets):
    count = len(pieces) // sets
    n = sum(w.shape[0] for w in pieces[:count])
    return [
        pltpu.VMEM((sets, n) + pieces[0].shape[1:], pieces[0].dtype),
        pltpu.SemaphoreType.DMA((sets, count)),
    ]


def attend(step, earlier, tokens, seg_col, seg_row, fills, slots, pieces, bias):
    rows = tokens.shape[0] // SLOTS
    return pl.pallas_call(
        partial(attend_kernel, step, len(pieces)),
        grid=(rows,),
        in_specs=[
            SCALARS,
            SCALARS,
            pl.BlockSpec((SLOTS, D), lambda r: (r, 0)),
            pl.BlockSpec((1, SLOTS, 1), lambda r: (r, 0, 0)),
            pl.BlockSpec((1, 1, SLOTS), lambda r: (r, 0, 0)),
            whole(bias),
        ]
        + [ANYWHERE] * (len(pieces) + len(earlier)),
        out_specs=[
            pl.BlockSpec((2, 1, WIDE, SLOTS), lambda r: (0, r, step, 0)),
            pl.BlockSpec((2, SLOTS, WIDE), lambda r: (0, r, step)),
            pl.BlockSpec((1, WIDE, SLOTS), lambda r: (r, step, 0)),
            pl.BlockSpec((1, 1, GROUP, SLOTS), lambda r: (r, step, 0, 0)),
        ],
        out_shape=[
            jax.ShapeDtypeStruct((2, rows, D, SLOTS), jnp.bfloat16),
            jax.ShapeDtypeStruct((2, rows * SLOTS, D), jnp.bfloat16),
            jax.ShapeDtypeStruct((rows, D, SLOTS), jnp.bfloat16),
            jax.ShapeDtypeStruct((rows, GROUPS, GROUP, SLOTS), jnp.float32),
        ],
        scratch_shapes=[
            pltpu.VMEM((sum(w.shape[0] for w in pieces),) + pieces[0].shape[1:], jnp.bfloat16),
            pltpu.SemaphoreType.DMA((len(pieces),)),
        ],
        input_output_aliases={6 + len(pieces) + i: i for i in range(len(earlier))},
        compiler_params=params(1),
        cost_estimate=cost(15e9, 10e6),
        name="attend",
    )(fills, slots, tokens, seg_col, seg_row, bias, *pieces, *earlier)


def attend_back(qk, kv, context_grad, delta, lse, seg_col, seg_row, fills, slots, weights, sum_one):
    rows = kv.shape[1] // SLOTS
    return pl.pallas_call(
        partial(attend_back_kernel, len(weights)),
        grid=(rows, GROUPS),
        in_specs=[
            SCALARS,
            SCALARS,
            pl.BlockSpec((2, 1, WIDE, SLOTS), lambda r, g: (0, r, g, 0)),
            pl.BlockSpec((2, SLOTS, WIDE), lambda r, g: (0, r, g)),
            pl.BlockSpec((1, WIDE, SLOTS), lambda r, g: (r, g, 0)),
            pl.BlockSpec((1, 1, GROUP, SLOTS), lambda r, g: (r, g, 0, 0)),
            pl.BlockSpec((1, 1, GROUP, SLOTS), lambda r, g: (r, g, 0, 0)),
            pl.BlockSpec((1, SLOTS, 1), lambda r, g: (r, 0, 0)),
            pl.BlockSpec((1, 1, SLOTS), lambda r, g: (r, 0, 0)),
        ]
        + [ANYWHERE] * len(weights)
        + [pl.BlockSpec((SLOTS, D), lambda r, g: (r, 0))],
        out_specs=[
            pl.BlockSpec((SLOTS, D), lambda r, g: (r, 0)),
            pl.BlockSpec((2, D), lambda r, g: (0, 0)),
        ],
        out_shape=[
            jax.ShapeDtypeStruct((rows * SLOTS, D), jnp.bfloat16),
            jax.ShapeDtypeStruct((2, D), jnp.float32),
        ],
        scratch_shapes=[
            pltpu.VMEM((SLOTS, SLOTS), jnp.float32),
            pltpu.VMEM((SLOTS, D), jnp.float32),
        ]
        + slot_scratch(weights, GROUPS),
        compiler_params=params(2),
        cost_estimate=cost(50e9, 30e6),
        name="attend_back",
    )(fills, slots, qk, kv, context_grad, delta, lse, seg_col, seg_row, *weights, sum_one)


def tiles(width):
    return pl.BlockSpec((TILE, width), lambda i: (i, 0))


PER_ROW = SLOTS // TILE
ROWS_T = pl.BlockSpec((1, D, TILE), lambda i: (i // PER_ROW, 0, i % PER_ROW))


def feed_front(slots, tokens, context, first, vectors, in_bias):
    count = tokens.shape[0]
    return pl.pallas_call(
        front_kernel,
        grid=(count // TILE,),
        in_specs=[SCALARS, tiles(D), ROWS_T, wholes(vectors), wholes(in_bias), whole(first)],
        out_specs=[tiles(D), tiles(128), tiles(D), tiles(2 * FIRST)],
        out_shape=[
            jax.ShapeDtypeStruct((count, D), jnp.float32),
            jax.ShapeDtypeStruct((count, 128), jnp.float32),
            jax.ShapeDtypeStruct((count, D), jnp.float32),
            jax.ShapeDtypeStruct((count, 2 * FIRST), jnp.bfloat16),
        ],
        scratch_shapes=[pltpu.VMEM((TILE, D), jnp.bfloat16)],
        compiler_params=params(1),
        cost_estimate=cost(25e9, 30e6),
        name="feed_front",
    )(slots, tokens, context, vectors, in_bias, first)


def feed_back(slots, front, cotangent, context, first, late, vectors, in_bias):
    count = cotangent.shape[0]
    return pl.pallas_call(
        partial(back_kernel, len(late)),
        grid=(count // TILE,),
        in_specs=[SCALARS, tiles(D), tiles(128), tiles(D), tiles(2 * FIRST), tiles(D), ROWS_T, wholes(vectors), wholes(in_bias), whole(first)]
        + [ANYWHERE] * len(late),
        out_specs=[
            tiles(D),
            ROWS_T,
            pl.BlockSpec((1, GROUPS, GROUP, TILE), lambda i: (i // PER_ROW, 0, 0, i % PER_ROW)),
            tiles(D),
            pl.BlockSpec((8, D), lambda i: (0, 0)),
        ],
        out_shape=[
            jax.ShapeDtypeStruct((count, D), jnp.bfloat16),
            jax.ShapeDtypeStruct((count // SLOTS, D, SLOTS), jnp.bfloat16),
            jax.ShapeDtypeStruct((count // SLOTS, GROUPS, GROUP, SLOTS), jnp.float32),
            jax.ShapeDtypeStruct((count, D), jnp.bfloat16),
            jax.ShapeDtypeStruct((8, D), jnp.float32),
        ],
        scratch_shapes=[
            pltpu.VMEM((TILE, 2 * LATE), jnp.bfloat16),
            pltpu.VMEM((TILE, D), jnp.float32),
            pltpu.VMEM((TILE, D), jnp.bfloat16),
        ]
        + slot_scratch(late, 2),
        compiler_params=params(1),
        cost_estimate=cost(75e9, 40e6),
        name="feed_back",
    )(slots, *front, cotangent, context, vectors, in_bias, first, *late)


def stage_bits(n):
    bits = n.bit_length() - 1
    in_z = -(-bits // 3)
    in_y = -(-(bits - in_z) // 2)
    in_x = bits - in_z - in_y
    x = list(range(in_x))
    y = list(range(in_x, in_x + in_y))
    z = list(range(in_x + in_y, bits))
    return z + y + x, z[::-1] + x + y


def partner(block, n, stage):
    bits = [order[stage] for order in stage_bits(n)]
    pairs = [(2 * i + core, 2 * (i ^ (1 << bits[core])) + core) for i in range(n) for core in range(2)]
    return lax.ppermute(block, ("rows", "tp"), pairs)


def joined(*blocks):
    return jnp.concatenate(blocks, 0)


def swap_cores(block):
    return lax.ppermute(block, "tp", [(0, 1), (1, 0)])


def after(value, *earlier):
    return lax.optimization_barrier((value, earlier))[0]


def together(*values):
    return lax.optimization_barrier(values)


def slot_table(n):
    apart = jnp.arange(n, dtype=jnp.int32) ^ lax.axis_index("rows")
    tables = []
    for order in stage_bits(n):
        tables.append(sum(((apart >> bit) & 1) << place for place, bit in enumerate(order)))
    core = lax.axis_index("tp")
    ordered = jnp.where(core == 0, jnp.stack(tables), jnp.stack(tables[::-1]))
    return jnp.concatenate([ordered, jnp.full((1, n), core, jnp.int32)], 0)


def sum_over_rows(values, n, beside):
    bits = n.bit_length() - 1

    def got(distance):
        return lax.ppermute(values, "rows", [(i, i ^ distance) for i in range(n)])

    for bit in range(0, bits - 1, 2):
        near, far, both = [got(j << bit) for j in (1, 2, 3)]
        near, far, both, beside = together(near, far, both, beside)
        values = (values + near) + (far + both)
    return values + got(1 << (bits - 1)) if bits % 2 else values, beside


def shards(
    tokens,
    segment_ids,
    fill_counts,
    qkv_weight,
    qv_bias,
    out_weight,
    out_bias,
    norm1_gain,
    norm1_bias,
    in_weight,
    in_bias,
    down_weight,
    down_bias,
    norm2_gain,
    norm2_bias,
    cotangent,
):
    n = lax.axis_size("rows")
    core = lax.axis_index("tp")
    rows_here = tokens.shape[0] // SLOTS
    down_t = down_weight.T

    last = n.bit_length() - 2

    def spread(block, stages):
        for stage in stages:
            block = joined(block, partner(block, n, stage))
        return block

    a = qkv_weight[None, :, :, :WIDE]
    a = joined(a, partner(a, n, 0))
    a, b = together(a, qkv_weight[None, :, :, WIDE:])
    a_got = partner(a, n, 1)
    b_got = partner(b, n, 0)
    first = jnp.concatenate([in_weight[:, :FIRST], down_t[:, :FIRST], out_weight.T], 1)

    a, a_got, b, b_got, first = together(a, a_got, b, b_got, first)
    first = lax.all_gather(first, ("rows", "tp"), axis=0, tiled=False).reshape((n, 2) + first.shape)
    a = joined(a, a_got)
    b = joined(b, b_got)
    for stage in range(2, last):
        a_got = partner(a, n, stage)
        a = a if stage == last - 1 else joined(a, a_got)
    b_got = partner(b, n, 1)
    segments = lax.dynamic_slice_in_dim(segment_ids, core * rows_here, rows_here, 0)
    fills = lax.dynamic_slice_in_dim(fill_counts, core * rows_here, rows_here, 0)
    slots = slot_table(n)
    small = (segments[:, :, None], segments[:, None, :], fills, slots)
    b_qv = (qv_bias, swap_cores(qv_bias))
    b_in = (in_bias, swap_cores(in_bias))
    late = jnp.concatenate([in_weight[:, FIRST:], down_t[:, FIRST:]], 1)[None]

    a, a_got, b, b_got, late, small, b_qv, b_in = together(a, a_got, b, b_got, late, small, b_qv, b_in)
    a = joined(a, a_got)
    a_other = swap_cores(a)
    a_got = partner(a, n, last)
    b = joined(b, b_got)

    def run(step, earlier, *pieces):
        return attend(step, earlier, tokens, *small, pieces, b_qv[step % 2])

    a, a_got, a_other, b, late = together(a, a_got, a_other, b, late)
    a_other_got = swap_cores(a_got)
    for stage in range(2, last):
        b_got = partner(b, n, stage)
        b = b if stage == last - 1 else joined(b, b_got)
    late_got = partner(late, n, 0)
    results = run(0, (), a, a_got)

    results, a_other_got, b, b_got, late, late_got = together(results, a_other_got, b, b_got, late, late_got)
    b = joined(b, b_got)
    late = joined(late, late_got)
    late_got = partner(late, n, 1)
    b_other = swap_cores(b)
    b_got = partner(b, n, last)
    results = run(1, results, a_other, a_other_got)

    results, b_other, b_got = together(results, b_other, b_got)
    b_other_got = swap_cores(b_got)
    results = run(2, results, b, b_got)

    results, b_other_got, late, late_got = together(results, b_other_got, late, late_got)
    late = joined(late, late_got)
    for stage in range(2, last):
        late_got = partner(late, n, stage)
        late = late if stage == last - 1 else joined(late, late_got)
    results = run(3, results, b_other, b_other_got)

    results, late, late_got = together(results, late, late_got)
    late_own = [late, late_got]
    late_others = [swap_cores(w) for w in late_own]
    late_far = [partner(w, n, last) for w in late_own]

    qk, kv, context, lse = results
    front = feed_front(slots, tokens, context, first, (out_bias, norm1_gain, norm1_bias, down_bias), b_in)

    front, late_others, late_far = together(front, late_others, late_far)
    late_others += [swap_cores(w) for w in late_far]
    vectors = (norm1_gain, norm1_bias, norm2_gain, norm2_bias)
    layer_out, context_grad, delta, sum_one, grads = feed_back(
        slots, front, cotangent, context, first, late_own + late_far + late_others, vectors, b_in
    )
    sums = jnp.sum(lax.all_gather(grads, ("rows", "tp"), axis=0), 0)
    sums = [sums[0], sums[1], sums[4:].reshape(-1), sums[2], sums[3]]
    a_set = [a, a_got, a_other, a_other_got]
    b_set = [b, b_got, b_other, b_other_got]
    tokens_grad, qv_grads = attend_back(
        qk, kv, context_grad, delta, lse, *small, a_set + b_set, sum_one
    )
    qv, sums = sum_over_rows(qv_grads + swap_cores(qv_grads), n, sums)
    return (layer_out, tokens_grad, qv, *sums)


def solution(mesh):
    return jax.shard_map(
        shards,
        mesh=mesh,
        in_specs=(
            P(("rows", "tp"), None),
            P("rows", None),
            P("rows"),
            P(None, "rows", "tp"),
            P(None, "tp"),
            P("tp", "rows"),
            P(),
            P(),
            P(),
            P("rows", "tp"),
            P("tp"),
            P("tp", "rows"),
            P(),
            P(),
            P(),
            P(("rows", "tp"), None),
        ),
        out_specs=(P(("rows", "tp"), None), P(("rows", "tp"), None), P(), P(), P(), P(), P(), P()),
        check_vma=False,
    )
```

```python
from functools import partial
import math

import jax
import jax.numpy as jnp
from jax import lax
from jax.experimental import pallas as pl
from jax.experimental.pallas import tpu as pltpu
from jax.sharding import PartitionSpec as P

D = 1024
FF = 4096
HEADS = 16
HEAD_DIM = 64
SLOTS = 512
GROUP = 4
WIDE = GROUP * HEAD_DIM
PAIR = 2 * HEAD_DIM
GROUPS = HEADS // GROUP
FRONT_TILE = SLOTS
TILE = 256
STRIP = 32
EPSILON = 1e-05
MASKED = -1e30
SCALE = 1.0 / math.sqrt(HEAD_DIM)
VMEM_BYTES = 60 * 2**20

NN = (((1,), (0,)), ((), ()))
NT = (((1,), (1,)), ((), ()))
TT = (((0,), (1,)), ((), ()))


def mul(left, right, dims=NN):
    return lax.dot_general(left, right, dims, preferred_element_type=jnp.float32)


def low(values):
    return values.astype(jnp.bfloat16)


def wide(values):
    return values.astype(jnp.float32)


def norm_forward(summed, gain_vec, shift_vec):
    row_mean = jnp.mean(summed, -1, keepdims=True)
    centered = summed - row_mean
    inverse = lax.rsqrt(jnp.mean(centered * centered, -1, keepdims=True) + EPSILON)
    normal = centered * inverse
    return (normal * gain_vec + shift_vec, normal, inverse)


def norm_backward(grad_in, normal, inverse, gain_vec):
    scaled = grad_in * gain_vec
    return inverse * (
        scaled
        - jnp.mean(scaled, -1, keepdims=True)
        - normal * jnp.mean(scaled * normal, -1, keepdims=True)
    )


def mask_bias(seg_col, seg_row, filled):
    keys = lax.broadcasted_iota(jnp.int32, (SLOTS, SLOTS), 0)
    places = lax.broadcasted_iota(jnp.int32, (SLOTS, SLOTS), 1)
    allowed = (seg_col == seg_row) & ((keys < filled) | (keys == places))
    return jnp.where(allowed, 0.0, MASKED)


def half_rows(rows, head):
    zeros = jnp.zeros((HEAD_DIM, rows.shape[1]), rows.dtype)
    return jnp.concatenate([rows, zeros] if head % 2 == 0 else [zeros, rows], 0)


def fetch(refs, scratch, sem, start=True):
    copies = []
    for i, ref in enumerate(refs):
        size = ref.shape[0]
        copies.append(pltpu.make_async_copy(ref, scratch.at[pl.ds(i * size, size)], sem.at[i]))
        if start:
            copies[-1].start()
    return copies


def fetch_sets(refs, scratch, sem, start=True):
    sets = scratch.shape[0]
    size = len(refs) // sets
    copies = []
    for i in range(sets):
        copies += fetch(refs[i * size : (i + 1) * size], scratch.at[i], sem.at[i], start)
    return copies


def first_or_later(step, body):
    @pl.when(step == 0)
    def _():
        body(True)

    @pl.when(step != 0)
    def _():
        body(False)


def wait_all(copies):
    for copy in copies:
        copy.wait()


def set_weight(w_ref, slot_ref, other, part):
    return jnp.concatenate([w_ref[slot_ref[other, c], part] for c in range(w_ref.shape[0])], 0)


def columns_of(w_ref, slot_ref, other, columns):
    there = w_ref.at[other]
    return jnp.concatenate([there[slot_ref[other, c], :, columns] for c in range(there.shape[0])], 0)


def attend_kernel(step, count, fill_ref, slot_ref, x_ref, segc_ref, segr_ref, b_ref, *rest):
    other, half = step % 2, step // 2
    qk_ref, kv_ref, ctx_ref, lse_ref, w_ref, sem = rest[-6:]

    @pl.when(pl.program_id(0) == 0)
    def _():
        wait_all(fetch(rest[:count], w_ref, sem))

    x = x_ref[...]
    weight = [set_weight(w_ref, slot_ref, other, i) for i in range(3)]
    columns = slice(half * WIDE, (half + 1) * WIDE)
    b_q, b_v = wide(b_ref[0:1, columns]), wide(b_ref[1:2, columns])
    bias = mask_bias(segc_ref[0], segr_ref[0], fill_ref[pl.program_id(0)])
    q = low(mul(x, weight[0]) + b_q)
    k = low(mul(x, weight[1]))
    v = low(mul(x, weight[2]) + b_v)
    q_t = (q * jnp.bfloat16(SCALE)).T
    v_t = v.T
    qk_ref[0, 0] = q_t
    qk_ref[1, 0] = k.T
    kv_ref[0] = k
    kv_ref[1] = v
    ones = jnp.ones((HEAD_DIM, SLOTS), jnp.bfloat16)

    def score(head):
        own = slice(head * HEAD_DIM, (head + 1) * HEAD_DIM)
        pair = slice(head // 2 * PAIR, (head // 2 + 1) * PAIR)
        return mul(k[:, pair], half_rows(q_t[own], head)) + bias

    def finish(head, top, probs):
        own = slice(head * HEAD_DIM, (head + 1) * HEAD_DIM)
        out = mul(jnp.concatenate([v_t[own], ones], 0), probs)
        total = out[HEAD_DIM : HEAD_DIM + 1]
        ctx_ref[0, own] = low(out[:HEAD_DIM] / total)
        lse_ref[0, 0, head : head + 1, :] = top + jnp.log(total)

    scores = score(0)
    done = None
    for head in range(GROUP):
        following = score(head + 1) if head + 1 < GROUP else None
        if done is not None:
            finish(head - 1, *done)
        top = jnp.max(scores, 0, keepdims=True)
        done = top, low(jnp.exp(scores - top))
        scores = following
    finish(GROUP - 1, *done)


def attend_back_kernel(count, fill_ref, slot_ref, qk_ref, kv_ref, dctx_ref, delta_ref, lse_ref, segc_ref, segr_ref, *rest):
    sum_ref, out_ref, qvb_ref, bias_ref, acc_ref, w_ref, sem = rest[-7:]
    row = pl.program_id(0)
    group = pl.program_id(1)

    @pl.when(group == 0)
    def _():
        bias_ref[...] = mask_bias(segc_ref[0], segr_ref[0], fill_ref[row])
        acc_ref[...] = wide(sum_ref[...])

    def body(arriving):
        if arriving:
            qvb_ref[...] = jnp.zeros_like(qvb_ref)
            fetch_sets(rest[:count], w_ref, sem)
        d_q, d_k, d_v = [], [], []
        for head in range(GROUP):
            own = slice(head * HEAD_DIM, (head + 1) * HEAD_DIM)
            pair = slice(head // 2 * PAIR, (head // 2 + 1) * PAIR)
            q_t, k_t, d_out_t = qk_ref[0, 0, own], qk_ref[1, 0, own], dctx_ref[0, own]
            scores = mul(kv_ref[0, :, pair], half_rows(q_t, head)) + bias_ref[...]
            probs = jnp.exp(scores - lse_ref[0, 0, head : head + 1, :])
            probs_low = low(probs)
            probs_grad = mul(kv_ref[1, :, pair], half_rows(d_out_t, head))
            scores_grad = low(probs * (probs_grad - delta_ref[0, 0, head : head + 1, :]))
            d_v.append(low(mul(d_out_t, probs_low, NT)))
            d_q.append(low(mul(k_t, scores_grad) * SCALE))
            d_k.append(low(mul(q_t, scores_grad, NT)))
        if arriving:
            wait_all(fetch_sets(rest[:count], w_ref, sem, start=False))
        ones = jnp.ones((16, SLOTS), jnp.bfloat16)
        place = (slot_ref[2, 0] ^ (group % 2)) * 2 + group // 2
        columns = pl.ds(pl.multiple_of(place * WIDE, WIDE), WIDE)
        total = acc_ref[...]
        for i, grad in enumerate((d_q, d_k, d_v)):
            grad = jnp.concatenate(grad, 0)
            weight = set_weight(w_ref.at[group], slot_ref, group % 2, i)
            total = total + mul(grad, weight, TT)
            if i != 1:
                qvb_ref[i // 2 : i // 2 + 1, columns] += mul(ones, grad, NT)[0:1]
        acc_ref[...] = total

    first_or_later(row * GROUPS + group, body)

    @pl.when(group == GROUPS - 1)
    def _():
        out_ref[...] = low(acc_ref[...])


def gelu_and_slope(v):
    phi = 0.5 * (1.0 + lax.erf(v * math.sqrt(0.5)))
    bell = jnp.exp(-0.5 * v * v) * (1.0 / math.sqrt(2.0 * math.pi))
    return v * phi, phi + v * bell


FIRST = 1024
LATE = FF // 2 - FIRST
LATE_PIECE = 1024
PIECES = [(False, other, 0, FIRST) for other in range(2)]
PIECES += [(True, other, start, LATE_PIECE) for other in range(2) for start in range(0, LATE, LATE_PIECE)]


def flat_of(piece):
    late, other, start, size = piece
    begin = 2 * FIRST + other * LATE + start if late else other * FIRST
    return slice(begin, begin + size)


def first_columns(first_ref, slot_ref, other, columns):
    n, _, chunk, _ = first_ref.shape
    return first_ref[:, slot_ref[2, 0] ^ other, :, columns].reshape(n * chunk, columns.size)


def piece_weight(first_ref, late_ref, slot_ref, piece, down):
    late, other, start, size = piece
    if late:
        return columns_of(late_ref, slot_ref, other, pl.ds(down * LATE + start, size))
    return first_columns(first_ref, slot_ref, other, pl.ds(down * FIRST + start, size))


assert FIRST == LATE == LATE_PIECE == D


def piece_bias(b_refs, piece):
    late, other, start, size = piece
    begin = FIRST * late + start
    return wide(b_refs[other][begin : begin + size]).reshape(1, size)


def out_columns(first_ref, slot_ref, group):
    return first_columns(first_ref, slot_ref, group % 2, pl.ds(2 * FIRST + group // 2 * WIDE, WIDE))


def row_of(ref):
    return wide(ref[...]).reshape(1, D)


def front_kernel(
    slot_ref, x_ref, ctx_ref, vec_refs, bi_refs, first_ref, normal_ref, inv_ref, branch_ref, slope_ref, low_ref
):
    out_bias, gain_one, bias_one, down_bias = [row_of(ref) for ref in vec_refs]
    out_weight = jnp.concatenate([out_columns(first_ref, slot_ref, group) for group in range(GROUPS)], 1)
    attention = mul(ctx_ref[0], out_weight, TT) + out_bias
    branch_ref[...] = attention
    for start in range(0, FRONT_TILE, STRIP):
        rows = slice(start, start + STRIP)
        normed, normal_one, inverse_one = norm_forward(wide(x_ref[rows]) + branch_ref[rows], gain_one, bias_one)
        normal_ref[rows] = normal_one
        inv_ref[rows] = jnp.broadcast_to(inverse_one, (STRIP, 128))
        low_ref[rows] = low(normed)
        branch_ref[rows] = normed + down_bias
    normed_low = low_ref[...]
    branch = branch_ref[...]

    def inner_of(piece):
        return mul(normed_low, piece_weight(first_ref, None, slot_ref, piece, 0)) + piece_bias(bi_refs, piece)

    inner = inner_of(PIECES[0])
    for piece in PIECES[:2]:
        following = inner_of(PIECES[1]) if piece is PIECES[0] else None
        act, slope = gelu_and_slope(inner)
        slope_ref[:, flat_of(piece)] = low(slope)
        branch = branch + mul(low(act), piece_weight(first_ref, None, slot_ref, piece, 1), NT)
        inner = following
    branch_ref[...] = branch


def back_kernel(
    count, slot_ref, normal_ref, inv_ref, branch_ref, slope_ref, ct_ref, ctx_ref, vec_refs, bi_refs, first_ref, *rest
):
    out_ref, dctx_ref, delta_ref, sum_ref, sums_ref, keep_ref, acc_ref, low_ref, late_ref, late_sem = rest[-10:]


    @pl.when(pl.program_id(0) == 0)
    def _():
        sums_ref[...] = jnp.zeros_like(sums_ref)
        wait_all(fetch_sets(rest[:count], late_ref, late_sem))

    gain_one, bias_one, gain_two, bias_two = [row_of(ref) for ref in vec_refs]
    weight = partial(piece_weight, first_ref, late_ref, slot_ref)
    strips = [slice(start, start + STRIP) for start in range(0, TILE, STRIP)]

    def add(total, term):
        term = jnp.sum(term.reshape(STRIP // 8, 8, D), 0)
        return term if total is None else total + term

    for rows in strips:
        low_ref[rows] = low(normal_ref[rows] * gain_one + bias_one)
    normed_low = low_ref[...]
    branch = branch_ref[...]
    def inner_of(piece):
        return mul(normed_low, weight(piece, 0)) + piece_bias(bi_refs, piece)

    late_pieces = PIECES[2:]
    inner = inner_of(late_pieces[0])
    for i, piece in enumerate(late_pieces):
        following = inner_of(late_pieces[i + 1]) if i + 1 < len(late_pieces) else None
        act, slope = gelu_and_slope(inner)
        flat = flat_of(piece)
        keep_ref[:, flat.start - 2 * FIRST : flat.stop - 2 * FIRST] = low(slope)
        branch = branch + mul(low(act), weight(piece, 1), NT)
        inner = following
    acc_ref[...] = branch
    sums = [None] * 4
    for rows in strips:
        final, normal_two, inverse_two = norm_forward(acc_ref[rows], gain_two, bias_two)
        out_ref[rows] = low(final)
        final_grad = wide(ct_ref[rows])
        sum_two = norm_backward(final_grad, normal_two, inverse_two, gain_two)
        acc_ref[rows] = sum_two
        low_ref[rows] = low(sum_two)
        sums[2] = add(sums[2], wide(low(sum_two)))
        sums[3] = add(sums[3], final_grad)
    branch_grad = low_ref[...]
    normed_grad = acc_ref[...]
    for piece in PIECES:
        flat = flat_of(piece)
        slope = keep_ref[:, flat.start - 2 * FIRST : flat.stop - 2 * FIRST] if piece[0] else slope_ref[:, flat]
        inner_grad = low(mul(branch_grad, weight(piece, 1)) * wide(slope))
        late, other = piece[:2]
        place = pl.ds(4 + 2 * (slot_ref[2, 0] ^ other) + int(late), 1)
        sums_ref[place, :] += jnp.sum(wide(inner_grad), 0, keepdims=True)
        normed_grad = normed_grad + mul(inner_grad, weight(piece, 0), NT)
    acc_ref[...] = normed_grad
    for rows in strips:
        normed_grad = acc_ref[rows]
        sum_one = low(norm_backward(normed_grad, normal_ref[rows], inv_ref[rows, 0:1], gain_one))
        sum_ref[rows] = sum_one
        sums[0] = add(sums[0], wide(sum_one))
        sums[1] = add(sums[1], normed_grad)
    sum_one = sum_ref[...]
    out_weight = jnp.concatenate([out_columns(first_ref, slot_ref, group) for group in range(GROUPS)], 1)
    all_grads = low(mul(sum_one, out_weight))
    for group in range(GROUPS):
        part = slice(group * WIDE, (group + 1) * WIDE)
        context_grad = all_grads[:, part].T
        dctx_ref[0, part] = context_grad
        product = wide(context_grad) * wide(ctx_ref[0, part])
        for head in range(GROUP):
            own = slice(head * HEAD_DIM, (head + 1) * HEAD_DIM)
            delta_ref[0, group, head : head + 1, :] = jnp.sum(product[own], 0, keepdims=True)
    for i, term in enumerate(sums):
        sums_ref[i : i + 1, :] += jnp.sum(term, 0, keepdims=True)


def params(grid_rank):
    return pltpu.CompilerParams(
        dimension_semantics=("arbitrary",) * grid_rank, vmem_limit_bytes=VMEM_BYTES
    )


def cost(flops, moved):
    return pl.CostEstimate(flops=int(flops), bytes_accessed=int(moved), transcendentals=0)


SCALARS = pl.BlockSpec(memory_space=pltpu.SMEM)
ANYWHERE = pl.BlockSpec(memory_space=pl.ANY)


def wholes(arrays):
    return tuple(whole(array) for array in arrays)


def whole(array):
    return pl.BlockSpec(array.shape, lambda *_: (0,) * array.ndim, pipeline_mode=pl.Buffered(1))


def slot_scratch(pieces, sets):
    count = len(pieces) // sets
    n = sum(w.shape[0] for w in pieces[:count])
    return [
        pltpu.VMEM((sets, n) + pieces[0].shape[1:], pieces[0].dtype),
        pltpu.SemaphoreType.DMA((sets, count)),
    ]


def attend(step, earlier, tokens, seg_col, seg_row, fills, slots, pieces, bias):
    rows = tokens.shape[0] // SLOTS
    return pl.pallas_call(
        partial(attend_kernel, step, len(pieces)),
        grid=(rows,),
        in_specs=[
            SCALARS,
            SCALARS,
            pl.BlockSpec((SLOTS, D), lambda r: (r, 0)),
            pl.BlockSpec((1, SLOTS, 1), lambda r: (r, 0, 0)),
            pl.BlockSpec((1, 1, SLOTS), lambda r: (r, 0, 0)),
            whole(bias),
        ]
        + [ANYWHERE] * (len(pieces) + len(earlier)),
        out_specs=[
            pl.BlockSpec((2, 1, WIDE, SLOTS), lambda r: (0, r, step, 0)),
            pl.BlockSpec((2, SLOTS, WIDE), lambda r: (0, r, step)),
            pl.BlockSpec((1, WIDE, SLOTS), lambda r: (r, step, 0)),
            pl.BlockSpec((1, 1, GROUP, SLOTS), lambda r: (r, step, 0, 0)),
        ],
        out_shape=[
            jax.ShapeDtypeStruct((2, rows, D, SLOTS), jnp.bfloat16),
            jax.ShapeDtypeStruct((2, rows * SLOTS, D), jnp.bfloat16),
            jax.ShapeDtypeStruct((rows, D, SLOTS), jnp.bfloat16),
            jax.ShapeDtypeStruct((rows, GROUPS, GROUP, SLOTS), jnp.float32),
        ],
        scratch_shapes=[
            pltpu.VMEM((sum(w.shape[0] for w in pieces),) + pieces[0].shape[1:], jnp.bfloat16),
            pltpu.SemaphoreType.DMA((len(pieces),)),
        ],
        input_output_aliases={6 + len(pieces) + i: i for i in range(len(earlier))},
        compiler_params=params(1),
        cost_estimate=cost(15e9, 10e6),
        name="attend",
    )(fills, slots, tokens, seg_col, seg_row, bias, *pieces, *earlier)


def attend_back(qk, kv, context_grad, delta, lse, seg_col, seg_row, fills, slots, weights, sum_one):
    rows = kv.shape[1] // SLOTS
    return pl.pallas_call(
        partial(attend_back_kernel, len(weights)),
        grid=(rows, GROUPS),
        in_specs=[
            SCALARS,
            SCALARS,
            pl.BlockSpec((2, 1, WIDE, SLOTS), lambda r, g: (0, r, g, 0)),
            pl.BlockSpec((2, SLOTS, WIDE), lambda r, g: (0, r, g)),
            pl.BlockSpec((1, WIDE, SLOTS), lambda r, g: (r, g, 0)),
            pl.BlockSpec((1, 1, GROUP, SLOTS), lambda r, g: (r, g, 0, 0)),
            pl.BlockSpec((1, 1, GROUP, SLOTS), lambda r, g: (r, g, 0, 0)),
            pl.BlockSpec((1, SLOTS, 1), lambda r, g: (r, 0, 0)),
            pl.BlockSpec((1, 1, SLOTS), lambda r, g: (r, 0, 0)),
        ]
        + [ANYWHERE] * len(weights)
        + [pl.BlockSpec((SLOTS, D), lambda r, g: (r, 0))],
        out_specs=[
            pl.BlockSpec((SLOTS, D), lambda r, g: (r, 0)),
            pl.BlockSpec((2, D), lambda r, g: (0, 0)),
        ],
        out_shape=[
            jax.ShapeDtypeStruct((rows * SLOTS, D), jnp.bfloat16),
            jax.ShapeDtypeStruct((2, D), jnp.float32),
        ],
        scratch_shapes=[
            pltpu.VMEM((SLOTS, SLOTS), jnp.float32),
            pltpu.VMEM((SLOTS, D), jnp.float32),
        ]
        + slot_scratch(weights, GROUPS),
        compiler_params=params(2),
        cost_estimate=cost(50e9, 30e6),
        name="attend_back",
    )(fills, slots, qk, kv, context_grad, delta, lse, seg_col, seg_row, *weights, sum_one)


def tiles(width, tile=TILE):
    return pl.BlockSpec((tile, width), lambda i: (i, 0))


PER_ROW = SLOTS // TILE
ROWS_T = pl.BlockSpec((1, D, TILE), lambda i: (i // PER_ROW, 0, i % PER_ROW))


def feed_front(slots, tokens, context, first, vectors, in_bias):
    count = tokens.shape[0]
    return pl.pallas_call(
        front_kernel,
        grid=(count // FRONT_TILE,),
        in_specs=[SCALARS, tiles(D, FRONT_TILE), pl.BlockSpec((1, D, SLOTS), lambda i: (i, 0, 0)), wholes(vectors), wholes(in_bias), whole(first)],
        out_specs=[tiles(D, FRONT_TILE), tiles(128, FRONT_TILE), tiles(D, FRONT_TILE), tiles(2 * FIRST, FRONT_TILE)],
        out_shape=[
            jax.ShapeDtypeStruct((count, D), jnp.float32),
            jax.ShapeDtypeStruct((count, 128), jnp.float32),
            jax.ShapeDtypeStruct((count, D), jnp.float32),
            jax.ShapeDtypeStruct((count, 2 * FIRST), jnp.bfloat16),
        ],
        scratch_shapes=[pltpu.VMEM((FRONT_TILE, D), jnp.bfloat16)],
        compiler_params=params(1),
        cost_estimate=cost(25e9, 30e6),
        name="feed_front",
    )(slots, tokens, context, vectors, in_bias, first)


def feed_back(slots, front, cotangent, context, first, late, vectors, in_bias):
    count = cotangent.shape[0]
    return pl.pallas_call(
        partial(back_kernel, len(late)),
        grid=(count // TILE,),
        in_specs=[SCALARS, tiles(D), tiles(128), tiles(D), tiles(2 * FIRST), tiles(D), ROWS_T, wholes(vectors), wholes(in_bias), whole(first)]
        + [ANYWHERE] * len(late),
        out_specs=[
            tiles(D),
            ROWS_T,
            pl.BlockSpec((1, GROUPS, GROUP, TILE), lambda i: (i // PER_ROW, 0, 0, i % PER_ROW)),
            tiles(D),
            pl.BlockSpec((8, D), lambda i: (0, 0)),
        ],
        out_shape=[
            jax.ShapeDtypeStruct((count, D), jnp.bfloat16),
            jax.ShapeDtypeStruct((count // SLOTS, D, SLOTS), jnp.bfloat16),
            jax.ShapeDtypeStruct((count // SLOTS, GROUPS, GROUP, SLOTS), jnp.float32),
            jax.ShapeDtypeStruct((count, D), jnp.bfloat16),
            jax.ShapeDtypeStruct((8, D), jnp.float32),
        ],
        scratch_shapes=[
            pltpu.VMEM((TILE, 2 * LATE), jnp.bfloat16),
            pltpu.VMEM((TILE, D), jnp.float32),
            pltpu.VMEM((TILE, D), jnp.bfloat16),
        ]
        + slot_scratch(late, 2),
        compiler_params=params(1),
        cost_estimate=cost(75e9, 40e6),
        name="feed_back",
    )(slots, *front, cotangent, context, vectors, in_bias, first, *late)


def stage_bits(n):
    bits = n.bit_length() - 1
    in_z = -(-bits // 3)
    in_y = -(-(bits - in_z) // 2)
    in_x = bits - in_z - in_y
    x = list(range(in_x))
    y = list(range(in_x, in_x + in_y))
    z = list(range(in_x + in_y, bits))
    return z + y + x, z[::-1] + x + y


def partner(block, n, stage):
    bits = [order[stage] for order in stage_bits(n)]
    pairs = [(2 * i + core, 2 * (i ^ (1 << bits[core])) + core) for i in range(n) for core in range(2)]
    return lax.ppermute(block, ("rows", "tp"), pairs)


def joined(*blocks):
    return jnp.concatenate(blocks, 0)


def swap_cores(block):
    return lax.ppermute(block, "tp", [(0, 1), (1, 0)])


def after(value, *earlier):
    return lax.optimization_barrier((value, earlier))[0]


def together(*values):
    return lax.optimization_barrier(values)


def slot_table(n):
    apart = jnp.arange(n, dtype=jnp.int32) ^ lax.axis_index("rows")
    tables = []
    for order in stage_bits(n):
        tables.append(sum(((apart >> bit) & 1) << place for place, bit in enumerate(order)))
    core = lax.axis_index("tp")
    ordered = jnp.where(core == 0, jnp.stack(tables), jnp.stack(tables[::-1]))
    return jnp.concatenate([ordered, jnp.full((1, n), core, jnp.int32)], 0)


def sum_over_rows(values, n, beside):
    bits = n.bit_length() - 1

    def got(distance):
        return lax.ppermute(values, "rows", [(i, i ^ distance) for i in range(n)])

    for bit in range(0, bits - 1, 2):
        near, far, both = [got(j << bit) for j in (1, 2, 3)]
        near, far, both, beside = together(near, far, both, beside)
        values = (values + near) + (far + both)
    return values + got(1 << (bits - 1)) if bits % 2 else values, beside


def shards(
    tokens,
    segment_ids,
    fill_counts,
    qkv_weight,
    qv_bias,
    out_weight,
    out_bias,
    norm1_gain,
    norm1_bias,
    in_weight,
    in_bias,
    down_weight,
    down_bias,
    norm2_gain,
    norm2_bias,
    cotangent,
):
    n = lax.axis_size("rows")
    core = lax.axis_index("tp")
    rows_here = tokens.shape[0] // SLOTS
    down_t = down_weight.T

    last = n.bit_length() - 2

    def spread(block, stages):
        for stage in stages:
            block = joined(block, partner(block, n, stage))
        return block

    a = qkv_weight[None, :, :, :WIDE]
    a = joined(a, partner(a, n, 0))
    a, b = together(a, qkv_weight[None, :, :, WIDE:])
    a_got = partner(a, n, 1)
    b_got = partner(b, n, 0)
    first = jnp.concatenate([in_weight[:, :FIRST], down_t[:, :FIRST], out_weight.T], 1)

    a, a_got, b, b_got, first = together(a, a_got, b, b_got, first)
    first = lax.all_gather(first, ("rows", "tp"), axis=0, tiled=False).reshape((n, 2) + first.shape)
    a = joined(a, a_got)
    b = joined(b, b_got)
    for stage in range(2, last):
        a_got = partner(a, n, stage)
        a = a if stage == last - 1 else joined(a, a_got)
    b_got = partner(b, n, 1)
    segments = lax.dynamic_slice_in_dim(segment_ids, core * rows_here, rows_here, 0)
    fills = lax.dynamic_slice_in_dim(fill_counts, core * rows_here, rows_here, 0)
    slots = slot_table(n)
    small = (segments[:, :, None], segments[:, None, :], fills, slots)
    b_qv = (qv_bias, swap_cores(qv_bias))
    b_in = (in_bias, swap_cores(in_bias))
    late = jnp.concatenate([in_weight[:, FIRST:], down_t[:, FIRST:]], 1)[None]

    a, a_got, b, b_got, late, small, b_qv, b_in = together(a, a_got, b, b_got, late, small, b_qv, b_in)
    a = joined(a, a_got)
    a_other = swap_cores(a)
    a_got = partner(a, n, last)
    b = joined(b, b_got)

    def run(step, earlier, *pieces):
        return attend(step, earlier, tokens, *small, pieces, b_qv[step % 2])

    a, a_got, a_other, b, late = together(a, a_got, a_other, b, late)
    a_other_got = swap_cores(a_got)
    for stage in range(2, last):
        b_got = partner(b, n, stage)
        b = b if stage == last - 1 else joined(b, b_got)
    late_got = partner(late, n, 0)
    results = run(0, (), a, a_got)

    results, a_other_got, b, b_got, late, late_got = together(results, a_other_got, b, b_got, late, late_got)
    b = joined(b, b_got)
    late = joined(late, late_got)
    late_got = partner(late, n, 1)
    b_other = swap_cores(b)
    b_got = partner(b, n, last)
    results = run(1, results, a_other, a_other_got)

    results, b_other, b_got = together(results, b_other, b_got)
    b_other_got = swap_cores(b_got)
    results = run(2, results, b, b_got)

    results, b_other_got, late, late_got = together(results, b_other_got, late, late_got)
    late = joined(late, late_got)
    for stage in range(2, last):
        late_got = partner(late, n, stage)
        late = late if stage == last - 1 else joined(late, late_got)
    results = run(3, results, b_other, b_other_got)

    results, late, late_got = together(results, late, late_got)
    late_own = [late, late_got]
    late_others = [swap_cores(w) for w in late_own]
    late_far = [partner(w, n, last) for w in late_own]

    qk, kv, context, lse = results
    front = feed_front(slots, tokens, context, first, (out_bias, norm1_gain, norm1_bias, down_bias), b_in)

    front, late_others, late_far = together(front, late_others, late_far)
    late_others += [swap_cores(w) for w in late_far]
    vectors = (norm1_gain, norm1_bias, norm2_gain, norm2_bias)
    layer_out, context_grad, delta, sum_one, grads = feed_back(
        slots, front, cotangent, context, first, late_own + late_far + late_others, vectors, b_in
    )
    sums = jnp.sum(lax.all_gather(grads, ("rows", "tp"), axis=0), 0)
    sums = [sums[0], sums[1], sums[4:].reshape(-1), sums[2], sums[3]]
    a_set = [a, a_got, a_other, a_other_got]
    b_set = [b, b_got, b_other, b_other_got]
    tokens_grad, qv_grads = attend_back(
        qk, kv, context_grad, delta, lse, *small, a_set + b_set, sum_one
    )
    qv, sums = sum_over_rows(qv_grads + swap_cores(qv_grads), n, sums)
    return (layer_out, tokens_grad, qv, *sums)


def solution(mesh):
    return jax.shard_map(
        shards,
        mesh=mesh,
        in_specs=(
            P(("rows", "tp"), None),
            P("rows", None),
            P("rows"),
            P(None, "rows", "tp"),
            P(None, "tp"),
            P("tp", "rows"),
            P(),
            P(),
            P(),
            P("rows", "tp"),
            P("tp"),
            P("tp", "rows"),
            P(),
            P(),
            P(),
            P(("rows", "tp"), None),
        ),
        out_specs=(P(("rows", "tp"), None), P(("rows", "tp"), None), P(), P(), P(), P(), P(), P()),
        check_vma=False,
    )
```

```python
from functools import partial
import math

import jax
import jax.numpy as jnp
from jax import lax
from jax.experimental import pallas as pl
from jax.experimental.pallas import tpu as pltpu
from jax.sharding import PartitionSpec as P

D = 1024
FF = 4096
HEADS = 16
HEAD_DIM = 64
SLOTS = 512
GROUP = 4
WIDE = GROUP * HEAD_DIM
PAIR = 2 * HEAD_DIM
GROUPS = HEADS // GROUP
FRONT_TILE = SLOTS
TILE = 256
STRIP = 32
EPSILON = 1e-05
MASKED = -1e30
SCALE = 1.0 / math.sqrt(HEAD_DIM)
VMEM_BYTES = 60 * 2**20

NN = (((1,), (0,)), ((), ()))
NT = (((1,), (1,)), ((), ()))
TT = (((0,), (1,)), ((), ()))


def mul(left, right, dims=NN):
    return lax.dot_general(left, right, dims, preferred_element_type=jnp.float32)


def low(values):
    return values.astype(jnp.bfloat16)


def wide(values):
    return values.astype(jnp.float32)


def norm_forward(summed, gain_vec, shift_vec):
    row_mean = jnp.mean(summed, -1, keepdims=True)
    centered = summed - row_mean
    inverse = lax.rsqrt(jnp.mean(centered * centered, -1, keepdims=True) + EPSILON)
    normal = centered * inverse
    return (normal * gain_vec + shift_vec, normal, inverse)


def norm_backward(grad_in, normal, inverse, gain_vec):
    scaled = grad_in * gain_vec
    return inverse * (
        scaled
        - jnp.mean(scaled, -1, keepdims=True)
        - normal * jnp.mean(scaled * normal, -1, keepdims=True)
    )


def mask_bias(seg_col, seg_row, filled):
    keys = lax.broadcasted_iota(jnp.int32, (SLOTS, SLOTS), 0)
    places = lax.broadcasted_iota(jnp.int32, (SLOTS, SLOTS), 1)
    allowed = (seg_col == seg_row) & ((keys < filled) | (keys == places))
    return jnp.where(allowed, 0.0, MASKED)


def half_rows(rows, head):
    zeros = jnp.zeros((HEAD_DIM, rows.shape[1]), rows.dtype)
    return jnp.concatenate([rows, zeros] if head % 2 == 0 else [zeros, rows], 0)


def fetch(refs, scratch, sem, start=True):
    copies = []
    for i, ref in enumerate(refs):
        size = ref.shape[0]
        copies.append(pltpu.make_async_copy(ref, scratch.at[pl.ds(i * size, size)], sem.at[i]))
        if start:
            copies[-1].start()
    return copies


def fetch_sets(refs, scratch, sem, start=True):
    sets = scratch.shape[0]
    size = len(refs) // sets
    copies = []
    for i in range(sets):
        copies += fetch(refs[i * size : (i + 1) * size], scratch.at[i], sem.at[i], start)
    return copies


def first_or_later(step, body):
    @pl.when(step == 0)
    def _():
        body(True)

    @pl.when(step != 0)
    def _():
        body(False)


def wait_all(copies):
    for copy in copies:
        copy.wait()


def set_weight(w_ref, slot_ref, other, part):
    return jnp.concatenate([w_ref[slot_ref[other, c], part] for c in range(w_ref.shape[0])], 0)


def columns_of(w_ref, slot_ref, other, columns):
    there = w_ref.at[other]
    return jnp.concatenate([there[slot_ref[other, c], :, columns] for c in range(there.shape[0])], 0)


def attend_kernel(step, count, fill_ref, slot_ref, x_ref, segc_ref, segr_ref, b_ref, *rest):
    other, half = step % 2, step // 2
    qk_ref, kv_ref, ctx_ref, lse_ref, w_ref, sem = rest[-6:]

    @pl.when(pl.program_id(0) == 0)
    def _():
        wait_all(fetch(rest[:count], w_ref, sem))

    x = x_ref[...]
    weight = [set_weight(w_ref, slot_ref, other, i) for i in range(3)]
    columns = slice(half * WIDE, (half + 1) * WIDE)
    biases = wide(b_ref[...])[:, columns]
    b_q, b_v = biases[0:1], biases[1:2]
    bias = mask_bias(segc_ref[0], segr_ref[0], fill_ref[pl.program_id(0)])
    q = low(mul(x, weight[0]) + b_q)
    k = low(mul(x, weight[1]))
    v = low(mul(x, weight[2]) + b_v)
    q_t = (q * jnp.bfloat16(SCALE)).T
    v_t = v.T
    qk_ref[0, 0] = q_t
    qk_ref[1, 0] = k.T
    kv_ref[0] = k
    kv_ref[1] = v
    ones = jnp.ones((HEAD_DIM, SLOTS), jnp.bfloat16)

    def score(head):
        own = slice(head * HEAD_DIM, (head + 1) * HEAD_DIM)
        pair = slice(head // 2 * PAIR, (head // 2 + 1) * PAIR)
        return mul(k[:, pair], half_rows(q_t[own], head)) + bias

    def finish(head, top, probs):
        own = slice(head * HEAD_DIM, (head + 1) * HEAD_DIM)
        out = mul(jnp.concatenate([v_t[own], ones], 0), probs)
        total = out[HEAD_DIM : HEAD_DIM + 1]
        ctx_ref[0, own] = low(out[:HEAD_DIM] / total)
        lse_ref[0, 0, head : head + 1, :] = top + jnp.log(total)

    scores = score(0)
    done = None
    for head in range(GROUP):
        following = score(head + 1) if head + 1 < GROUP else None
        if done is not None:
            finish(head - 1, *done)
        top = jnp.max(scores, 0, keepdims=True)
        done = top, low(jnp.exp(scores - top))
        scores = following
    finish(GROUP - 1, *done)


def attend_back_kernel(count, fill_ref, slot_ref, qk_ref, kv_ref, dctx_ref, delta_ref, lse_ref, segc_ref, segr_ref, *rest):
    sum_ref, out_ref, qvb_ref, bias_ref, acc_ref, w_ref, sem = rest[-7:]
    row = pl.program_id(0)
    group = pl.program_id(1)

    @pl.when(group == 0)
    def _():
        bias_ref[...] = mask_bias(segc_ref[0], segr_ref[0], fill_ref[row])
        acc_ref[...] = wide(sum_ref[...])

    def body(arriving):
        if arriving:
            qvb_ref[...] = jnp.zeros_like(qvb_ref)
            fetch_sets(rest[:count], w_ref, sem)
        d_q, d_k, d_v = [], [], []
        for head in range(GROUP):
            own = slice(head * HEAD_DIM, (head + 1) * HEAD_DIM)
            pair = slice(head // 2 * PAIR, (head // 2 + 1) * PAIR)
            q_t, k_t, d_out_t = qk_ref[0, 0, own], qk_ref[1, 0, own], dctx_ref[0, own]
            scores = mul(kv_ref[0, :, pair], half_rows(q_t, head)) + bias_ref[...]
            probs = jnp.exp(scores - lse_ref[0, 0, head : head + 1, :])
            probs_low = low(probs)
            probs_grad = mul(kv_ref[1, :, pair], half_rows(d_out_t, head))
            scores_grad = low(probs * (probs_grad - delta_ref[0, 0, head : head + 1, :]))
            d_v.append(low(mul(d_out_t, probs_low, NT)))
            d_q.append(low(mul(k_t, scores_grad) * SCALE))
            d_k.append(low(mul(q_t, scores_grad, NT)))
        if arriving:
            wait_all(fetch_sets(rest[:count], w_ref, sem, start=False))
        ones = jnp.ones((16, SLOTS), jnp.bfloat16)
        place = (slot_ref[2, 0] ^ (group % 2)) * 2 + group // 2
        columns = pl.ds(pl.multiple_of(place * WIDE, WIDE), WIDE)
        total = acc_ref[...]
        for i, grad in enumerate((d_q, d_k, d_v)):
            grad = jnp.concatenate(grad, 0)
            weight = set_weight(w_ref.at[group], slot_ref, group % 2, i)
            total = total + mul(grad, weight, TT)
            if i != 1:
                qvb_ref[i // 2 : i // 2 + 1, columns] += mul(ones, grad, NT)[0:1]
        acc_ref[...] = total

    first_or_later(row * GROUPS + group, body)

    @pl.when(group == GROUPS - 1)
    def _():
        out_ref[...] = low(acc_ref[...])


def gelu_and_slope(v):
    phi = 0.5 * (1.0 + lax.erf(v * math.sqrt(0.5)))
    bell = jnp.exp(-0.5 * v * v) * (1.0 / math.sqrt(2.0 * math.pi))
    return v * phi, phi + v * bell


FIRST = 1024
LATE = FF // 2 - FIRST
LATE_PIECE = 1024
PIECES = [(False, other, 0, FIRST) for other in range(2)]
PIECES += [(True, other, start, LATE_PIECE) for other in range(2) for start in range(0, LATE, LATE_PIECE)]


def flat_of(piece):
    late, other, start, size = piece
    begin = 2 * FIRST + other * LATE + start if late else other * FIRST
    return slice(begin, begin + size)


def first_columns(first_ref, slot_ref, other, columns):
    n, _, chunk, _ = first_ref.shape
    return first_ref[:, slot_ref[2, 0] ^ other, :, columns].reshape(n * chunk, columns.size)


def piece_weight(first_ref, late_ref, slot_ref, piece, down):
    late, other, start, size = piece
    if late:
        return columns_of(late_ref, slot_ref, other, pl.ds(down * LATE + start, size))
    return first_columns(first_ref, slot_ref, other, pl.ds(down * FIRST + start, size))


assert FIRST == LATE == LATE_PIECE == D


def piece_bias(b_refs, piece):
    late, other, start, size = piece
    begin = FIRST * late + start
    return wide(b_refs[other][...]).reshape(1, FF // 2)[:, begin : begin + size]


def out_columns(first_ref, slot_ref, group):
    return first_columns(first_ref, slot_ref, group % 2, pl.ds(2 * FIRST + group // 2 * WIDE, WIDE))


def row_of(ref):
    return wide(ref[...]).reshape(1, D)


def front_kernel(
    slot_ref, x_ref, ctx_ref, vec_refs, bi_refs, first_ref, normal_ref, inv_ref, branch_ref, slope_ref, low_ref
):
    out_bias, gain_one, bias_one, down_bias = [row_of(ref) for ref in vec_refs]
    out_weight = jnp.concatenate([out_columns(first_ref, slot_ref, group) for group in range(GROUPS)], 1)
    attention = mul(ctx_ref[0], out_weight, TT) + out_bias
    branch_ref[...] = attention
    for start in range(0, FRONT_TILE, STRIP):
        rows = slice(start, start + STRIP)
        normed, normal_one, inverse_one = norm_forward(wide(x_ref[rows]) + branch_ref[rows], gain_one, bias_one)
        normal_ref[rows] = normal_one
        inv_ref[rows] = jnp.broadcast_to(inverse_one, (STRIP, 128))
        low_ref[rows] = low(normed)
        branch_ref[rows] = normed + down_bias
    normed_low = low_ref[...]
    branch = branch_ref[...]

    def inner_of(piece):
        return mul(normed_low, piece_weight(first_ref, None, slot_ref, piece, 0)) + piece_bias(bi_refs, piece)

    inner = inner_of(PIECES[0])
    for piece in PIECES[:2]:
        following = inner_of(PIECES[1]) if piece is PIECES[0] else None
        act, slope = gelu_and_slope(inner)
        slope_ref[:, flat_of(piece)] = low(slope)
        branch = branch + mul(low(act), piece_weight(first_ref, None, slot_ref, piece, 1), NT)
        inner = following
    branch_ref[...] = branch


def back_kernel(
    count, slot_ref, normal_ref, inv_ref, branch_ref, slope_ref, ct_ref, ctx_ref, vec_refs, bi_refs, first_ref, *rest
):
    out_ref, dctx_ref, delta_ref, sum_ref, sums_ref, keep_ref, acc_ref, low_ref, late_ref, late_sem = rest[-10:]


    @pl.when(pl.program_id(0) == 0)
    def _():
        sums_ref[...] = jnp.zeros_like(sums_ref)
        wait_all(fetch_sets(rest[:count], late_ref, late_sem))

    gain_one, bias_one, gain_two, bias_two = [row_of(ref) for ref in vec_refs]
    weight = partial(piece_weight, first_ref, late_ref, slot_ref)
    strips = [slice(start, start + STRIP) for start in range(0, TILE, STRIP)]

    def add(total, term):
        term = jnp.sum(term.reshape(STRIP // 8, 8, D), 0)
        return term if total is None else total + term

    for rows in strips:
        low_ref[rows] = low(normal_ref[rows] * gain_one + bias_one)
    normed_low = low_ref[...]
    branch = branch_ref[...]
    def inner_of(piece):
        return mul(normed_low, weight(piece, 0)) + piece_bias(bi_refs, piece)

    late_pieces = PIECES[2:]
    inner = inner_of(late_pieces[0])
    for i, piece in enumerate(late_pieces):
        following = inner_of(late_pieces[i + 1]) if i + 1 < len(late_pieces) else None
        act, slope = gelu_and_slope(inner)
        flat = flat_of(piece)
        keep_ref[:, flat.start - 2 * FIRST : flat.stop - 2 * FIRST] = low(slope)
        branch = branch + mul(low(act), weight(piece, 1), NT)
        inner = following
    acc_ref[...] = branch
    sums = [None] * 4
    for rows in strips:
        final, normal_two, inverse_two = norm_forward(acc_ref[rows], gain_two, bias_two)
        out_ref[rows] = low(final)
        final_grad = wide(ct_ref[rows])
        sum_two = norm_backward(final_grad, normal_two, inverse_two, gain_two)
        acc_ref[rows] = sum_two
        low_ref[rows] = low(sum_two)
        sums[2] = add(sums[2], wide(low(sum_two)))
        sums[3] = add(sums[3], final_grad)
    branch_grad = low_ref[...]
    normed_grad = acc_ref[...]
    for piece in PIECES:
        flat = flat_of(piece)
        slope = keep_ref[:, flat.start - 2 * FIRST : flat.stop - 2 * FIRST] if piece[0] else slope_ref[:, flat]
        inner_grad = low(mul(branch_grad, weight(piece, 1)) * wide(slope))
        late, other = piece[:2]
        place = pl.ds(4 + 2 * (slot_ref[2, 0] ^ other) + int(late), 1)
        sums_ref[place, :] += jnp.sum(wide(inner_grad), 0, keepdims=True)
        normed_grad = normed_grad + mul(inner_grad, weight(piece, 0), NT)
    acc_ref[...] = normed_grad
    for rows in strips:
        normed_grad = acc_ref[rows]
        sum_one = low(norm_backward(normed_grad, normal_ref[rows], inv_ref[rows, 0:1], gain_one))
        sum_ref[rows] = sum_one
        sums[0] = add(sums[0], wide(sum_one))
        sums[1] = add(sums[1], normed_grad)
    sum_one = sum_ref[...]
    out_weight = jnp.concatenate([out_columns(first_ref, slot_ref, group) for group in range(GROUPS)], 1)
    all_grads = low(mul(sum_one, out_weight))
    for group in range(GROUPS):
        part = slice(group * WIDE, (group + 1) * WIDE)
        context_grad = all_grads[:, part].T
        dctx_ref[0, part] = context_grad
        product = wide(context_grad) * wide(ctx_ref[0, part])
        for head in range(GROUP):
            own = slice(head * HEAD_DIM, (head + 1) * HEAD_DIM)
            delta_ref[0, group, head : head + 1, :] = jnp.sum(product[own], 0, keepdims=True)
    for i, term in enumerate(sums):
        sums_ref[i : i + 1, :] += jnp.sum(term, 0, keepdims=True)


def params(grid_rank):
    return pltpu.CompilerParams(
        dimension_semantics=("arbitrary",) * grid_rank, vmem_limit_bytes=VMEM_BYTES
    )


def cost(flops, moved):
    return pl.CostEstimate(flops=int(flops), bytes_accessed=int(moved), transcendentals=0)


SCALARS = pl.BlockSpec(memory_space=pltpu.SMEM)
ANYWHERE = pl.BlockSpec(memory_space=pl.ANY)


def wholes(arrays):
    return tuple(whole(array) for array in arrays)


def whole(array):
    return pl.BlockSpec(array.shape, lambda *_: (0,) * array.ndim, pipeline_mode=pl.Buffered(1))


def slot_scratch(pieces, sets):
    count = len(pieces) // sets
    n = sum(w.shape[0] for w in pieces[:count])
    return [
        pltpu.VMEM((sets, n) + pieces[0].shape[1:], pieces[0].dtype),
        pltpu.SemaphoreType.DMA((sets, count)),
    ]


def attend(step, earlier, tokens, seg_col, seg_row, fills, slots, pieces, bias):
    rows = tokens.shape[0] // SLOTS
    return pl.pallas_call(
        partial(attend_kernel, step, len(pieces)),
        grid=(rows,),
        in_specs=[
            SCALARS,
            SCALARS,
            pl.BlockSpec((SLOTS, D), lambda r: (r, 0)),
            pl.BlockSpec((1, SLOTS, 1), lambda r: (r, 0, 0)),
            pl.BlockSpec((1, 1, SLOTS), lambda r: (r, 0, 0)),
            whole(bias),
        ]
        + [ANYWHERE] * (len(pieces) + len(earlier)),
        out_specs=[
            pl.BlockSpec((2, 1, WIDE, SLOTS), lambda r: (0, r, step, 0)),
            pl.BlockSpec((2, SLOTS, WIDE), lambda r: (0, r, step)),
            pl.BlockSpec((1, WIDE, SLOTS), lambda r: (r, step, 0)),
            pl.BlockSpec((1, 1, GROUP, SLOTS), lambda r: (r, step, 0, 0)),
        ],
        out_shape=[
            jax.ShapeDtypeStruct((2, rows, D, SLOTS), jnp.bfloat16),
            jax.ShapeDtypeStruct((2, rows * SLOTS, D), jnp.bfloat16),
            jax.ShapeDtypeStruct((rows, D, SLOTS), jnp.bfloat16),
            jax.ShapeDtypeStruct((rows, GROUPS, GROUP, SLOTS), jnp.float32),
        ],
        scratch_shapes=[
            pltpu.VMEM((sum(w.shape[0] for w in pieces),) + pieces[0].shape[1:], jnp.bfloat16),
            pltpu.SemaphoreType.DMA((len(pieces),)),
        ],
        input_output_aliases={6 + len(pieces) + i: i for i in range(len(earlier))},
        compiler_params=params(1),
        cost_estimate=cost(15e9, 10e6),
        name="attend",
    )(fills, slots, tokens, seg_col, seg_row, bias, *pieces, *earlier)


def attend_back(qk, kv, context_grad, delta, lse, seg_col, seg_row, fills, slots, weights, sum_one):
    rows = kv.shape[1] // SLOTS
    return pl.pallas_call(
        partial(attend_back_kernel, len(weights)),
        grid=(rows, GROUPS),
        in_specs=[
            SCALARS,
            SCALARS,
            pl.BlockSpec((2, 1, WIDE, SLOTS), lambda r, g: (0, r, g, 0)),
            pl.BlockSpec((2, SLOTS, WIDE), lambda r, g: (0, r, g)),
            pl.BlockSpec((1, WIDE, SLOTS), lambda r, g: (r, g, 0)),
            pl.BlockSpec((1, 1, GROUP, SLOTS), lambda r, g: (r, g, 0, 0)),
            pl.BlockSpec((1, 1, GROUP, SLOTS), lambda r, g: (r, g, 0, 0)),
            pl.BlockSpec((1, SLOTS, 1), lambda r, g: (r, 0, 0)),
            pl.BlockSpec((1, 1, SLOTS), lambda r, g: (r, 0, 0)),
        ]
        + [ANYWHERE] * len(weights)
        + [pl.BlockSpec((SLOTS, D), lambda r, g: (r, 0))],
        out_specs=[
            pl.BlockSpec((SLOTS, D), lambda r, g: (r, 0)),
            pl.BlockSpec((2, D), lambda r, g: (0, 0)),
        ],
        out_shape=[
            jax.ShapeDtypeStruct((rows * SLOTS, D), jnp.bfloat16),
            jax.ShapeDtypeStruct((2, D), jnp.float32),
        ],
        scratch_shapes=[
            pltpu.VMEM((SLOTS, SLOTS), jnp.float32),
            pltpu.VMEM((SLOTS, D), jnp.float32),
        ]
        + slot_scratch(weights, GROUPS),
        compiler_params=params(2),
        cost_estimate=cost(50e9, 30e6),
        name="attend_back",
    )(fills, slots, qk, kv, context_grad, delta, lse, seg_col, seg_row, *weights, sum_one)


def tiles(width, tile=TILE):
    return pl.BlockSpec((tile, width), lambda i: (i, 0))


PER_ROW = SLOTS // TILE
ROWS_T = pl.BlockSpec((1, D, TILE), lambda i: (i // PER_ROW, 0, i % PER_ROW))


def feed_front(slots, tokens, context, first, vectors, in_bias):
    count = tokens.shape[0]
    return pl.pallas_call(
        front_kernel,
        grid=(count // FRONT_TILE,),
        in_specs=[SCALARS, tiles(D, FRONT_TILE), pl.BlockSpec((1, D, SLOTS), lambda i: (i, 0, 0)), wholes(vectors), wholes(in_bias), whole(first)],
        out_specs=[tiles(D, FRONT_TILE), tiles(128, FRONT_TILE), tiles(D, FRONT_TILE), tiles(2 * FIRST, FRONT_TILE)],
        out_shape=[
            jax.ShapeDtypeStruct((count, D), jnp.float32),
            jax.ShapeDtypeStruct((count, 128), jnp.float32),
            jax.ShapeDtypeStruct((count, D), jnp.float32),
            jax.ShapeDtypeStruct((count, 2 * FIRST), jnp.bfloat16),
        ],
        scratch_shapes=[pltpu.VMEM((FRONT_TILE, D), jnp.bfloat16)],
        compiler_params=params(1),
        cost_estimate=cost(25e9, 30e6),
        name="feed_front",
    )(slots, tokens, context, vectors, in_bias, first)


def feed_back(slots, front, cotangent, context, first, late, vectors, in_bias):
    count = cotangent.shape[0]
    return pl.pallas_call(
        partial(back_kernel, len(late)),
        grid=(count // TILE,),
        in_specs=[SCALARS, tiles(D), tiles(128), tiles(D), tiles(2 * FIRST), tiles(D), ROWS_T, wholes(vectors), wholes(in_bias), whole(first)]
        + [ANYWHERE] * len(late),
        out_specs=[
            tiles(D),
            ROWS_T,
            pl.BlockSpec((1, GROUPS, GROUP, TILE), lambda i: (i // PER_ROW, 0, 0, i % PER_ROW)),
            tiles(D),
            pl.BlockSpec((8, D), lambda i: (0, 0)),
        ],
        out_shape=[
            jax.ShapeDtypeStruct((count, D), jnp.bfloat16),
            jax.ShapeDtypeStruct((count // SLOTS, D, SLOTS), jnp.bfloat16),
            jax.ShapeDtypeStruct((count // SLOTS, GROUPS, GROUP, SLOTS), jnp.float32),
            jax.ShapeDtypeStruct((count, D), jnp.bfloat16),
            jax.ShapeDtypeStruct((8, D), jnp.float32),
        ],
        scratch_shapes=[
            pltpu.VMEM((TILE, 2 * LATE), jnp.bfloat16),
            pltpu.VMEM((TILE, D), jnp.float32),
            pltpu.VMEM((TILE, D), jnp.bfloat16),
        ]
        + slot_scratch(late, 2),
        compiler_params=params(1),
        cost_estimate=cost(75e9, 40e6),
        name="feed_back",
    )(slots, *front, cotangent, context, vectors, in_bias, first, *late)


def stage_bits(n):
    bits = n.bit_length() - 1
    in_z = -(-bits // 3)
    in_y = -(-(bits - in_z) // 2)
    in_x = bits - in_z - in_y
    x = list(range(in_x))
    y = list(range(in_x, in_x + in_y))
    z = list(range(in_x + in_y, bits))
    return z + y + x, z[::-1] + x + y


def partner(block, n, stage):
    bits = [order[stage] for order in stage_bits(n)]
    pairs = [(2 * i + core, 2 * (i ^ (1 << bits[core])) + core) for i in range(n) for core in range(2)]
    return lax.ppermute(block, ("rows", "tp"), pairs)


def joined(*blocks):
    return jnp.concatenate(blocks, 0)


def swap_cores(block):
    return lax.ppermute(block, "tp", [(0, 1), (1, 0)])


def after(value, *earlier):
    return lax.optimization_barrier((value, earlier))[0]


def together(*values):
    return lax.optimization_barrier(values)


def slot_table(n):
    apart = jnp.arange(n, dtype=jnp.int32) ^ lax.axis_index("rows")
    tables = []
    for order in stage_bits(n):
        tables.append(sum(((apart >> bit) & 1) << place for place, bit in enumerate(order)))
    core = lax.axis_index("tp")
    ordered = jnp.where(core == 0, jnp.stack(tables), jnp.stack(tables[::-1]))
    return jnp.concatenate([ordered, jnp.full((1, n), core, jnp.int32)], 0)


def sum_over_rows(values, n, beside, steps):
    bits = n.bit_length() - 1

    def got(distance):
        return lax.ppermute(values, "rows", [(i, i ^ distance) for i in range(n)])

    for bit in range(0, bits - 1, 2):
        near, far, both = [got(j << bit) for j in (1, 2, 3)]
        if steps:
            beside = steps[0](beside)
            steps = steps[1:]
        near, far, both, beside = together(near, far, both, beside)
        values = (values + near) + (far + both)
    values = values + got(1 << (bits - 1)) if bits % 2 else values
    for step in steps:
        beside = step(beside)
    return values, beside


def shards(
    tokens,
    segment_ids,
    fill_counts,
    qkv_weight,
    qv_bias,
    out_weight,
    out_bias,
    norm1_gain,
    norm1_bias,
    in_weight,
    in_bias,
    down_weight,
    down_bias,
    norm2_gain,
    norm2_bias,
    cotangent,
):
    n = lax.axis_size("rows")
    core = lax.axis_index("tp")
    rows_here = tokens.shape[0] // SLOTS
    down_t = down_weight.T

    last = n.bit_length() - 2

    def spread(block, stages):
        for stage in stages:
            block = joined(block, partner(block, n, stage))
        return block

    a = qkv_weight[None, :, :, :WIDE]
    a = joined(a, partner(a, n, 0))
    a, b = together(a, qkv_weight[None, :, :, WIDE:])
    a_got = partner(a, n, 1)
    b_got = partner(b, n, 0)
    first = jnp.concatenate([in_weight[:, :FIRST], down_t[:, :FIRST], out_weight.T], 1)

    a, a_got, b, b_got, first = together(a, a_got, b, b_got, first)
    first = lax.all_gather(first, ("rows", "tp"), axis=0, tiled=False).reshape((n, 2) + first.shape)
    a = joined(a, a_got)
    b = joined(b, b_got)
    for stage in range(2, last):
        a_got = partner(a, n, stage)
        a = a if stage == last - 1 else joined(a, a_got)
    b_got = partner(b, n, 1)
    segments = lax.dynamic_slice_in_dim(segment_ids, core * rows_here, rows_here, 0)
    fills = lax.dynamic_slice_in_dim(fill_counts, core * rows_here, rows_here, 0)
    slots = slot_table(n)
    small = (segments[:, :, None], segments[:, None, :], fills, slots)
    b_qv = (qv_bias, swap_cores(qv_bias))
    b_in = (in_bias, swap_cores(in_bias))
    late = jnp.concatenate([in_weight[:, FIRST:], down_t[:, FIRST:]], 1)[None]

    a, a_got, b, b_got, late, small, b_qv, b_in = together(a, a_got, b, b_got, late, small, b_qv, b_in)
    a = joined(a, a_got)
    a_other = swap_cores(a)
    a_got = partner(a, n, last)
    b = joined(b, b_got)

    def run(step, earlier, *pieces):
        return attend(step, earlier, tokens, *small, pieces, b_qv[step % 2])

    a, a_got, a_other, b, late = together(a, a_got, a_other, b, late)
    a_other_got = swap_cores(a_got)
    for stage in range(2, last):
        b_got = partner(b, n, stage)
        b = b if stage == last - 1 else joined(b, b_got)
    late_got = partner(late, n, 0)
    results = run(0, (), a, a_got)

    results, a_other_got, b, b_got, late, late_got = together(results, a_other_got, b, b_got, late, late_got)
    b = joined(b, b_got)
    late = joined(late, late_got)
    late_got = partner(late, n, 1)
    b_other = swap_cores(b)
    b_got = partner(b, n, last)
    results = run(1, results, a_other, a_other_got)

    results, b_other, b_got = together(results, b_other, b_got)
    b_other_got = swap_cores(b_got)
    results = run(2, results, b, b_got)

    results, b_other_got, late, late_got = together(results, b_other_got, late, late_got)
    late = joined(late, late_got)
    for stage in range(2, last):
        late_got = partner(late, n, stage)
        late = late if stage == last - 1 else joined(late, late_got)
    results = run(3, results, b_other, b_other_got)

    results, late, late_got = together(results, late, late_got)
    late_own = [late, late_got]
    late_others = [swap_cores(w) for w in late_own]
    late_far = [partner(w, n, last) for w in late_own]

    qk, kv, context, lse = results
    front = feed_front(slots, tokens, context, first, (out_bias, norm1_gain, norm1_bias, down_bias), b_in)

    front, late_others, late_far = together(front, late_others, late_far)
    late_others += [swap_cores(w) for w in late_far]
    vectors = (norm1_gain, norm1_bias, norm2_gain, norm2_bias)
    layer_out, context_grad, delta, sum_one, grads = feed_back(
        slots, front, cotangent, context, first, late_own + late_far + late_others, vectors, b_in
    )
    grads = lax.all_gather(grads, ("rows", "tp"), axis=0)

    def summed(grads):
        return jnp.sum(grads, 0)

    def taken_apart(sums):
        return sums[0], sums[1], sums[4:].reshape(-1), sums[2], sums[3]

    a_set = [a, a_got, a_other, a_other_got]
    b_set = [b, b_got, b_other, b_other_got]
    tokens_grad, qv_grads = attend_back(
        qk, kv, context_grad, delta, lse, *small, a_set + b_set, sum_one
    )
    qv, sums = sum_over_rows(qv_grads + swap_cores(qv_grads), n, grads, (summed, taken_apart))
    return (layer_out, tokens_grad, qv, *sums)


def solution(mesh):
    return jax.shard_map(
        shards,
        mesh=mesh,
        in_specs=(
            P(("rows", "tp"), None),
            P("rows", None),
            P("rows"),
            P(None, "rows", "tp"),
            P(None, "tp"),
            P("tp", "rows"),
            P(),
            P(),
            P(),
            P("rows", "tp"),
            P("tp"),
            P("tp", "rows"),
            P(),
            P(),
            P(),
            P(("rows", "tp"), None),
        ),
        out_specs=(P(("rows", "tp"), None), P(("rows", "tp"), None), P(), P(), P(), P(), P(), P()),
        check_vma=False,
    )
```

```python
from functools import partial
import math

import jax
import jax.numpy as jnp
from jax import lax
from jax.experimental import pallas as pl
from jax.experimental.pallas import tpu as pltpu
from jax.sharding import PartitionSpec as P

D = 1024
FF = 4096
HEADS = 16
HEAD_DIM = 64
SLOTS = 512
GROUP = 4
WIDE = GROUP * HEAD_DIM
PAIR = 2 * HEAD_DIM
GROUPS = HEADS // GROUP
FRONT_TILE = SLOTS
TILE = 256
STRIP = 32
EPSILON = 1e-05
MASKED = -1e30
SCALE = 1.0 / math.sqrt(HEAD_DIM)
VMEM_BYTES = 60 * 2**20

NN = (((1,), (0,)), ((), ()))
NT = (((1,), (1,)), ((), ()))
TT = (((0,), (1,)), ((), ()))


def mul(left, right, dims=NN):
    return lax.dot_general(left, right, dims, preferred_element_type=jnp.float32)


def low(values):
    return values.astype(jnp.bfloat16)


def wide(values):
    return values.astype(jnp.float32)


def norm_forward(summed, gain_vec, shift_vec):
    row_mean = jnp.mean(summed, -1, keepdims=True)
    centered = summed - row_mean
    inverse = lax.rsqrt(jnp.mean(centered * centered, -1, keepdims=True) + EPSILON)
    normal = centered * inverse
    return (normal * gain_vec + shift_vec, normal, inverse)


def norm_backward(grad_in, normal, inverse, gain_vec):
    scaled = grad_in * gain_vec
    return inverse * (
        scaled
        - jnp.mean(scaled, -1, keepdims=True)
        - normal * jnp.mean(scaled * normal, -1, keepdims=True)
    )


def mask_bias(seg_col, seg_row, filled):
    keys = lax.broadcasted_iota(jnp.int32, (SLOTS, SLOTS), 0)
    places = lax.broadcasted_iota(jnp.int32, (SLOTS, SLOTS), 1)
    allowed = (seg_col == seg_row) & ((keys < filled) | (keys == places))
    return jnp.where(allowed, 0.0, MASKED)


def half_rows(rows, head):
    zeros = jnp.zeros((HEAD_DIM, rows.shape[1]), rows.dtype)
    return jnp.concatenate([rows, zeros] if head % 2 == 0 else [zeros, rows], 0)


def fetch(refs, scratch, sem, start=True):
    copies = []
    for i, ref in enumerate(refs):
        size = ref.shape[0]
        copies.append(pltpu.make_async_copy(ref, scratch.at[pl.ds(i * size, size)], sem.at[i]))
        if start:
            copies[-1].start()
    return copies


def fetch_sets(refs, scratch, sem, start=True):
    sets = scratch.shape[0]
    size = len(refs) // sets
    copies = []
    for i in range(sets):
        copies += fetch(refs[i * size : (i + 1) * size], scratch.at[i], sem.at[i], start)
    return copies


def first_or_later(step, body):
    @pl.when(step == 0)
    def _():
        body(True)

    @pl.when(step != 0)
    def _():
        body(False)


def wait_all(copies):
    for copy in copies:
        copy.wait()


def set_weight(w_ref, slot_ref, other, part):
    return jnp.concatenate([w_ref[slot_ref[other, c], part] for c in range(w_ref.shape[0])], 0)


def columns_of(w_ref, slot_ref, other, columns):
    there = w_ref.at[other]
    return jnp.concatenate([there[slot_ref[other, c], :, columns] for c in range(there.shape[0])], 0)


def attend_kernel(step, count, fill_ref, slot_ref, x_ref, segc_ref, segr_ref, b_ref, *rest):
    other, half = step % 2, step // 2
    qk_ref, kv_ref, ctx_ref, lse_ref, w_ref, sem, block_ref, block_sem = rest[-8:]
    row = pl.program_id(0)

    def block_copy(r):
        return pltpu.make_async_copy(x_ref.at[pl.ds(r * SLOTS, SLOTS)], block_ref.at[r % 2], block_sem.at[r % 2])

    @pl.when(pl.program_id(0) == 0)
    def _():
        block_copy(row).start()
        wait_all(fetch(rest[:count], w_ref, sem))

    block_copy(row).wait()

    @pl.when(row + 1 < pl.num_programs(0))
    def _():
        block_copy(row + 1).start()

    x = block_ref[row % 2]
    weight = [set_weight(w_ref, slot_ref, other, i) for i in range(3)]
    columns = slice(half * WIDE, (half + 1) * WIDE)
    biases = wide(b_ref[...])[:, columns]
    b_q, b_v = biases[0:1], biases[1:2]
    bias = mask_bias(segc_ref[0], segr_ref[0], fill_ref[pl.program_id(0)])
    q = low(mul(x, weight[0]) + b_q)
    k = low(mul(x, weight[1]))
    v = low(mul(x, weight[2]) + b_v)
    q_t = (q * jnp.bfloat16(SCALE)).T
    v_t = v.T
    qk_ref[0, 0] = q_t
    qk_ref[1, 0] = k.T
    kv_ref[0] = k
    kv_ref[1] = v
    ones = jnp.ones((HEAD_DIM, SLOTS), jnp.bfloat16)

    def score(head):
        own = slice(head * HEAD_DIM, (head + 1) * HEAD_DIM)
        pair = slice(head // 2 * PAIR, (head // 2 + 1) * PAIR)
        return mul(k[:, pair], half_rows(q_t[own], head)) + bias

    def finish(head, top, probs):
        own = slice(head * HEAD_DIM, (head + 1) * HEAD_DIM)
        out = mul(jnp.concatenate([v_t[own], ones], 0), probs)
        total = out[HEAD_DIM : HEAD_DIM + 1]
        ctx_ref[0, own] = low(out[:HEAD_DIM] / total)
        lse_ref[0, 0, head : head + 1, :] = top + jnp.log(total)

    scores = score(0)
    done = None
    for head in range(GROUP):
        following = score(head + 1) if head + 1 < GROUP else None
        if done is not None:
            finish(head - 1, *done)
        top = jnp.max(scores, 0, keepdims=True)
        done = top, low(jnp.exp(scores - top))
        scores = following
    finish(GROUP - 1, *done)


def attend_back_kernel(count, fill_ref, slot_ref, qk_ref, kv_ref, dctx_ref, delta_ref, lse_ref, segc_ref, segr_ref, *rest):
    sum_ref, out_ref, qvb_ref, bias_ref, acc_ref, w_ref, sem = rest[-7:]
    row = pl.program_id(0)
    group = pl.program_id(1)

    @pl.when(group == 0)
    def _():
        bias_ref[...] = mask_bias(segc_ref[0], segr_ref[0], fill_ref[row])
        acc_ref[...] = wide(sum_ref[...])

    def body(arriving):
        if arriving:
            qvb_ref[...] = jnp.zeros_like(qvb_ref)
            fetch_sets(rest[:count], w_ref, sem)
        d_q, d_k, d_v = [], [], []
        for head in range(GROUP):
            own = slice(head * HEAD_DIM, (head + 1) * HEAD_DIM)
            pair = slice(head // 2 * PAIR, (head // 2 + 1) * PAIR)
            q_t, k_t, d_out_t = qk_ref[0, 0, own], qk_ref[1, 0, own], dctx_ref[0, own]
            scores = mul(kv_ref[0, :, pair], half_rows(q_t, head)) + bias_ref[...]
            probs = jnp.exp(scores - lse_ref[0, 0, head : head + 1, :])
            probs_low = low(probs)
            probs_grad = mul(kv_ref[1, :, pair], half_rows(d_out_t, head))
            scores_grad = low(probs * (probs_grad - delta_ref[0, 0, head : head + 1, :]))
            d_v.append(low(mul(d_out_t, probs_low, NT)))
            d_q.append(low(mul(k_t, scores_grad) * SCALE))
            d_k.append(low(mul(q_t, scores_grad, NT)))
        if arriving:
            wait_all(fetch_sets(rest[:count], w_ref, sem, start=False))
        ones = jnp.ones((16, SLOTS), jnp.bfloat16)
        place = (slot_ref[2, 0] ^ (group % 2)) * 2 + group // 2
        columns = pl.ds(pl.multiple_of(place * WIDE, WIDE), WIDE)
        total = acc_ref[...]
        for i, grad in enumerate((d_q, d_k, d_v)):
            grad = jnp.concatenate(grad, 0)
            weight = set_weight(w_ref.at[group], slot_ref, group % 2, i)
            total = total + mul(grad, weight, TT)
            if i != 1:
                qvb_ref[i // 2 : i // 2 + 1, columns] += mul(ones, grad, NT)[0:1]
        acc_ref[...] = total

    first_or_later(row * GROUPS + group, body)

    @pl.when(group == GROUPS - 1)
    def _():
        out_ref[...] = low(acc_ref[...])


def gelu_and_slope(v):
    phi = 0.5 * (1.0 + lax.erf(v * math.sqrt(0.5)))
    bell = jnp.exp(-0.5 * v * v) * (1.0 / math.sqrt(2.0 * math.pi))
    return v * phi, phi + v * bell


FIRST = 1024
LATE = FF // 2 - FIRST
LATE_PIECE = 1024
PIECES = [(False, other, 0, FIRST) for other in range(2)]
PIECES += [(True, other, start, LATE_PIECE) for other in range(2) for start in range(0, LATE, LATE_PIECE)]


def flat_of(piece):
    late, other, start, size = piece
    begin = 2 * FIRST + other * LATE + start if late else other * FIRST
    return slice(begin, begin + size)


def first_columns(first_ref, slot_ref, other, columns):
    n, _, chunk, _ = first_ref.shape
    return first_ref[:, slot_ref[2, 0] ^ other, :, columns].reshape(n * chunk, columns.size)


def piece_weight(first_ref, late_ref, slot_ref, piece, down):
    late, other, start, size = piece
    if late:
        return columns_of(late_ref, slot_ref, other, pl.ds(down * LATE + start, size))
    return first_columns(first_ref, slot_ref, other, pl.ds(down * FIRST + start, size))


assert FIRST == LATE == LATE_PIECE == D


def piece_bias(b_refs, piece):
    late, other, start, size = piece
    begin = FIRST * late + start
    return wide(b_refs[other][...]).reshape(1, FF // 2)[:, begin : begin + size]


def out_columns(first_ref, slot_ref, group):
    return first_columns(first_ref, slot_ref, group % 2, pl.ds(2 * FIRST + group // 2 * WIDE, WIDE))


def row_of(ref):
    return wide(ref[...]).reshape(1, D)


def front_kernel(
    slot_ref, x_ref, ctx_ref, vec_refs, bi_refs, first_ref, normal_ref, inv_ref, branch_ref, slope_ref, low_ref
):
    out_bias, gain_one, bias_one, down_bias = [row_of(ref) for ref in vec_refs]
    out_weight = jnp.concatenate([out_columns(first_ref, slot_ref, group) for group in range(GROUPS)], 1)
    attention = mul(ctx_ref[0], out_weight, TT) + out_bias
    branch_ref[...] = attention
    for start in range(0, FRONT_TILE, STRIP):
        rows = slice(start, start + STRIP)
        normed, normal_one, inverse_one = norm_forward(wide(x_ref[rows]) + branch_ref[rows], gain_one, bias_one)
        normal_ref[rows] = normal_one
        inv_ref[rows] = jnp.broadcast_to(inverse_one, (STRIP, 128))
        low_ref[rows] = low(normed)
        branch_ref[rows] = normed + down_bias
    normed_low = low_ref[...]
    branch = branch_ref[...]

    def inner_of(piece):
        return mul(normed_low, piece_weight(first_ref, None, slot_ref, piece, 0)) + piece_bias(bi_refs, piece)

    inner = inner_of(PIECES[0])
    for piece in PIECES[:2]:
        following = inner_of(PIECES[1]) if piece is PIECES[0] else None
        act, slope = gelu_and_slope(inner)
        slope_ref[:, flat_of(piece)] = low(slope)
        branch = branch + mul(low(act), piece_weight(first_ref, None, slot_ref, piece, 1), NT)
        inner = following
    branch_ref[...] = branch


def back_kernel(
    count, slot_ref, normal_ref, inv_ref, branch_ref, slope_ref, ct_ref, ctx_ref, vec_refs, bi_refs, first_ref, *rest
):
    out_ref, dctx_ref, delta_ref, sum_ref, sums_ref, keep_ref, acc_ref, low_ref, late_ref, late_sem = rest[-10:]


    @pl.when(pl.program_id(0) == 0)
    def _():
        sums_ref[...] = jnp.zeros_like(sums_ref)
        wait_all(fetch_sets(rest[:count], late_ref, late_sem))

    gain_one, bias_one, gain_two, bias_two = [row_of(ref) for ref in vec_refs]
    weight = partial(piece_weight, first_ref, late_ref, slot_ref)
    strips = [slice(start, start + STRIP) for start in range(0, TILE, STRIP)]

    def add(total, term):
        term = jnp.sum(term.reshape(STRIP // 8, 8, D), 0)
        return term if total is None else total + term

    for rows in strips:
        low_ref[rows] = low(normal_ref[rows] * gain_one + bias_one)
    normed_low = low_ref[...]
    branch = branch_ref[...]
    def inner_of(piece):
        return mul(normed_low, weight(piece, 0)) + piece_bias(bi_refs, piece)

    late_pieces = PIECES[2:]
    inner = inner_of(late_pieces[0])
    for i, piece in enumerate(late_pieces):
        following = inner_of(late_pieces[i + 1]) if i + 1 < len(late_pieces) else None
        act, slope = gelu_and_slope(inner)
        flat = flat_of(piece)
        keep_ref[:, flat.start - 2 * FIRST : flat.stop - 2 * FIRST] = low(slope)
        branch = branch + mul(low(act), weight(piece, 1), NT)
        inner = following
    acc_ref[...] = branch
    sums = [None] * 4
    for rows in strips:
        final, normal_two, inverse_two = norm_forward(acc_ref[rows], gain_two, bias_two)
        out_ref[rows] = low(final)
        final_grad = wide(ct_ref[rows])
        sum_two = norm_backward(final_grad, normal_two, inverse_two, gain_two)
        acc_ref[rows] = sum_two
        low_ref[rows] = low(sum_two)
        sums[2] = add(sums[2], wide(low(sum_two)))
        sums[3] = add(sums[3], final_grad)
    branch_grad = low_ref[...]
    normed_grad = acc_ref[...]
    for piece in PIECES:
        flat = flat_of(piece)
        slope = keep_ref[:, flat.start - 2 * FIRST : flat.stop - 2 * FIRST] if piece[0] else slope_ref[:, flat]
        inner_grad = low(mul(branch_grad, weight(piece, 1)) * wide(slope))
        late, other = piece[:2]
        place = pl.ds(4 + 2 * (slot_ref[2, 0] ^ other) + int(late), 1)
        sums_ref[place, :] += jnp.sum(wide(inner_grad), 0, keepdims=True)
        normed_grad = normed_grad + mul(inner_grad, weight(piece, 0), NT)
    acc_ref[...] = normed_grad
    for rows in strips:
        normed_grad = acc_ref[rows]
        sum_one = low(norm_backward(normed_grad, normal_ref[rows], inv_ref[rows, 0:1], gain_one))
        sum_ref[rows] = sum_one
        sums[0] = add(sums[0], wide(sum_one))
        sums[1] = add(sums[1], normed_grad)
    sum_one = sum_ref[...]
    out_weight = jnp.concatenate([out_columns(first_ref, slot_ref, group) for group in range(GROUPS)], 1)
    all_grads = low(mul(sum_one, out_weight))
    for group in range(GROUPS):
        part = slice(group * WIDE, (group + 1) * WIDE)
        context_grad = all_grads[:, part].T
        dctx_ref[0, part] = context_grad
        product = wide(context_grad) * wide(ctx_ref[0, part])
        for head in range(GROUP):
            own = slice(head * HEAD_DIM, (head + 1) * HEAD_DIM)
            delta_ref[0, group, head : head + 1, :] = jnp.sum(product[own], 0, keepdims=True)
    for i, term in enumerate(sums):
        sums_ref[i : i + 1, :] += jnp.sum(term, 0, keepdims=True)


def params(grid_rank):
    return pltpu.CompilerParams(
        dimension_semantics=("arbitrary",) * grid_rank, vmem_limit_bytes=VMEM_BYTES
    )


def cost(flops, moved):
    return pl.CostEstimate(flops=int(flops), bytes_accessed=int(moved), transcendentals=0)


SCALARS = pl.BlockSpec(memory_space=pltpu.SMEM)
ANYWHERE = pl.BlockSpec(memory_space=pl.ANY)


def wholes(arrays):
    return tuple(whole(array) for array in arrays)


def whole(array):
    return pl.BlockSpec(array.shape, lambda *_: (0,) * array.ndim, pipeline_mode=pl.Buffered(1))


def slot_scratch(pieces, sets):
    count = len(pieces) // sets
    n = sum(w.shape[0] for w in pieces[:count])
    return [
        pltpu.VMEM((sets, n) + pieces[0].shape[1:], pieces[0].dtype),
        pltpu.SemaphoreType.DMA((sets, count)),
    ]


def attend(step, earlier, tokens, seg_col, seg_row, fills, slots, pieces, bias):
    rows = tokens.shape[0] // SLOTS
    return pl.pallas_call(
        partial(attend_kernel, step, len(pieces)),
        grid=(rows,),
        in_specs=[
            SCALARS,
            SCALARS,
            ANYWHERE,
            pl.BlockSpec((1, SLOTS, 1), lambda r: (r, 0, 0)),
            pl.BlockSpec((1, 1, SLOTS), lambda r: (r, 0, 0)),
            whole(bias),
        ]
        + [ANYWHERE] * (len(pieces) + len(earlier)),
        out_specs=[
            pl.BlockSpec((2, 1, WIDE, SLOTS), lambda r: (0, r, step, 0)),
            pl.BlockSpec((2, SLOTS, WIDE), lambda r: (0, r, step)),
            pl.BlockSpec((1, WIDE, SLOTS), lambda r: (r, step, 0)),
            pl.BlockSpec((1, 1, GROUP, SLOTS), lambda r: (r, step, 0, 0)),
        ],
        out_shape=[
            jax.ShapeDtypeStruct((2, rows, D, SLOTS), jnp.bfloat16),
            jax.ShapeDtypeStruct((2, rows * SLOTS, D), jnp.bfloat16),
            jax.ShapeDtypeStruct((rows, D, SLOTS), jnp.bfloat16),
            jax.ShapeDtypeStruct((rows, GROUPS, GROUP, SLOTS), jnp.float32),
        ],
        scratch_shapes=[
            pltpu.VMEM((sum(w.shape[0] for w in pieces),) + pieces[0].shape[1:], jnp.bfloat16),
            pltpu.SemaphoreType.DMA((len(pieces),)),
            pltpu.VMEM((2, SLOTS, D), jnp.bfloat16),
            pltpu.SemaphoreType.DMA((2,)),
        ],
        input_output_aliases={6 + len(pieces) + i: i for i in range(len(earlier))},
        compiler_params=params(1),
        cost_estimate=cost(15e9, 10e6),
        name="attend",
    )(fills, slots, tokens, seg_col, seg_row, bias, *pieces, *earlier)


def attend_back(qk, kv, context_grad, delta, lse, seg_col, seg_row, fills, slots, weights, sum_one):
    rows = kv.shape[1] // SLOTS
    return pl.pallas_call(
        partial(attend_back_kernel, len(weights)),
        grid=(rows, GROUPS),
        in_specs=[
            SCALARS,
            SCALARS,
            pl.BlockSpec((2, 1, WIDE, SLOTS), lambda r, g: (0, r, g, 0)),
            pl.BlockSpec((2, SLOTS, WIDE), lambda r, g: (0, r, g)),
            pl.BlockSpec((1, WIDE, SLOTS), lambda r, g: (r, g, 0)),
            pl.BlockSpec((1, 1, GROUP, SLOTS), lambda r, g: (r, g, 0, 0)),
            pl.BlockSpec((1, 1, GROUP, SLOTS), lambda r, g: (r, g, 0, 0)),
            pl.BlockSpec((1, SLOTS, 1), lambda r, g: (r, 0, 0)),
            pl.BlockSpec((1, 1, SLOTS), lambda r, g: (r, 0, 0)),
        ]
        + [ANYWHERE] * len(weights)
        + [pl.BlockSpec((SLOTS, D), lambda r, g: (r, 0))],
        out_specs=[
            pl.BlockSpec((SLOTS, D), lambda r, g: (r, 0)),
            pl.BlockSpec((2, D), lambda r, g: (0, 0)),
        ],
        out_shape=[
            jax.ShapeDtypeStruct((rows * SLOTS, D), jnp.bfloat16),
            jax.ShapeDtypeStruct((2, D), jnp.float32),
        ],
        scratch_shapes=[
            pltpu.VMEM((SLOTS, SLOTS), jnp.float32),
            pltpu.VMEM((SLOTS, D), jnp.float32),
        ]
        + slot_scratch(weights, GROUPS),
        compiler_params=params(2),
        cost_estimate=cost(50e9, 30e6),
        name="attend_back",
    )(fills, slots, qk, kv, context_grad, delta, lse, seg_col, seg_row, *weights, sum_one)


def tiles(width, tile=TILE):
    return pl.BlockSpec((tile, width), lambda i: (i, 0))


PER_ROW = SLOTS // TILE
ROWS_T = pl.BlockSpec((1, D, TILE), lambda i: (i // PER_ROW, 0, i % PER_ROW))


def feed_front(slots, tokens, context, first, vectors, in_bias):
    count = tokens.shape[0]
    return pl.pallas_call(
        front_kernel,
        grid=(count // FRONT_TILE,),
        in_specs=[SCALARS, tiles(D, FRONT_TILE), pl.BlockSpec((1, D, SLOTS), lambda i: (i, 0, 0)), wholes(vectors), wholes(in_bias), whole(first)],
        out_specs=[tiles(D, FRONT_TILE), tiles(128, FRONT_TILE), tiles(D, FRONT_TILE), tiles(2 * FIRST, FRONT_TILE)],
        out_shape=[
            jax.ShapeDtypeStruct((count, D), jnp.float32),
            jax.ShapeDtypeStruct((count, 128), jnp.float32),
            jax.ShapeDtypeStruct((count, D), jnp.float32),
            jax.ShapeDtypeStruct((count, 2 * FIRST), jnp.bfloat16),
        ],
        scratch_shapes=[pltpu.VMEM((FRONT_TILE, D), jnp.bfloat16)],
        compiler_params=params(1),
        cost_estimate=cost(25e9, 30e6),
        name="feed_front",
    )(slots, tokens, context, vectors, in_bias, first)


def feed_back(slots, front, cotangent, context, first, late, vectors, in_bias):
    count = cotangent.shape[0]
    return pl.pallas_call(
        partial(back_kernel, len(late)),
        grid=(count // TILE,),
        in_specs=[SCALARS, tiles(D), tiles(128), tiles(D), tiles(2 * FIRST), tiles(D), ROWS_T, wholes(vectors), wholes(in_bias), whole(first)]
        + [ANYWHERE] * len(late),
        out_specs=[
            tiles(D),
            ROWS_T,
            pl.BlockSpec((1, GROUPS, GROUP, TILE), lambda i: (i // PER_ROW, 0, 0, i % PER_ROW)),
            tiles(D),
            pl.BlockSpec((8, D), lambda i: (0, 0)),
        ],
        out_shape=[
            jax.ShapeDtypeStruct((count, D), jnp.bfloat16),
            jax.ShapeDtypeStruct((count // SLOTS, D, SLOTS), jnp.bfloat16),
            jax.ShapeDtypeStruct((count // SLOTS, GROUPS, GROUP, SLOTS), jnp.float32),
            jax.ShapeDtypeStruct((count, D), jnp.bfloat16),
            jax.ShapeDtypeStruct((8, D), jnp.float32),
        ],
        scratch_shapes=[
            pltpu.VMEM((TILE, 2 * LATE), jnp.bfloat16),
            pltpu.VMEM((TILE, D), jnp.float32),
            pltpu.VMEM((TILE, D), jnp.bfloat16),
        ]
        + slot_scratch(late, 2),
        compiler_params=params(1),
        cost_estimate=cost(75e9, 40e6),
        name="feed_back",
    )(slots, *front, cotangent, context, vectors, in_bias, first, *late)


def stage_bits(n):
    bits = n.bit_length() - 1
    in_z = -(-bits // 3)
    in_y = -(-(bits - in_z) // 2)
    in_x = bits - in_z - in_y
    x = list(range(in_x))
    y = list(range(in_x, in_x + in_y))
    z = list(range(in_x + in_y, bits))
    return z + y + x, z[::-1] + x + y


def partner(block, n, stage):
    bits = [order[stage] for order in stage_bits(n)]
    pairs = [(2 * i + core, 2 * (i ^ (1 << bits[core])) + core) for i in range(n) for core in range(2)]
    return lax.ppermute(block, ("rows", "tp"), pairs)


def joined(*blocks):
    return jnp.concatenate(blocks, 0)


def swap_cores(block):
    return lax.ppermute(block, "tp", [(0, 1), (1, 0)])


def after(value, *earlier):
    return lax.optimization_barrier((value, earlier))[0]


def together(*values):
    return lax.optimization_barrier(values)


def slot_table(n):
    apart = jnp.arange(n, dtype=jnp.int32) ^ lax.axis_index("rows")
    tables = []
    for order in stage_bits(n):
        tables.append(sum(((apart >> bit) & 1) << place for place, bit in enumerate(order)))
    core = lax.axis_index("tp")
    ordered = jnp.where(core == 0, jnp.stack(tables), jnp.stack(tables[::-1]))
    return jnp.concatenate([ordered, jnp.full((1, n), core, jnp.int32)], 0)


def sum_over_rows(values, n, beside, steps):
    bits = n.bit_length() - 1

    def got(distance):
        return lax.ppermute(values, "rows", [(i, i ^ distance) for i in range(n)])

    for bit in range(0, bits - 1, 2):
        near, far, both = [got(j << bit) for j in (1, 2, 3)]
        if steps:
            beside = steps[0](beside)
            steps = steps[1:]
        near, far, both, beside = together(near, far, both, beside)
        values = (values + near) + (far + both)
    values = values + got(1 << (bits - 1)) if bits % 2 else values
    for step in steps:
        beside = step(beside)
    return values, beside


def shards(
    tokens,
    segment_ids,
    fill_counts,
    qkv_weight,
    qv_bias,
    out_weight,
    out_bias,
    norm1_gain,
    norm1_bias,
    in_weight,
    in_bias,
    down_weight,
    down_bias,
    norm2_gain,
    norm2_bias,
    cotangent,
):
    n = lax.axis_size("rows")
    core = lax.axis_index("tp")
    rows_here = tokens.shape[0] // SLOTS
    down_t = down_weight.T

    last = n.bit_length() - 2

    def spread(block, stages):
        for stage in stages:
            block = joined(block, partner(block, n, stage))
        return block

    a = qkv_weight[None, :, :, :WIDE]
    a = joined(a, partner(a, n, 0))
    a, b = together(a, qkv_weight[None, :, :, WIDE:])
    a_got = partner(a, n, 1)
    b_got = partner(b, n, 0)
    first = jnp.concatenate([in_weight[:, :FIRST], down_t[:, :FIRST], out_weight.T], 1)

    a, a_got, b, b_got, first = together(a, a_got, b, b_got, first)
    first = lax.all_gather(first, ("rows", "tp"), axis=0, tiled=False).reshape((n, 2) + first.shape)
    a = joined(a, a_got)
    b = joined(b, b_got)
    for stage in range(2, last):
        a_got = partner(a, n, stage)
        a = a if stage == last - 1 else joined(a, a_got)
    b_got = partner(b, n, 1)
    segments = lax.dynamic_slice_in_dim(segment_ids, core * rows_here, rows_here, 0)
    fills = lax.dynamic_slice_in_dim(fill_counts, core * rows_here, rows_here, 0)
    slots = slot_table(n)
    small = (segments[:, :, None], segments[:, None, :], fills, slots)
    b_qv = (qv_bias, swap_cores(qv_bias))
    b_in = (in_bias, swap_cores(in_bias))
    late = jnp.concatenate([in_weight[:, FIRST:], down_t[:, FIRST:]], 1)[None]

    a, a_got, b, b_got, late, small, b_qv, b_in = together(a, a_got, b, b_got, late, small, b_qv, b_in)
    a = joined(a, a_got)
    a_other = swap_cores(a)
    a_got = partner(a, n, last)
    b = joined(b, b_got)

    def run(step, earlier, *pieces):
        return attend(step, earlier, tokens, *small, pieces, b_qv[step % 2])

    a, a_got, a_other, b, late = together(a, a_got, a_other, b, late)
    a_other_got = swap_cores(a_got)
    for stage in range(2, last):
        b_got = partner(b, n, stage)
        b = b if stage == last - 1 else joined(b, b_got)
    late_got = partner(late, n, 0)
    results = run(0, (), a, a_got)

    results, a_other_got, b, b_got, late, late_got = together(results, a_other_got, b, b_got, late, late_got)
    b = joined(b, b_got)
    late = joined(late, late_got)
    late_got = partner(late, n, 1)
    b_other = swap_cores(b)
    b_got = partner(b, n, last)
    results = run(1, results, a_other, a_other_got)

    results, b_other, b_got = together(results, b_other, b_got)
    b_other_got = swap_cores(b_got)
    results = run(2, results, b, b_got)

    results, b_other_got, late, late_got = together(results, b_other_got, late, late_got)
    late = joined(late, late_got)
    for stage in range(2, last):
        late_got = partner(late, n, stage)
        late = late if stage == last - 1 else joined(late, late_got)
    results = run(3, results, b_other, b_other_got)

    results, late, late_got = together(results, late, late_got)
    late_own = [late, late_got]
    late_others = [swap_cores(w) for w in late_own]
    late_far = [partner(w, n, last) for w in late_own]

    qk, kv, context, lse = results
    front = feed_front(slots, tokens, context, first, (out_bias, norm1_gain, norm1_bias, down_bias), b_in)

    front, late_others, late_far = together(front, late_others, late_far)
    late_others += [swap_cores(w) for w in late_far]
    vectors = (norm1_gain, norm1_bias, norm2_gain, norm2_bias)
    layer_out, context_grad, delta, sum_one, grads = feed_back(
        slots, front, cotangent, context, first, late_own + late_far + late_others, vectors, b_in
    )
    grads = lax.all_gather(grads, ("rows", "tp"), axis=0)

    def summed(grads):
        return jnp.sum(grads, 0)

    def taken_apart(sums):
        return sums[0], sums[1], sums[4:].reshape(-1), sums[2], sums[3]

    a_set = [a, a_got, a_other, a_other_got]
    b_set = [b, b_got, b_other, b_other_got]
    tokens_grad, qv_grads = attend_back(
        qk, kv, context_grad, delta, lse, *small, a_set + b_set, sum_one
    )
    qv, sums = sum_over_rows(qv_grads + swap_cores(qv_grads), n, grads, (summed, taken_apart))
    return (layer_out, tokens_grad, qv, *sums)


def solution(mesh):
    return jax.shard_map(
        shards,
        mesh=mesh,
        in_specs=(
            P(("rows", "tp"), None),
            P("rows", None),
            P("rows"),
            P(None, "rows", "tp"),
            P(None, "tp"),
            P("tp", "rows"),
            P(),
            P(),
            P(),
            P("rows", "tp"),
            P("tp"),
            P("tp", "rows"),
            P(),
            P(),
            P(),
            P(("rows", "tp"), None),
        ),
        out_specs=(P(("rows", "tp"), None), P(("rows", "tp"), None), P(), P(), P(), P(), P(), P()),
        check_vma=False,
    )
```
